32 devices in a mesh: shard: 4 (over z), tensor: 4 (over y, x), section: 2 (over core).
Axes of the slice: x: 2, y: 2, z: 4, core: 2. Of those that a mesh axis runs over, the one named last changes fastest.
Arguments:
- grad_parts: bfloat16 [4, 2, 4, 1024, 1024], P('shard', 'section', None, 'tensor'), may hold values from -45 to 45
- vector_grads: bfloat16 [4, 2, 4, 1024], P('shard', 'section', None, 'tensor'), may hold values from -6 to 6
- momentum: float32 [2, 4, 1024, 1024], P('section', None, ('tensor', 'shard')), may hold values from -6 to 6
- weights: bfloat16 [2, 4, 1024, 1024], P('section', None, ('tensor', 'shard')), may hold values from -0.1875 to 0.1875
- vectors: float32 [2, 4, 1024], P('section', None, ('tensor', 'shard')), may hold values from 0.5 to 1.5
- first_moment: float32 [2, 4, 1024], P('section', None, ('tensor', 'shard')), may hold values from -3 to 3
- second_moment: float32 [2, 4, 1024], P('section', None, ('tensor', 'shard')), may hold values from 0.05 to 2
Outputs:
- new_momentum: float32 [2, 4, 1024, 1024], P('section', None, ('tensor', 'shard'))
- orthogonal_update: bfloat16 [2, 4, 1024, 1024], P('section', None, ('tensor', 'shard'))
- new_weights: bfloat16 [2, 4, 1024, 1024], P('section', None, ('tensor', 'shard'))
- adam_direction: float32 [2, 4, 1024], P('section', None, ('tensor', 'shard'))
- new_vectors: float32 [2, 4, 1024], P('section', None, ('tensor', 'shard'))
The draws below stay inside these ranges and needn't reach their ends.
All inputs are finite; a program needn't handle non-finite values.
Results may differ from the reference program's by a relative error of at most 0.0048.
The reference program's roundings to bfloat16 on the way (of `scaled`, `block_gram`, `gram_matrix` and `first_product`) count: a program that leaves them out, or rounds other values in their place, can miss the bound.
Values may be sent and summed in bfloat16 or wider, within the bound.
No kernel may reach another device: no remote copies, remote signals or barrier semaphores. Data moves between devices by JAX's collectives and lax.ppermute only.
A program may use at most 64 MiB of HBM per device.

```python
import math
import jax
import jax.numpy as jnp
from jax import lax

D = 1024
MATS = 4
VECS = 4
NS_STEPS = 2
N_SHARD = 4
N_TENSOR = 4
N_SECTION = 2


def row_weighting(key):
    block_pick = jax.random.randint(jax.random.fold_in(key, 101), (N_SECTION, MATS, 1, 1), 0, N_TENSOR)
    row_block = (jnp.arange(D) // (D // N_TENSOR)).reshape(1, 1, D, 1)
    return jnp.where(row_block == block_pick, 1.0, 0.1).astype(jnp.float32)


def draw_grad_parts(key, part):
    keys = jax.random.split(key, 5)
    row_scale = jnp.exp(jax.random.uniform(keys[0], (1, N_SECTION, MATS, D, 1), jnp.float32, 0.0, math.log(10.0)))
    col_scale = jnp.exp(jax.random.uniform(keys[1], (1, N_SECTION, MATS, 1, D), jnp.float32, 0.0, math.log(10.0)))
    ramp = 1.0 + 2.0 * jnp.arange(D, dtype=jnp.float32).reshape(1, 1, 1, D, 1) / (D - 1)
    heavier = jax.random.randint(jax.random.fold_in(key, 202), (), 0, N_SECTION)
    ratio = jax.random.uniform(jax.random.fold_in(key, 203), (), jnp.float32, 2.5, 4.0)
    section_gain = jnp.where(jnp.arange(N_SECTION) == heavier, 1.75, 1.75 / ratio).astype(jnp.float32).reshape(1, N_SECTION, 1, 1, 1)
    light_rows = row_weighting(key)[None]
    values = jax.random.truncated_normal(keys[4], -4.0, 4.0, (N_SHARD, N_SECTION, MATS, D, D), jnp.float32)
    return (0.02 * values * row_scale * col_scale * ramp * section_gain * light_rows).astype(jnp.bfloat16)


def draw_momentum(key, part):
    light_rows = row_weighting(key)
    value_key = jax.random.fold_in(key, 303)
    values = jax.random.truncated_normal(value_key, -6.0, 6.0, (N_SECTION, MATS, D, D), jnp.float32)
    return (values * light_rows).astype(jnp.float32)


def strengthened(array, own_key, source, target, blocks, factor):
    def block_of(position):
        return (jnp.arange(array.shape[position]) // (array.shape[position] // blocks)).reshape((-1,) + (1,) * (array.ndim - 1 - position))

    one_side = jax.random.permutation(own_key, blocks)[block_of(target)]
    far = (block_of(target) + blocks // 2) % blocks
    return jnp.where((block_of(source) == one_side) | (block_of(source) == far), factor * array, array)


def levels(own_key, extent, shards, smallest, high):
    def one(axis_at, shards_of):
        draws = jax.random.uniform(jax.random.fold_in(jax.random.fold_in(own_key, 6), axis_at), (shards_of,), jnp.float32, smallest / len(shards), high / len(shards))
        return jnp.repeat(jnp.exp(draws), extent[axis_at] // shards_of).reshape((-1,) + (1,) * (len(extent) - axis_at - 1))

    level = one(*shards[0])
    for cut in shards[1:]:
        level = level * one(*cut)
    return level


def gaussian(own_key, dims, width, bound, shards=(), held_as=jnp.bfloat16):
    factor_of = levels(own_key, dims, shards, -0.22, 0.18) if shards else 1.0
    values = jax.random.normal(own_key, dims, jnp.float32) * width * factor_of
    return jnp.minimum(jnp.maximum(values, -bound), bound).astype(held_as)


def noise_with(rng, shape, spread, most, cuts, heavy, kind=jnp.bfloat16):
    drawn = spread * jax.random.normal(rng, shape, jnp.float32)
    if cuts:
        drawn = drawn * levels(rng, shape, cuts, -0.22, 0.18)
    return jnp.clip(strengthened(drawn, jax.random.fold_in(rng, 3), *heavy), -most, most).astype(kind)


def setup_inputs(seed: int = 0) -> dict:
    seeds = jax.random.split(jax.random.key(seed), 8)
    return {
        "grad_parts": draw_grad_parts(jax.random.fold_in(seeds[7], 71), 0),
        "vector_grads": noise_with(seeds[1], (N_SHARD, N_SECTION, VECS, D), 1.0, 6.0, ((0, 4), (1, 2), (3, 4)), (0, 3, 4, 2.0)),
        "momentum": draw_momentum(jax.random.fold_in(seeds[7], 71), 0),
        "weights": gaussian(seeds[3], (N_SECTION, MATS, D, D), D ** -0.5, 0.1875, ((0, 2), (2, 16))),
        "vectors": jnp.clip(1.0 + 0.1 * jax.random.normal(seeds[4], (N_SECTION, VECS, D), jnp.float32), 0.5, 1.5),
        "first_moment": gaussian(seeds[5], (N_SECTION, VECS, D), 0.5, 3.0, ((0, 2), (2, 16)), jnp.float32),
        "second_moment": jnp.clip(jnp.exp(math.log(2.0) - 3.6888794 * jax.random.uniform(seeds[6], (N_SECTION, VECS, D), jnp.float32) ** levels(seeds[6], (N_SECTION, VECS, D), ((0, 2), (2, 16)), -0.2, 0.2)), 0.05, 2.0),
    }


ns_first = 3.4445
ns_second = -4.775
ns_third = 2.0315
mom_beta = 0.95
max_norm = 1024.0
muon_rate = 0.02
muon_decay = 0.1
adam_rate = 0.001
adam_decay = 0.01

def orthogonalize(matrix):
    for iteration in range(NS_STEPS):
        blocks = matrix.reshape(N_TENSOR, D // N_TENSOR, D).astype(jnp.float32)
        block_gram = jnp.einsum('brc,brd->bcd', blocks, blocks, precision=lax.Precision.HIGHEST)
        rounded = lax.optimization_barrier(block_gram.astype(jnp.bfloat16)).astype(jnp.float32)
        gram_matrix = lax.optimization_barrier(jnp.sum(rounded, axis=0)).astype(jnp.bfloat16)
        first_product = jnp.dot(matrix, gram_matrix, preferred_element_type=jnp.float32).astype(jnp.bfloat16)
        second_product = jnp.dot(first_product, gram_matrix, preferred_element_type=jnp.float32)
        combined = ns_first * matrix.astype(jnp.float32) + ns_second * first_product.astype(jnp.float32) + ns_third * second_product
        matrix = combined.astype(jnp.bfloat16)
    return matrix

def reference(grad_parts, vector_grads, momentum, weights, vectors, first_moment, second_moment):

    def add_part(part_index, accumulated):
        return accumulated + grad_parts[part_index].astype(jnp.float32)
    grad_sum = lax.fori_loop(0, N_SHARD, add_part, jnp.zeros(grad_parts.shape[1:], jnp.float32))
    vector_sum = lax.optimization_barrier(jnp.sum(vector_grads.astype(jnp.float32), axis=0))
    grand_total = jnp.sum(grad_sum * grad_sum) + jnp.sum(vector_sum * vector_sum)
    clip_factor = jnp.minimum(1.0, max_norm / (jnp.sqrt(grand_total) + 1e-06))
    new_momentum = mom_beta * momentum + clip_factor * grad_sum
    nesterov = clip_factor * grad_sum + mom_beta * new_momentum
    update_norm = lax.optimization_barrier(jnp.sum(nesterov * nesterov, axis=(2, 3), keepdims=True))
    scaled = (nesterov / (jnp.sqrt(update_norm) + 1e-07)).astype(jnp.bfloat16)
    orthogonal_update = jnp.stack([jnp.stack([orthogonalize(scaled[section_index, matrix_index]) for matrix_index in range(MATS)]) for section_index in range(N_SECTION)])
    muon_scale = 0.2 * math.sqrt(D)
    new_weights = (weights.astype(jnp.float32) * (1.0 - muon_rate * muon_decay) - muon_rate * muon_scale * orthogonal_update.astype(jnp.float32)).astype(jnp.bfloat16)
    vector_clipped = clip_factor * vector_sum
    updated_first = 0.9 * first_moment + 0.1 * vector_clipped
    updated_second = 0.999 * second_moment + 0.001 * vector_clipped * vector_clipped
    adam_direction = updated_first / (jnp.sqrt(updated_second) + 1e-08)
    new_vectors = vectors * (1.0 - adam_rate * adam_decay) - adam_rate * adam_direction
    return (new_momentum, orthogonal_update, new_weights, adam_direction, new_vectors)
```

```python
import math

import jax
import jax.numpy as jnp
from jax import lax
from jax.experimental import pallas as pl
from jax.experimental.pallas import tpu as pltpu
from jax.sharding import PartitionSpec as P

D = 1024
NS_STEPS = 2


ns_first = 3.4445
ns_second = -4.775
ns_third = 2.0315
mom_beta = 0.95
max_norm = 1024.0
muon_rate = 0.02
muon_decay = 0.1
adam_rate = 0.001
adam_decay = 0.01

VECTOR_ROWS = 16
MESH_AXES = ("shard", "tensor", "section")


def gram_of(blocks, gram_ref):
    width = blocks[0].shape[1]
    step = 256
    for start in range(0, width, step):
        total = None
        for block in blocks:
            whole = block[...]
            part = whole[:, start : start + step]
            product = lax.dot_general(
                whole, part, (((0,), (0,)), ((), ())), preferred_element_type=jnp.float32
            )
            rounded = product.astype(jnp.bfloat16).astype(jnp.float32)
            total = rounded if total is None else total + rounded
        gram_ref[:, start : start + step] = total.astype(jnp.bfloat16)


def polynomial(block, gram_ref):
    gram = gram_ref[...]
    first = jnp.dot(block, gram, preferred_element_type=jnp.float32).astype(jnp.bfloat16)
    second = jnp.dot(first, gram, preferred_element_type=jnp.float32)
    combined = (
        ns_first * block.astype(jnp.float32)
        + ns_second * first.astype(jnp.float32)
        + ns_third * second
    )
    return combined.astype(jnp.bfloat16)


def orthogonalize_kernel(*refs):
    count = len(refs) - 3
    blocks = refs[:count]
    out_ref, gram_ref, next_ref = refs[count:]
    for iteration in range(NS_STEPS - 1):
        gram_of(blocks, gram_ref)
        for position in range(count):
            next_ref[position] = polynomial(blocks[position][...], gram_ref)
        blocks = [next_ref.at[position] for position in range(count)]
    gram_of(blocks, gram_ref)
    out_ref[...] = polynomial(blocks[0][...], gram_ref)


def orthogonalize(blocks):
    height, width = blocks[0].shape
    return pl.pallas_call(
        orthogonalize_kernel,
        out_shape=jax.ShapeDtypeStruct((height, width), jnp.bfloat16),
        scratch_shapes=[
            pltpu.VMEM((width, width), jnp.bfloat16),
            pltpu.VMEM((len(blocks), height, width), jnp.bfloat16),
        ],
        compiler_params=pltpu.CompilerParams(vmem_limit_bytes=48 * 2**20),
    )(*blocks)


def per_device(grad_parts, vector_grads, momentum, weights, vectors, first_moment, second_moment):
    shard_count = lax.axis_size("shard")
    tensor_count = lax.axis_size("tensor")
    section_count = lax.axis_size("section")
    shard_index = lax.axis_index("shard")
    _, matrix_count, local_height, width = momentum.shape
    vector_width = vectors.shape[2]
    own_momentum = momentum[0]

    rows = matrix_count * local_height
    by_target = (
        grad_parts.reshape(matrix_count, shard_count, local_height, width)
        .transpose(1, 0, 2, 3)
        .reshape(shard_count, rows, width)
    )
    vector_line = jnp.broadcast_to(
        vector_grads.reshape(1, 1, width), (shard_count, VECTOR_ROWS, width)
    )
    payload = jnp.concatenate([by_target, vector_line], axis=1)
    arrived = lax.all_to_all(payload, "shard", split_axis=0, concat_axis=0, tiled=True)
    grad_rows = jnp.sum(arrived[:, :rows].astype(jnp.float32), axis=0).reshape(
        matrix_count, local_height, width
    )
    vector_whole = jnp.sum(arrived[:, rows].astype(jnp.float32), axis=0).reshape(
        vectors.shape[1], vector_width * shard_count
    )
    vector_rows = lax.dynamic_slice_in_dim(
        vector_whole, shard_index * vector_width, vector_width, 1
    )

    grad_squares = jnp.sum(grad_rows * grad_rows, axis=(1, 2))
    cross = jnp.sum(grad_rows * own_momentum, axis=(1, 2))
    momentum_squares = jnp.sum(own_momentum * own_momentum, axis=(1, 2))
    own_total = jnp.sum(grad_squares) + jnp.sum(vector_rows * vector_rows)
    same_section = (
        jnp.arange(section_count) == lax.axis_index("section")
    ).astype(jnp.float32)[:, None]
    matrix_figures = jnp.concatenate([grad_squares, cross, momentum_squares])
    line = jnp.concatenate(
        [
            same_section * matrix_figures[None],
            jnp.broadcast_to(own_total, (section_count, 1)),
            jnp.zeros((section_count, 127 - 3 * matrix_count), jnp.float32),
        ],
        axis=1,
    )
    others = shard_count * tensor_count
    figures = jnp.broadcast_to(line[None, :, None, :], (others, section_count, 8, 128)).reshape(
        others * section_count, 8, 128
    )
    figures = lax.all_to_all(figures, MESH_AXES, split_axis=0, concat_axis=0, tiled=True)
    sums = jnp.sum(figures[:, 0, :], axis=0)
    grand_total = sums[3 * matrix_count]
    clip_factor = jnp.minimum(1.0, max_norm / (jnp.sqrt(grand_total) + 1e-06))
    grad_scale = (1.0 + mom_beta) * clip_factor
    momentum_scale = mom_beta * mom_beta
    update_norm = (
        grad_scale * grad_scale * sums[:matrix_count]
        + 2.0 * grad_scale * momentum_scale * sums[matrix_count : 2 * matrix_count]
        + momentum_scale * momentum_scale * sums[2 * matrix_count : 3 * matrix_count]
    )
    update_norm = jnp.maximum(update_norm, 0.0)[:, None, None]

    new_momentum = mom_beta * own_momentum + clip_factor * grad_rows
    nesterov = clip_factor * grad_rows + mom_beta * new_momentum
    scaled = (nesterov / (jnp.sqrt(update_norm) + 1e-07)).astype(jnp.bfloat16)

    owner_count = shard_count // matrix_count
    if owner_count == 1:
        row_block = lax.all_to_all(scaled, "shard", split_axis=0, concat_axis=0, tiled=True)
        row_block = row_block.reshape(shard_count * local_height, width)
    else:
        everything = lax.all_gather(scaled, "shard", axis=1, tiled=True)
        row_block = lax.dynamic_index_in_dim(
            everything, shard_index // owner_count, 0, keepdims=False
        )

    blocks = [row_block]
    for offset in range(1, tensor_count):
        pairs = [(i, i ^ offset) for i in range(tensor_count)]
        blocks.append(lax.ppermute(row_block, "tensor", pairs))
    own_result = orthogonalize(blocks)

    if owner_count == 1:
        own_update = lax.all_to_all(
            own_result.reshape(shard_count, local_height, width),
            "shard",
            split_axis=0,
            concat_axis=0,
            tiled=True,
        )
    else:
        piece_length = local_height * width // owner_count
        split_rows = own_result.reshape(shard_count, owner_count, piece_length)
        returning = lax.dynamic_index_in_dim(
            split_rows, shard_index % owner_count, 1, keepdims=False
        )
        received = lax.all_to_all(returning, "shard", split_axis=0, concat_axis=0, tiled=True)
        own_update = received.reshape(matrix_count, local_height, width)
    orthogonal_update = own_update[None]
    muon_scale = 0.2 * math.sqrt(D)
    new_weights = (
        weights.astype(jnp.float32) * (1.0 - muon_rate * muon_decay)
        - muon_rate * muon_scale * orthogonal_update.astype(jnp.float32)
    ).astype(jnp.bfloat16)
    vector_clipped = clip_factor * vector_rows
    updated_first = 0.9 * first_moment + 0.1 * vector_clipped
    updated_second = 0.999 * second_moment + 0.001 * vector_clipped * vector_clipped
    adam_direction = updated_first / (jnp.sqrt(updated_second) + 1e-08)
    new_vectors = vectors * (1.0 - adam_rate * adam_decay) - adam_rate * adam_direction
    return (new_momentum[None], orthogonal_update, new_weights, adam_direction, new_vectors)


def solution(mesh):
    in_specs = (
        P("shard", "section", None, "tensor", None),
        P("shard", "section", None, "tensor"),
        P("section", None, ("tensor", "shard"), None),
        P("section", None, ("tensor", "shard"), None),
        P("section", None, ("tensor", "shard")),
        P("section", None, ("tensor", "shard")),
        P("section", None, ("tensor", "shard")),
    )
    out_specs = (
        P("section", None, ("tensor", "shard"), None),
        P("section", None, ("tensor", "shard"), None),
        P("section", None, ("tensor", "shard"), None),
        P("section", None, ("tensor", "shard")),
        P("section", None, ("tensor", "shard")),
    )
    return jax.shard_map(
        per_device, mesh=mesh, in_specs=in_specs, out_specs=out_specs, check_vma=False
    )
```

```python
import functools
import math

import jax
import jax.numpy as jnp
from jax import lax
from jax.experimental import pallas as pl
from jax.experimental.pallas import tpu as pltpu
from jax.sharding import PartitionSpec as P

D = 1024
NS_STEPS = 2


ns_first = 3.4445
ns_second = -4.775
ns_third = 2.0315
mom_beta = 0.95
max_norm = 1024.0
muon_rate = 0.02
muon_decay = 0.1
adam_rate = 0.001
adam_decay = 0.01

VECTOR_ROWS = 16
FIGURES = 16
LANES = 128
MESH_AXES = ("shard", "tensor", "section")


def gram_of(blocks, gram_ref):
    width = blocks[0].shape[1]
    step = 256
    for start in range(0, width, step):
        total = None
        for block in blocks:
            whole = block[...]
            part = whole[:, start : start + step]
            product = lax.dot_general(
                whole, part, (((0,), (0,)), ((), ())), preferred_element_type=jnp.float32
            )
            rounded = product.astype(jnp.bfloat16).astype(jnp.float32)
            total = rounded if total is None else total + rounded
        gram_ref[:, start : start + step] = total.astype(jnp.bfloat16)


def polynomial(block, gram_ref):
    gram = gram_ref[...]
    first = jnp.dot(block, gram, preferred_element_type=jnp.float32).astype(jnp.bfloat16)
    second = jnp.dot(first, gram, preferred_element_type=jnp.float32)
    combined = (
        ns_first * block.astype(jnp.float32)
        + ns_second * first.astype(jnp.float32)
        + ns_third * second
    )
    return combined.astype(jnp.bfloat16)


def orthogonalize_kernel(count, pieces, *refs):
    height, width = refs[0].shape
    inputs = refs[: count * pieces]
    outputs = refs[count * pieces : count * pieces + pieces]
    gram_ref, start_ref, next_ref = refs[count * pieces + pieces :]
    for position in range(count):
        for piece in range(pieces):
            start_ref[position, piece * height : (piece + 1) * height, :] = inputs[
                position * pieces + piece
            ][...]
    current, other = start_ref, next_ref
    for iteration in range(NS_STEPS - 1):
        gram_of([current.at[position] for position in range(count)], gram_ref)
        for position in range(count):
            other[position] = polynomial(current[position], gram_ref)
        current, other = other, current
    gram_of([current.at[position] for position in range(count)], gram_ref)
    result = polynomial(current[0], gram_ref)
    for piece in range(pieces):
        outputs[piece][...] = result[piece * height : (piece + 1) * height, :]


def orthogonalize(blocks):
    count, pieces = len(blocks), len(blocks[0])
    height, width = blocks[0][0].shape
    return pl.pallas_call(
        functools.partial(orthogonalize_kernel, count, pieces),
        out_shape=[jax.ShapeDtypeStruct((height, width), jnp.bfloat16)] * pieces,
        scratch_shapes=[
            pltpu.VMEM((width, width), jnp.bfloat16),
            pltpu.VMEM((count, pieces * height, width), jnp.bfloat16),
            pltpu.VMEM((count, pieces * height, width), jnp.bfloat16),
        ],
        compiler_params=pltpu.CompilerParams(vmem_limit_bytes=48 * 2**20),
    )(*[piece for block in blocks for piece in block])


def folded(array):
    line = jnp.sum(array, axis=0, keepdims=True)
    total = line[:, :LANES]
    for start in range(LANES, line.shape[1], LANES):
        total = total + line[:, start : start + LANES]
    return total


def sum_kernel(shard_count, section_ref, *refs):
    parts = refs[:shard_count]
    vector_parts = refs[shard_count : 2 * shard_count]
    momentum_ref, grad_ref, vector_ref, figures_ref = refs[2 * shard_count :]
    vector = vector_parts[0][...].astype(jnp.float32)
    for part in vector_parts[1:]:
        vector = vector + part[...].astype(jnp.float32)
    vector_ref[...] = vector
    total = folded(vector * vector) * (1.0 / shard_count)
    squares, crosses, momentum_squares = [], [], []
    for matrix in range(momentum_ref.shape[0]):
        grad = parts[0][matrix].astype(jnp.float32)
        for part in parts[1:]:
            grad = grad + part[matrix].astype(jnp.float32)
        grad_ref[matrix] = grad
        old = momentum_ref[matrix]
        squares.append(folded(grad * grad))
        crosses.append(folded(grad * old))
        momentum_squares.append(folded(old * old))
        total = total + squares[-1]
    lines = squares + crosses + momentum_squares + [total]
    lines = lines + [jnp.zeros_like(total)] * (FIGURES - len(lines))
    tile = jnp.concatenate(lines, axis=0)
    line_index = lax.broadcasted_iota(jnp.int32, tile.shape, 0)
    total_only = jnp.where(line_index == 3 * momentum_ref.shape[0], tile, 0.0)
    for section in range(figures_ref.shape[1]):
        chosen = jnp.where(section_ref[0] == section, tile, total_only)
        figures_ref[:, section] = jnp.broadcast_to(
            chosen[None], (figures_ref.shape[0],) + tile.shape
        )


def scale_kernel(matrix_count, order_ref, figures_ref, grad_ref, momentum_ref, *refs):
    outputs, clip_ref = refs[:matrix_count], refs[matrix_count]
    sums = jnp.sum(jnp.sum(figures_ref[...], axis=0), axis=1, keepdims=True)
    total = sums[3 * matrix_count : 3 * matrix_count + 1]
    clip = jnp.minimum(1.0, max_norm / (jnp.sqrt(total) + 1e-06))
    clip_ref[...] = jnp.broadcast_to(clip, clip_ref.shape)
    grad_scale = (1.0 + mom_beta) * clip
    momentum_scale = mom_beta * mom_beta
    update_norm = (
        grad_scale * grad_scale * sums[:matrix_count]
        + 2.0 * grad_scale * momentum_scale * sums[matrix_count : 2 * matrix_count]
        + momentum_scale * momentum_scale * sums[2 * matrix_count : 3 * matrix_count]
    )
    inverse = 1.0 / (jnp.sqrt(jnp.maximum(update_norm, 0.0)) + 1e-07)
    position = lax.broadcasted_iota(jnp.int32, inverse.shape, 0)
    for place in range(matrix_count):
        matrix = order_ref[place]
        factor = jnp.sum(jnp.where(position == matrix, inverse, 0.0), axis=0, keepdims=True)
        clipped = clip * grad_ref[matrix]
        nesterov = clipped + mom_beta * (mom_beta * momentum_ref[matrix] + clipped)
        outputs[place][...] = (nesterov * factor).astype(jnp.bfloat16)


def end_kernel(matrix_count, order_ref, *refs):
    arrived = refs[:matrix_count]
    weights_ref, update_ref, new_weights_ref = refs[matrix_count:]
    step_size = muon_rate * (0.2 * math.sqrt(D))
    for place in range(matrix_count):
        matrix = order_ref[place]
        update = arrived[place][...]
        update_ref[matrix] = update
        new_weights_ref[matrix] = (
            weights_ref[matrix].astype(jnp.float32) * (1.0 - muon_rate * muon_decay)
            - step_size * update.astype(jnp.float32)
        ).astype(jnp.bfloat16)


def on_device(kernel, scalars, operands, out_shape):
    return pl.pallas_call(
        kernel,
        out_shape=out_shape,
        in_specs=[pl.BlockSpec(memory_space=pltpu.SMEM)]
        + [pl.BlockSpec(memory_space=pltpu.VMEM)] * len(operands),
        compiler_params=pltpu.CompilerParams(vmem_limit_bytes=32 * 2**20),
    )(scalars, *operands)


def swapped(array, axis, offset):
    pairs = [(i, i ^ offset) for i in range(lax.axis_size(axis))]
    return lax.ppermute(array, axis, pairs)


def per_device(grad_parts, vector_grads, momentum, weights, vectors, first_moment, second_moment):
    shard_count = lax.axis_size("shard")
    tensor_count = lax.axis_size("tensor")
    section_count = lax.axis_size("section")
    _, matrix_count, local_height, width = momentum.shape
    if shard_count != matrix_count or shard_count != 4 or tensor_count != 4:
        return general_device(
            grad_parts, vector_grads, momentum, weights, vectors, first_moment, second_moment
        )
    shard_index = lax.axis_index("shard")
    order = shard_index ^ jnp.arange(shard_count, dtype=jnp.int32)
    own_momentum = momentum[0]
    vector_count, vector_width = vectors.shape[1:]

    by_rows = grad_parts.reshape(matrix_count, shard_count, local_height, width)
    own_vectors = vector_grads.reshape(vector_count, shard_count * vector_width)
    parts = [None] * shard_count
    vector_parts = [own_vectors] + [None] * (shard_count - 1)
    for offset in reversed(range(shard_count)):
        rows = lax.dynamic_index_in_dim(by_rows, shard_index ^ offset, 1, keepdims=False)
        parts[offset] = swapped(rows, "shard", offset) if offset else rows
    for offset in range(1, shard_count):
        vector_parts[offset] = swapped(own_vectors, "shard", offset)

    others = shard_count * tensor_count
    grad_rows, vector_whole, figures = on_device(
        functools.partial(sum_kernel, shard_count),
        lax.axis_index("section").astype(jnp.int32).reshape(1),
        parts + vector_parts + [own_momentum],
        [
            jax.ShapeDtypeStruct(own_momentum.shape, jnp.float32),
            jax.ShapeDtypeStruct(own_vectors.shape, jnp.float32),
            jax.ShapeDtypeStruct((others, section_count, FIGURES, LANES), jnp.float32),
        ],
    )
    figures = lax.all_to_all(
        figures.reshape(others * section_count, FIGURES, LANES),
        MESH_AXES,
        split_axis=0,
        concat_axis=0,
        tiled=True,
    )
    *scaled, clip_tile = on_device(
        functools.partial(scale_kernel, matrix_count),
        order,
        [figures, grad_rows, own_momentum],
        [jax.ShapeDtypeStruct((local_height, width), jnp.bfloat16)] * matrix_count
        + [jax.ShapeDtypeStruct((8, LANES), jnp.float32)],
    )

    blocks = [[], [], [], []]
    for offset in range(shard_count):
        piece = swapped(scaled[offset], "shard", offset) if offset else scaled[0]
        near = swapped(piece, "tensor", 1)
        side = swapped(piece, "tensor", 2)
        far = swapped(near, "tensor", 2) if offset % 2 == 0 else swapped(side, "tensor", 1)
        for block, held in zip(blocks, (piece, near, side, far)):
            block.append(held)
    results = orthogonalize(blocks)

    arrived = [
        swapped(results[offset], "shard", offset) if offset else results[0]
        for offset in range(shard_count)
    ]
    orthogonal_update, new_weights = on_device(
        functools.partial(end_kernel, matrix_count),
        order,
        arrived + [weights[0]],
        [jax.ShapeDtypeStruct(own_momentum.shape, jnp.bfloat16)] * 2,
    )

    clip_factor = clip_tile[0, 0]
    new_momentum = mom_beta * own_momentum + clip_factor * grad_rows
    vector_rows = lax.dynamic_slice_in_dim(
        vector_whole, shard_index * vector_width, vector_width, 1
    )
    vector_clipped = clip_factor * vector_rows
    updated_first = 0.9 * first_moment + 0.1 * vector_clipped
    updated_second = 0.999 * second_moment + 0.001 * vector_clipped * vector_clipped
    adam_direction = updated_first / (jnp.sqrt(updated_second) + 1e-08)
    new_vectors = vectors * (1.0 - adam_rate * adam_decay) - adam_rate * adam_direction
    return (
        new_momentum[None],
        orthogonal_update[None],
        new_weights[None],
        adam_direction,
        new_vectors,
    )


def general_device(grad_parts, vector_grads, momentum, weights, vectors, first_moment, second_moment):
    shard_count = lax.axis_size("shard")
    tensor_count = lax.axis_size("tensor")
    section_count = lax.axis_size("section")
    shard_index = lax.axis_index("shard")
    _, matrix_count, local_height, width = momentum.shape
    vector_width = vectors.shape[2]
    own_momentum = momentum[0]

    rows = matrix_count * local_height
    by_target = (
        grad_parts.reshape(matrix_count, shard_count, local_height, width)
        .transpose(1, 0, 2, 3)
        .reshape(shard_count, rows, width)
    )
    vector_line = jnp.broadcast_to(
        vector_grads.reshape(1, 1, width), (shard_count, VECTOR_ROWS, width)
    )
    payload = jnp.concatenate([by_target, vector_line], axis=1)
    arrived = lax.all_to_all(payload, "shard", split_axis=0, concat_axis=0, tiled=True)
    grad_rows = jnp.sum(arrived[:, :rows].astype(jnp.float32), axis=0).reshape(
        matrix_count, local_height, width
    )
    vector_whole = jnp.sum(arrived[:, rows].astype(jnp.float32), axis=0).reshape(
        vectors.shape[1], vector_width * shard_count
    )
    vector_rows = lax.dynamic_slice_in_dim(
        vector_whole, shard_index * vector_width, vector_width, 1
    )

    grad_squares = jnp.sum(grad_rows * grad_rows, axis=(1, 2))
    cross = jnp.sum(grad_rows * own_momentum, axis=(1, 2))
    momentum_squares = jnp.sum(own_momentum * own_momentum, axis=(1, 2))
    own_total = jnp.sum(grad_squares) + jnp.sum(vector_rows * vector_rows)
    same_section = (
        jnp.arange(section_count) == lax.axis_index("section")
    ).astype(jnp.float32)[:, None]
    matrix_figures = jnp.concatenate([grad_squares, cross, momentum_squares])
    line = jnp.concatenate(
        [
            same_section * matrix_figures[None],
            jnp.broadcast_to(own_total, (section_count, 1)),
            jnp.zeros((section_count, 127 - 3 * matrix_count), jnp.float32),
        ],
        axis=1,
    )
    others = shard_count * tensor_count
    figures = jnp.broadcast_to(line[None, :, None, :], (others, section_count, 8, 128)).reshape(
        others * section_count, 8, 128
    )
    figures = lax.all_to_all(figures, MESH_AXES, split_axis=0, concat_axis=0, tiled=True)
    sums = jnp.sum(figures[:, 0, :], axis=0)
    grand_total = sums[3 * matrix_count]
    clip_factor = jnp.minimum(1.0, max_norm / (jnp.sqrt(grand_total) + 1e-06))
    grad_scale = (1.0 + mom_beta) * clip_factor
    momentum_scale = mom_beta * mom_beta
    update_norm = (
        grad_scale * grad_scale * sums[:matrix_count]
        + 2.0 * grad_scale * momentum_scale * sums[matrix_count : 2 * matrix_count]
        + momentum_scale * momentum_scale * sums[2 * matrix_count : 3 * matrix_count]
    )
    update_norm = jnp.maximum(update_norm, 0.0)[:, None, None]

    new_momentum = mom_beta * own_momentum + clip_factor * grad_rows
    nesterov = clip_factor * grad_rows + mom_beta * new_momentum
    scaled = (nesterov / (jnp.sqrt(update_norm) + 1e-07)).astype(jnp.bfloat16)

    owner_count = shard_count // matrix_count
    if owner_count == 1:
        row_block = lax.all_to_all(scaled, "shard", split_axis=0, concat_axis=0, tiled=True)
        row_block = row_block.reshape(shard_count * local_height, width)
    else:
        everything = lax.all_gather(scaled, "shard", axis=1, tiled=True)
        row_block = lax.dynamic_index_in_dim(
            everything, shard_index // owner_count, 0, keepdims=False
        )

    blocks = [row_block]
    for offset in range(1, tensor_count):
        pairs = [(i, i ^ offset) for i in range(tensor_count)]
        blocks.append(lax.ppermute(row_block, "tensor", pairs))
    (own_result,) = orthogonalize([[block] for block in blocks])

    if owner_count == 1:
        own_update = lax.all_to_all(
            own_result.reshape(shard_count, local_height, width),
            "shard",
            split_axis=0,
            concat_axis=0,
            tiled=True,
        )
    else:
        piece_length = local_height * width // owner_count
        split_rows = own_result.reshape(shard_count, owner_count, piece_length)
        returning = lax.dynamic_index_in_dim(
            split_rows, shard_index % owner_count, 1, keepdims=False
        )
        received = lax.all_to_all(returning, "shard", split_axis=0, concat_axis=0, tiled=True)
        own_update = received.reshape(matrix_count, local_height, width)
    orthogonal_update = own_update[None]
    muon_scale = 0.2 * math.sqrt(D)
    new_weights = (
        weights.astype(jnp.float32) * (1.0 - muon_rate * muon_decay)
        - muon_rate * muon_scale * orthogonal_update.astype(jnp.float32)
    ).astype(jnp.bfloat16)
    vector_clipped = clip_factor * vector_rows
    updated_first = 0.9 * first_moment + 0.1 * vector_clipped
    updated_second = 0.999 * second_moment + 0.001 * vector_clipped * vector_clipped
    adam_direction = updated_first / (jnp.sqrt(updated_second) + 1e-08)
    new_vectors = vectors * (1.0 - adam_rate * adam_decay) - adam_rate * adam_direction
    return (new_momentum[None], orthogonal_update, new_weights, adam_direction, new_vectors)


def solution(mesh):
    in_specs = (
        P("shard", "section", None, "tensor", None),
        P("shard", "section", None, "tensor"),
        P("section", None, ("tensor", "shard"), None),
        P("section", None, ("tensor", "shard"), None),
        P("section", None, ("tensor", "shard")),
        P("section", None, ("tensor", "shard")),
        P("section", None, ("tensor", "shard")),
    )
    out_specs = (
        P("section", None, ("tensor", "shard"), None),
        P("section", None, ("tensor", "shard"), None),
        P("section", None, ("tensor", "shard"), None),
        P("section", None, ("tensor", "shard")),
        P("section", None, ("tensor", "shard")),
    )
    return jax.shard_map(
        per_device, mesh=mesh, in_specs=in_specs, out_specs=out_specs, check_vma=False
    )
```

```python
import functools
import math

import jax
import jax.numpy as jnp
from jax import lax
from jax.experimental import pallas as pl
from jax.experimental.pallas import tpu as pltpu
from jax.sharding import PartitionSpec as P

D = 1024
NS_STEPS = 2


ns_first = 3.4445
ns_second = -4.775
ns_third = 2.0315
mom_beta = 0.95
max_norm = 1024.0
muon_rate = 0.02
muon_decay = 0.1
adam_rate = 0.001
adam_decay = 0.01

VECTOR_ROWS = 16
FIGURES = 16
MIB = 2**20
LANES = 128
MESH_AXES = ("shard", "tensor", "section")


def gram_of(blocks, gram_ref):
    width = blocks[0].shape[1]
    step = 256
    for start in range(0, width, step):
        total = None
        for block in blocks:
            whole = block[...]
            part = whole[:, start : start + step]
            product = lax.dot_general(
                whole, part, (((0,), (0,)), ((), ())), preferred_element_type=jnp.float32
            )
            rounded = product.astype(jnp.bfloat16).astype(jnp.float32)
            total = rounded if total is None else total + rounded
        gram_ref[:, start : start + step] = total.astype(jnp.bfloat16)


def polynomial(block, gram_ref):
    gram = gram_ref[...]
    first = jnp.dot(block, gram, preferred_element_type=jnp.float32).astype(jnp.bfloat16)
    second = jnp.dot(first, gram, preferred_element_type=jnp.float32)
    combined = (
        ns_first * block.astype(jnp.float32)
        + ns_second * first.astype(jnp.float32)
        + ns_third * second
    )
    return combined.astype(jnp.bfloat16)


def orthogonalize_kernel(count, pieces, *refs):
    height, width = refs[0].shape
    inputs = refs[: count * pieces]
    outputs = refs[count * pieces : count * pieces + pieces]
    gram_ref, start_ref, next_ref = refs[count * pieces + pieces :]
    for position in range(count):
        for piece in range(pieces):
            start_ref[position, piece * height : (piece + 1) * height, :] = inputs[
                position * pieces + piece
            ][...]
    current, other = start_ref, next_ref
    for iteration in range(NS_STEPS - 1):
        gram_of([current.at[position] for position in range(count)], gram_ref)
        for position in range(count):
            other[position] = polynomial(current[position], gram_ref)
        current, other = other, current
    gram_of([current.at[position] for position in range(count)], gram_ref)
    result = polynomial(current[0], gram_ref)
    for piece in range(pieces):
        outputs[piece][...] = result[piece * height : (piece + 1) * height, :]


def orthogonalize(blocks):
    count, pieces = len(blocks), len(blocks[0])
    height, width = blocks[0][0].shape
    return pl.pallas_call(
        functools.partial(orthogonalize_kernel, count, pieces),
        out_shape=[jax.ShapeDtypeStruct((height, width), jnp.bfloat16)] * pieces,
        scratch_shapes=[
            pltpu.VMEM((width, width), jnp.bfloat16),
            pltpu.VMEM((count, pieces * height, width), jnp.bfloat16),
            pltpu.VMEM((count, pieces * height, width), jnp.bfloat16),
        ],
        compiler_params=pltpu.CompilerParams(vmem_limit_bytes=24 * MIB),
    )(*[piece for block in blocks for piece in block])


def folded(array):
    line = jnp.sum(array, axis=0, keepdims=True)
    total = line[:, :LANES]
    for start in range(LANES, line.shape[1], LANES):
        total = total + line[:, start : start + LANES]
    return total


def sum_kernel(shard_count, section_ref, *refs):
    parts = refs[:shard_count]
    vector_parts = refs[shard_count : 2 * shard_count]
    momentum_ref, grad_ref, vector_ref, figures_ref = refs[2 * shard_count :]
    vector = vector_parts[0][...].astype(jnp.float32)
    for part in vector_parts[1:]:
        vector = vector + part[...].astype(jnp.float32)
    vector_ref[...] = vector
    total = folded(vector * vector) * (1.0 / shard_count)
    squares, crosses, momentum_squares = [], [], []
    for matrix in range(momentum_ref.shape[0]):
        grad = parts[0][matrix].astype(jnp.float32)
        for part in parts[1:]:
            grad = grad + part[matrix].astype(jnp.float32)
        grad_ref[matrix] = grad
        old = momentum_ref[matrix]
        squares.append(folded(grad * grad))
        crosses.append(folded(grad * old))
        momentum_squares.append(folded(old * old))
        total = total + squares[-1]
    lines = squares + crosses + momentum_squares + [total]
    lines = lines + [jnp.zeros_like(total)] * (FIGURES - len(lines))
    tile = jnp.concatenate(lines, axis=0)
    sums = jnp.sum(tile, axis=1, keepdims=True)
    line_index = lax.broadcasted_iota(jnp.int32, tile.shape, 0)
    lane_index = lax.broadcasted_iota(jnp.int32, tile.shape, 1)
    line = jnp.sum(jnp.where(line_index == lane_index, sums, 0.0), axis=0, keepdims=True)
    total_only = jnp.where(lane_index[:1] == 3 * momentum_ref.shape[0], line, 0.0)
    for section in range(figures_ref.shape[1]):
        chosen = jnp.where(section_ref[0] == section, line, total_only)
        figures_ref[:, section] = jnp.broadcast_to(
            chosen[None], (figures_ref.shape[0],) + line.shape
        )


def scale_kernel(matrix_count, order_ref, figures_ref, grad_ref, momentum_ref, *refs):
    outputs = refs[:matrix_count]
    clip_ref, new_momentum_ref = refs[matrix_count:]
    line = jnp.sum(figures_ref[...], axis=0)
    line_index = lax.broadcasted_iota(jnp.int32, (FIGURES, LANES), 0)
    lane_index = lax.broadcasted_iota(jnp.int32, (FIGURES, LANES), 1)
    sums = jnp.sum(jnp.where(line_index == lane_index, line, 0.0), axis=1, keepdims=True)
    total = sums[3 * matrix_count : 3 * matrix_count + 1]
    clip = jnp.minimum(1.0, max_norm / (jnp.sqrt(total) + 1e-06))
    clip_ref[...] = jnp.broadcast_to(clip, clip_ref.shape)
    grad_scale = (1.0 + mom_beta) * clip
    momentum_scale = mom_beta * mom_beta
    update_norm = (
        grad_scale * grad_scale * sums[:matrix_count]
        + 2.0 * grad_scale * momentum_scale * sums[matrix_count : 2 * matrix_count]
        + momentum_scale * momentum_scale * sums[2 * matrix_count : 3 * matrix_count]
    )
    inverse = 1.0 / (jnp.sqrt(jnp.maximum(update_norm, 0.0)) + 1e-07)
    position = lax.broadcasted_iota(jnp.int32, inverse.shape, 0)
    for place in range(matrix_count):
        matrix = order_ref[place]
        factor = jnp.sum(jnp.where(position == matrix, inverse, 0.0), axis=0, keepdims=True)
        clipped = clip * grad_ref[matrix]
        new_momentum = mom_beta * momentum_ref[matrix] + clipped
        new_momentum_ref[matrix] = new_momentum
        nesterov = clipped + mom_beta * new_momentum
        outputs[place][...] = (nesterov * factor).astype(jnp.bfloat16)


def end_kernel(matrix_count, order_ref, *refs):
    arrived = refs[:matrix_count]
    weights_ref, update_ref, new_weights_ref = refs[matrix_count:]
    step_size = muon_rate * (0.2 * math.sqrt(D))
    for place in range(matrix_count):
        matrix = order_ref[place]
        update = arrived[place][...]
        update_ref[matrix] = update
        new_weights_ref[matrix] = (
            weights_ref[matrix].astype(jnp.float32) * (1.0 - muon_rate * muon_decay)
            - step_size * update.astype(jnp.float32)
        ).astype(jnp.bfloat16)


def on_device(kernel, scalars, operands, out_shape):
    return pl.pallas_call(
        kernel,
        out_shape=out_shape,
        in_specs=[pl.BlockSpec(memory_space=pltpu.SMEM)]
        + [pl.BlockSpec(memory_space=pltpu.VMEM)] * len(operands),
        compiler_params=pltpu.CompilerParams(vmem_limit_bytes=12 * MIB),
    )(scalars, *operands)


def swapped(array, axis, offset):
    pairs = [(i, i ^ offset) for i in range(lax.axis_size(axis))]
    return lax.ppermute(array, axis, pairs)


def after(array, earlier):
    return lax.optimization_barrier((array, earlier))[0]


def per_device(grad_parts, vector_grads, momentum, weights, vectors, first_moment, second_moment):
    shard_count = lax.axis_size("shard")
    tensor_count = lax.axis_size("tensor")
    section_count = lax.axis_size("section")
    _, matrix_count, local_height, width = momentum.shape
    if shard_count != matrix_count or shard_count != 4 or tensor_count != 4:
        return general_device(
            grad_parts, vector_grads, momentum, weights, vectors, first_moment, second_moment
        )
    shard_index = lax.axis_index("shard")
    order = shard_index ^ jnp.arange(shard_count, dtype=jnp.int32)
    own_momentum = momentum[0]
    vector_count, vector_width = vectors.shape[1:]

    by_rows = grad_parts.reshape(matrix_count, shard_count, local_height, width)
    own_vectors = vector_grads.reshape(vector_count, shard_count * vector_width)
    vector_parts = [own_vectors] + [
        swapped(own_vectors, "shard", offset) for offset in range(1, shard_count)
    ]
    parts = [None] * shard_count
    index = shard_index
    for offset in reversed(range(shard_count)):
        rows = lax.dynamic_index_in_dim(by_rows, index ^ offset, 1, keepdims=False)
        index, rows, vector_parts = lax.optimization_barrier((index, rows, vector_parts))
        parts[offset] = swapped(rows, "shard", offset) if offset else rows

    others = shard_count * tensor_count
    grad_rows, vector_whole, figures = on_device(
        functools.partial(sum_kernel, shard_count),
        lax.axis_index("section").astype(jnp.int32).reshape(1),
        parts + vector_parts + [own_momentum],
        [
            jax.ShapeDtypeStruct(own_momentum.shape, jnp.float32),
            jax.ShapeDtypeStruct(own_vectors.shape, jnp.float32),
            jax.ShapeDtypeStruct((others, section_count, 1, LANES), jnp.float32),
        ],
    )
    figures = lax.all_to_all(
        figures.reshape(others * section_count, 1, LANES),
        MESH_AXES,
        split_axis=0,
        concat_axis=0,
        tiled=True,
    )
    *scaled, clip_tile, new_momentum = on_device(
        functools.partial(scale_kernel, matrix_count),
        order,
        [figures, grad_rows, own_momentum],
        [jax.ShapeDtypeStruct((local_height, width), jnp.bfloat16)] * matrix_count
        + [
            jax.ShapeDtypeStruct((8, LANES), jnp.float32),
            jax.ShapeDtypeStruct(own_momentum.shape, jnp.float32),
        ],
    )

    pieces = [scaled[0]] + [None] * 3
    for offset in (2, 3, 1):
        pieces[offset] = swapped(scaled[offset], "shard", offset)
    near, side, far = [None] * 4, [None] * 4, [None] * 4
    near[0] = swapped(pieces[0], "tensor", 1)
    side[0] = swapped(pieces[0], "tensor", 2)
    far[0] = swapped(near[0], "tensor", 2)
    near[1] = swapped(pieces[1], "tensor", 1)
    side[1] = swapped(after(pieces[1], side[0]), "tensor", 2)
    far[1] = swapped(side[1], "tensor", 1)
    near[2] = swapped(after(pieces[2], far[0]), "tensor", 1)
    side[2] = swapped(after(pieces[2], near[1]), "tensor", 2)
    far[2] = swapped(near[2], "tensor", 2)
    near[3] = swapped(after(pieces[3], far[1]), "tensor", 1)
    side[3] = swapped(after(pieces[3], side[2]), "tensor", 2)
    far[3] = swapped(side[3], "tensor", 1)
    results = orthogonalize([pieces, near, side, far])

    arrived = [
        swapped(results[offset], "shard", offset) if offset else results[0]
        for offset in range(shard_count)
    ]
    orthogonal_update, new_weights = on_device(
        functools.partial(end_kernel, matrix_count),
        order,
        arrived + [weights[0]],
        [jax.ShapeDtypeStruct(own_momentum.shape, jnp.bfloat16)] * 2,
    )

    clip_factor = after(clip_tile, results[0])[0, 0]
    vector_rows = lax.dynamic_slice_in_dim(
        vector_whole, shard_index * vector_width, vector_width, 1
    )
    vector_clipped = clip_factor * vector_rows
    updated_first = 0.9 * first_moment + 0.1 * vector_clipped
    updated_second = 0.999 * second_moment + 0.001 * vector_clipped * vector_clipped
    adam_direction = updated_first / (jnp.sqrt(updated_second) + 1e-08)
    new_vectors = vectors * (1.0 - adam_rate * adam_decay) - adam_rate * adam_direction
    return (
        new_momentum[None],
        orthogonal_update[None],
        new_weights[None],
        adam_direction,
        new_vectors,
    )


def general_device(grad_parts, vector_grads, momentum, weights, vectors, first_moment, second_moment):
    shard_count = lax.axis_size("shard")
    tensor_count = lax.axis_size("tensor")
    section_count = lax.axis_size("section")
    shard_index = lax.axis_index("shard")
    _, matrix_count, local_height, width = momentum.shape
    vector_width = vectors.shape[2]
    own_momentum = momentum[0]

    rows = matrix_count * local_height
    by_target = (
        grad_parts.reshape(matrix_count, shard_count, local_height, width)
        .transpose(1, 0, 2, 3)
        .reshape(shard_count, rows, width)
    )
    vector_line = jnp.broadcast_to(
        vector_grads.reshape(1, 1, width), (shard_count, VECTOR_ROWS, width)
    )
    payload = jnp.concatenate([by_target, vector_line], axis=1)
    arrived = lax.all_to_all(payload, "shard", split_axis=0, concat_axis=0, tiled=True)
    grad_rows = jnp.sum(arrived[:, :rows].astype(jnp.float32), axis=0).reshape(
        matrix_count, local_height, width
    )
    vector_whole = jnp.sum(arrived[:, rows].astype(jnp.float32), axis=0).reshape(
        vectors.shape[1], vector_width * shard_count
    )
    vector_rows = lax.dynamic_slice_in_dim(
        vector_whole, shard_index * vector_width, vector_width, 1
    )

    grad_squares = jnp.sum(grad_rows * grad_rows, axis=(1, 2))
    cross = jnp.sum(grad_rows * own_momentum, axis=(1, 2))
    momentum_squares = jnp.sum(own_momentum * own_momentum, axis=(1, 2))
    own_total = jnp.sum(grad_squares) + jnp.sum(vector_rows * vector_rows)
    same_section = (
        jnp.arange(section_count) == lax.axis_index("section")
    ).astype(jnp.float32)[:, None]
    matrix_figures = jnp.concatenate([grad_squares, cross, momentum_squares])
    line = jnp.concatenate(
        [
            same_section * matrix_figures[None],
            jnp.broadcast_to(own_total, (section_count, 1)),
            jnp.zeros((section_count, 127 - 3 * matrix_count), jnp.float32),
        ],
        axis=1,
    )
    others = shard_count * tensor_count
    figures = jnp.broadcast_to(line[None, :, None, :], (others, section_count, 8, 128)).reshape(
        others * section_count, 8, 128
    )
    figures = lax.all_to_all(figures, MESH_AXES, split_axis=0, concat_axis=0, tiled=True)
    sums = jnp.sum(figures[:, 0, :], axis=0)
    grand_total = sums[3 * matrix_count]
    clip_factor = jnp.minimum(1.0, max_norm / (jnp.sqrt(grand_total) + 1e-06))
    grad_scale = (1.0 + mom_beta) * clip_factor
    momentum_scale = mom_beta * mom_beta
    update_norm = (
        grad_scale * grad_scale * sums[:matrix_count]
        + 2.0 * grad_scale * momentum_scale * sums[matrix_count : 2 * matrix_count]
        + momentum_scale * momentum_scale * sums[2 * matrix_count : 3 * matrix_count]
    )
    update_norm = jnp.maximum(update_norm, 0.0)[:, None, None]

    new_momentum = mom_beta * own_momentum + clip_factor * grad_rows
    nesterov = clip_factor * grad_rows + mom_beta * new_momentum
    scaled = (nesterov / (jnp.sqrt(update_norm) + 1e-07)).astype(jnp.bfloat16)

    owner_count = shard_count // matrix_count
    if owner_count == 1:
        row_block = lax.all_to_all(scaled, "shard", split_axis=0, concat_axis=0, tiled=True)
        row_block = row_block.reshape(shard_count * local_height, width)
    else:
        everything = lax.all_gather(scaled, "shard", axis=1, tiled=True)
        row_block = lax.dynamic_index_in_dim(
            everything, shard_index // owner_count, 0, keepdims=False
        )

    blocks = [row_block]
    for offset in range(1, tensor_count):
        pairs = [(i, i ^ offset) for i in range(tensor_count)]
        blocks.append(lax.ppermute(row_block, "tensor", pairs))
    (own_result,) = orthogonalize([[block] for block in blocks])

    if owner_count == 1:
        own_update = lax.all_to_all(
            own_result.reshape(shard_count, local_height, width),
            "shard",
            split_axis=0,
            concat_axis=0,
            tiled=True,
        )
    else:
        piece_length = local_height * width // owner_count
        split_rows = own_result.reshape(shard_count, owner_count, piece_length)
        returning = lax.dynamic_index_in_dim(
            split_rows, shard_index % owner_count, 1, keepdims=False
        )
        received = lax.all_to_all(returning, "shard", split_axis=0, concat_axis=0, tiled=True)
        own_update = received.reshape(matrix_count, local_height, width)
    orthogonal_update = own_update[None]
    muon_scale = 0.2 * math.sqrt(D)
    new_weights = (
        weights.astype(jnp.float32) * (1.0 - muon_rate * muon_decay)
        - muon_rate * muon_scale * orthogonal_update.astype(jnp.float32)
    ).astype(jnp.bfloat16)
    vector_clipped = clip_factor * vector_rows
    updated_first = 0.9 * first_moment + 0.1 * vector_clipped
    updated_second = 0.999 * second_moment + 0.001 * vector_clipped * vector_clipped
    adam_direction = updated_first / (jnp.sqrt(updated_second) + 1e-08)
    new_vectors = vectors * (1.0 - adam_rate * adam_decay) - adam_rate * adam_direction
    return (new_momentum[None], orthogonal_update, new_weights, adam_direction, new_vectors)


def solution(mesh):
    in_specs = (
        P("shard", "section", None, "tensor", None),
        P("shard", "section", None, "tensor"),
        P("section", None, ("tensor", "shard"), None),
        P("section", None, ("tensor", "shard"), None),
        P("section", None, ("tensor", "shard")),
        P("section", None, ("tensor", "shard")),
        P("section", None, ("tensor", "shard")),
    )
    out_specs = (
        P("section", None, ("tensor", "shard"), None),
        P("section", None, ("tensor", "shard"), None),
        P("section", None, ("tensor", "shard"), None),
        P("section", None, ("tensor", "shard")),
        P("section", None, ("tensor", "shard")),
    )
    return jax.shard_map(
        per_device, mesh=mesh, in_specs=in_specs, out_specs=out_specs, check_vma=False
    )
```

```python
import functools
import math

import jax
import jax.numpy as jnp
from jax import lax
from jax.experimental import pallas as pl
from jax.experimental.pallas import tpu as pltpu
from jax.sharding import PartitionSpec as P

D = 1024
NS_STEPS = 2


ns_first = 3.4445
ns_second = -4.775
ns_third = 2.0315
mom_beta = 0.95
max_norm = 1024.0
muon_rate = 0.02
muon_decay = 0.1
adam_rate = 0.001
adam_decay = 0.01

VECTOR_ROWS = 16
FIGURES = 16
MIB = 2**20
LANES = 128
MESH_AXES = ("shard", "tensor", "section")


def gram_of(blocks, gram_ref):
    width = blocks[0].shape[1]
    step = 256
    for start in range(0, width, step):
        total = None
        for block in blocks:
            whole = block[...]
            part = whole[:, start : start + step]
            product = lax.dot_general(
                whole, part, (((0,), (0,)), ((), ())), preferred_element_type=jnp.float32
            )
            rounded = product.astype(jnp.bfloat16).astype(jnp.float32)
            total = rounded if total is None else total + rounded
        gram_ref[:, start : start + step] = total.astype(jnp.bfloat16)


def polynomial(block, gram_ref):
    gram = gram_ref[...]
    first = jnp.dot(block, gram, preferred_element_type=jnp.float32).astype(jnp.bfloat16)
    second = jnp.dot(first, gram, preferred_element_type=jnp.float32)
    combined = (
        ns_first * block.astype(jnp.float32)
        + ns_second * first.astype(jnp.float32)
        + ns_third * second
    )
    return combined.astype(jnp.bfloat16)


def orthogonalize_kernel(count, pieces, *refs):
    height, width = refs[0].shape
    inputs = refs[: count * pieces]
    outputs = refs[count * pieces : count * pieces + pieces]
    gram_ref, start_ref, next_ref = refs[count * pieces + pieces :]
    for position in range(count):
        for piece in range(pieces):
            start_ref[position, piece * height : (piece + 1) * height, :] = inputs[
                position * pieces + piece
            ][...]
    current, other = start_ref, next_ref
    for iteration in range(NS_STEPS - 1):
        gram_of([current.at[position] for position in range(count)], gram_ref)
        for position in range(count):
            other[position] = polynomial(current[position], gram_ref)
        current, other = other, current
    gram_of([current.at[position] for position in range(count)], gram_ref)
    result = polynomial(current[0], gram_ref)
    for piece in range(pieces):
        outputs[piece][...] = result[piece * height : (piece + 1) * height, :]


def orthogonalize(blocks):
    count, pieces = len(blocks), len(blocks[0])
    height, width = blocks[0][0].shape
    return pl.pallas_call(
        functools.partial(orthogonalize_kernel, count, pieces),
        out_shape=[jax.ShapeDtypeStruct((height, width), jnp.bfloat16)] * pieces,
        scratch_shapes=[
            pltpu.VMEM((width, width), jnp.bfloat16),
            pltpu.VMEM((count, pieces * height, width), jnp.bfloat16),
            pltpu.VMEM((count, pieces * height, width), jnp.bfloat16),
        ],
        compiler_params=pltpu.CompilerParams(vmem_limit_bytes=32 * MIB),
    )(*[piece for block in blocks for piece in block])


def folded(array):
    line = jnp.sum(array, axis=0, keepdims=True)
    total = line[:, :LANES]
    for start in range(LANES, line.shape[1], LANES):
        total = total + line[:, start : start + LANES]
    return total


def slices_kernel(count, place_ref, grad_ref, *refs):
    outputs, semaphores = refs[:count], refs[count]
    copies = [
        pltpu.make_async_copy(
            grad_ref.at[:, place_ref[offset]], outputs[offset], semaphores.at[offset]
        )
        for offset in range(count)
    ]
    for copy in reversed(copies):
        copy.start()
    for copy in reversed(copies):
        copy.wait()


def row_slices(place, by_rows):
    matrix_count, shard_count, height, width = by_rows.shape
    return pl.pallas_call(
        functools.partial(slices_kernel, shard_count),
        out_shape=[jax.ShapeDtypeStruct((matrix_count, height, width), by_rows.dtype)]
        * shard_count,
        in_specs=[
            pl.BlockSpec(memory_space=pltpu.SMEM),
            pl.BlockSpec(memory_space=pltpu.HBM),
        ],
        out_specs=[pl.BlockSpec(memory_space=pltpu.HBM)] * shard_count,
        scratch_shapes=[pltpu.SemaphoreType.DMA((shard_count,))],
    )(place, by_rows)


def sum_kernel(shard_count, place_ref, *refs):
    parts = refs[:shard_count]
    vector_parts, momentum_ref, grad_ref, vector_ref, figures_ref = refs[shard_count:]
    vector = jnp.sum(vector_parts[...].astype(jnp.float32), axis=0)
    vector_ref[...] = vector
    total = folded(vector * vector) * (1.0 / shard_count)
    squares, crosses, momentum_squares = [], [], []
    for matrix in range(momentum_ref.shape[0]):
        grad = parts[0][matrix].astype(jnp.float32)
        for part in parts[1:]:
            grad = grad + part[matrix].astype(jnp.float32)
        grad_ref[matrix] = grad
        old = momentum_ref[matrix]
        squares.append(folded(grad * grad))
        crosses.append(folded(grad * old))
        momentum_squares.append(folded(old * old))
        total = total + squares[-1]
    lines = squares + crosses + momentum_squares + [total]
    lines = lines + [jnp.zeros_like(total)] * (FIGURES - len(lines))
    tile = jnp.concatenate(lines, axis=0)
    sums = jnp.sum(tile, axis=1, keepdims=True)
    line_index = lax.broadcasted_iota(jnp.int32, tile.shape, 0)
    lane_index = lax.broadcasted_iota(jnp.int32, tile.shape, 1)
    line = jnp.sum(jnp.where(line_index == lane_index, sums, 0.0), axis=0, keepdims=True)
    total_only = jnp.where(lane_index[:1] == 3 * momentum_ref.shape[0], line, 0.0)
    for section in range(figures_ref.shape[1]):
        chosen = jnp.where(place_ref[shard_count] == section, line, total_only)
        figures_ref[:, section] = jnp.broadcast_to(
            chosen[None], (figures_ref.shape[0],) + line.shape
        )


def scale_kernel(matrix_count, place_ref, figures_ref, grad_ref, momentum_ref, *refs):
    outputs = refs[:matrix_count]
    clip_ref, new_momentum_ref = refs[matrix_count:]
    line = jnp.sum(figures_ref[...], axis=0)
    line_index = lax.broadcasted_iota(jnp.int32, (FIGURES, LANES), 0)
    lane_index = lax.broadcasted_iota(jnp.int32, (FIGURES, LANES), 1)
    sums = jnp.sum(jnp.where(line_index == lane_index, line, 0.0), axis=1, keepdims=True)
    total = sums[3 * matrix_count : 3 * matrix_count + 1]
    clip = jnp.minimum(1.0, max_norm / (jnp.sqrt(total) + 1e-06))
    clip_ref[...] = jnp.broadcast_to(clip, clip_ref.shape)
    grad_scale = (1.0 + mom_beta) * clip
    momentum_scale = mom_beta * mom_beta
    update_norm = (
        grad_scale * grad_scale * sums[:matrix_count]
        + 2.0 * grad_scale * momentum_scale * sums[matrix_count : 2 * matrix_count]
        + momentum_scale * momentum_scale * sums[2 * matrix_count : 3 * matrix_count]
    )
    inverse = 1.0 / (jnp.sqrt(jnp.maximum(update_norm, 0.0)) + 1e-07)
    position = lax.broadcasted_iota(jnp.int32, inverse.shape, 0)
    for place in range(matrix_count):
        matrix = place_ref[place]
        factor = jnp.sum(jnp.where(position == matrix, inverse, 0.0), axis=0, keepdims=True)
        clipped = clip * grad_ref[matrix]
        new_momentum = mom_beta * momentum_ref[matrix] + clipped
        new_momentum_ref[matrix] = new_momentum
        nesterov = clipped + mom_beta * new_momentum
        outputs[place][...] = (nesterov * factor).astype(jnp.bfloat16)


def end_kernel(matrix_count, place_ref, *refs):
    arrived = refs[:matrix_count]
    weights_ref, update_ref, new_weights_ref = refs[matrix_count:]
    step_size = muon_rate * (0.2 * math.sqrt(D))
    for place in range(matrix_count):
        matrix = place_ref[place]
        update = arrived[place][...]
        update_ref[matrix] = update
        new_weights_ref[matrix] = (
            weights_ref[matrix].astype(jnp.float32) * (1.0 - muon_rate * muon_decay)
            - step_size * update.astype(jnp.float32)
        ).astype(jnp.bfloat16)


def vectors_kernel(
    place_ref, clip_ref, sums_ref, vectors_ref, first_ref, second_ref, direction_ref, new_ref
):
    width = vectors_ref.shape[1]
    count = sums_ref.shape[1] // width
    rows = sums_ref[:, :width]
    for position in range(1, count):
        part = sums_ref[:, position * width : (position + 1) * width]
        rows = jnp.where(place_ref[0] == position, part, rows)
    clipped = clip_ref[0:1, 0:1] * rows
    updated_first = 0.9 * first_ref[...] + 0.1 * clipped
    updated_second = 0.999 * second_ref[...] + 0.001 * clipped * clipped
    direction = updated_first / (jnp.sqrt(updated_second) + 1e-08)
    direction_ref[...] = direction
    new_ref[...] = vectors_ref[...] * (1.0 - adam_rate * adam_decay) - adam_rate * direction


def on_device(kernel, scalars, operands, out_shape):
    return pl.pallas_call(
        kernel,
        out_shape=out_shape,
        in_specs=[pl.BlockSpec(memory_space=pltpu.SMEM)]
        + [pl.BlockSpec(memory_space=pltpu.VMEM)] * len(operands),
        compiler_params=pltpu.CompilerParams(vmem_limit_bytes=16 * MIB),
    )(scalars, *operands)


def swapped(array, axis, offset):
    pairs = [(i, i ^ offset) for i in range(lax.axis_size(axis))]
    return lax.ppermute(array, axis, pairs)


def after(array, earlier):
    return lax.optimization_barrier((array, earlier))[0]


def per_device(grad_parts, vector_grads, momentum, weights, vectors, first_moment, second_moment):
    shard_count = lax.axis_size("shard")
    tensor_count = lax.axis_size("tensor")
    section_count = lax.axis_size("section")
    _, matrix_count, local_height, width = momentum.shape
    if shard_count != matrix_count or shard_count != 4 or tensor_count != 4:
        return general_device(
            grad_parts, vector_grads, momentum, weights, vectors, first_moment, second_moment
        )
    vector_count, vector_width = vectors.shape[1:]
    own_momentum = momentum[0]
    position = jnp.arange(shard_count + 1, dtype=jnp.int32)
    place = jnp.where(
        position == shard_count,
        lax.axis_index("section").astype(jnp.int32),
        lax.axis_index("shard").astype(jnp.int32) ^ position,
    )

    by_rows = grad_parts.reshape(matrix_count, shard_count, local_height, width)
    parts = list(row_slices(place, by_rows))
    for offset in reversed(range(1, shard_count)):
        parts[offset] = swapped(parts[offset], "shard", offset)
    vector_parts = lax.all_to_all(
        jnp.broadcast_to(vector_grads[0], (shard_count, vector_count, vector_width * shard_count)),
        "shard",
        split_axis=0,
        concat_axis=0,
        tiled=True,
    )

    others = shard_count * tensor_count
    grad_rows, vector_whole, figures = on_device(
        functools.partial(sum_kernel, shard_count),
        place,
        parts + [vector_parts, own_momentum],
        [
            jax.ShapeDtypeStruct(own_momentum.shape, jnp.float32),
            jax.ShapeDtypeStruct(vector_parts.shape[1:], jnp.float32),
            jax.ShapeDtypeStruct((others, section_count, 1, LANES), jnp.float32),
        ],
    )
    figures = lax.all_to_all(
        figures.reshape(others * section_count, 1, LANES),
        MESH_AXES,
        split_axis=0,
        concat_axis=0,
        tiled=True,
    )
    *scaled, clip_tile, new_momentum = on_device(
        functools.partial(scale_kernel, matrix_count),
        place,
        [figures, grad_rows, own_momentum],
        [jax.ShapeDtypeStruct((local_height, width), jnp.bfloat16)] * matrix_count
        + [
            jax.ShapeDtypeStruct((8, LANES), jnp.float32),
            jax.ShapeDtypeStruct(own_momentum.shape, jnp.float32),
        ],
    )

    pieces = [scaled[0]] + [None] * 3
    for offset in (2, 3, 1):
        pieces[offset] = swapped(scaled[offset], "shard", offset)
    near, side, far = [None] * 4, [None] * 4, [None] * 4
    near[0] = swapped(pieces[0], "tensor", 1)
    side[0] = swapped(pieces[0], "tensor", 2)
    far[0] = swapped(near[0], "tensor", 2)
    near[1] = swapped(pieces[1], "tensor", 1)
    side[1] = swapped(after(pieces[1], side[0]), "tensor", 2)
    far[1] = swapped(side[1], "tensor", 1)
    near[2] = swapped(after(pieces[2], far[0]), "tensor", 1)
    side[2] = swapped(after(pieces[2], near[1]), "tensor", 2)
    far[2] = swapped(near[2], "tensor", 2)
    near[3] = swapped(after(pieces[3], far[1]), "tensor", 1)
    side[3] = swapped(after(pieces[3], side[2]), "tensor", 2)
    far[3] = swapped(side[3], "tensor", 1)
    results = orthogonalize([pieces, near, side, far])

    arrived = [
        swapped(results[offset], "shard", offset) if offset else results[0]
        for offset in range(shard_count)
    ]
    orthogonal_update, new_weights = on_device(
        functools.partial(end_kernel, matrix_count),
        place,
        arrived + [weights[0]],
        [jax.ShapeDtypeStruct(own_momentum.shape, jnp.bfloat16)] * 2,
    )

    adam_direction, new_vectors = on_device(
        vectors_kernel,
        place,
        [clip_tile, vector_whole, vectors[0], first_moment[0], second_moment[0]],
        [jax.ShapeDtypeStruct(vectors.shape[1:], jnp.float32)] * 2,
    )
    return (
        new_momentum[None],
        orthogonal_update[None],
        new_weights[None],
        adam_direction[None],
        new_vectors[None],
    )


def general_device(grad_parts, vector_grads, momentum, weights, vectors, first_moment, second_moment):
    shard_count = lax.axis_size("shard")
    tensor_count = lax.axis_size("tensor")
    section_count = lax.axis_size("section")
    shard_index = lax.axis_index("shard")
    _, matrix_count, local_height, width = momentum.shape
    vector_width = vectors.shape[2]
    own_momentum = momentum[0]

    rows = matrix_count * local_height
    by_target = (
        grad_parts.reshape(matrix_count, shard_count, local_height, width)
        .transpose(1, 0, 2, 3)
        .reshape(shard_count, rows, width)
    )
    vector_line = jnp.broadcast_to(
        vector_grads.reshape(1, 1, width), (shard_count, VECTOR_ROWS, width)
    )
    payload = jnp.concatenate([by_target, vector_line], axis=1)
    arrived = lax.all_to_all(payload, "shard", split_axis=0, concat_axis=0, tiled=True)
    grad_rows = jnp.sum(arrived[:, :rows].astype(jnp.float32), axis=0).reshape(
        matrix_count, local_height, width
    )
    vector_whole = jnp.sum(arrived[:, rows].astype(jnp.float32), axis=0).reshape(
        vectors.shape[1], vector_width * shard_count
    )
    vector_rows = lax.dynamic_slice_in_dim(
        vector_whole, shard_index * vector_width, vector_width, 1
    )

    grad_squares = jnp.sum(grad_rows * grad_rows, axis=(1, 2))
    cross = jnp.sum(grad_rows * own_momentum, axis=(1, 2))
    momentum_squares = jnp.sum(own_momentum * own_momentum, axis=(1, 2))
    own_total = jnp.sum(grad_squares) + jnp.sum(vector_rows * vector_rows)
    same_section = (
        jnp.arange(section_count) == lax.axis_index("section")
    ).astype(jnp.float32)[:, None]
    matrix_figures = jnp.concatenate([grad_squares, cross, momentum_squares])
    line = jnp.concatenate(
        [
            same_section * matrix_figures[None],
            jnp.broadcast_to(own_total, (section_count, 1)),
            jnp.zeros((section_count, 127 - 3 * matrix_count), jnp.float32),
        ],
        axis=1,
    )
    others = shard_count * tensor_count
    figures = jnp.broadcast_to(line[None, :, None, :], (others, section_count, 8, 128)).reshape(
        others * section_count, 8, 128
    )
    figures = lax.all_to_all(figures, MESH_AXES, split_axis=0, concat_axis=0, tiled=True)
    sums = jnp.sum(figures[:, 0, :], axis=0)
    grand_total = sums[3 * matrix_count]
    clip_factor = jnp.minimum(1.0, max_norm / (jnp.sqrt(grand_total) + 1e-06))
    grad_scale = (1.0 + mom_beta) * clip_factor
    momentum_scale = mom_beta * mom_beta
    update_norm = (
        grad_scale * grad_scale * sums[:matrix_count]
        + 2.0 * grad_scale * momentum_scale * sums[matrix_count : 2 * matrix_count]
        + momentum_scale * momentum_scale * sums[2 * matrix_count : 3 * matrix_count]
    )
    update_norm = jnp.maximum(update_norm, 0.0)[:, None, None]

    new_momentum = mom_beta * own_momentum + clip_factor * grad_rows
    nesterov = clip_factor * grad_rows + mom_beta * new_momentum
    scaled = (nesterov / (jnp.sqrt(update_norm) + 1e-07)).astype(jnp.bfloat16)

    owner_count = shard_count // matrix_count
    if owner_count == 1:
        row_block = lax.all_to_all(scaled, "shard", split_axis=0, concat_axis=0, tiled=True)
        row_block = row_block.reshape(shard_count * local_height, width)
    else:
        everything = lax.all_gather(scaled, "shard", axis=1, tiled=True)
        row_block = lax.dynamic_index_in_dim(
            everything, shard_index // owner_count, 0, keepdims=False
        )

    blocks = [row_block]
    for offset in range(1, tensor_count):
        pairs = [(i, i ^ offset) for i in range(tensor_count)]
        blocks.append(lax.ppermute(row_block, "tensor", pairs))
    (own_result,) = orthogonalize([[block] for block in blocks])

    if owner_count == 1:
        own_update = lax.all_to_all(
            own_result.reshape(shard_count, local_height, width),
            "shard",
            split_axis=0,
            concat_axis=0,
            tiled=True,
        )
    else:
        piece_length = local_height * width // owner_count
        split_rows = own_result.reshape(shard_count, owner_count, piece_length)
        returning = lax.dynamic_index_in_dim(
            split_rows, shard_index % owner_count, 1, keepdims=False
        )
        received = lax.all_to_all(returning, "shard", split_axis=0, concat_axis=0, tiled=True)
        own_update = received.reshape(matrix_count, local_height, width)
    orthogonal_update = own_update[None]
    muon_scale = 0.2 * math.sqrt(D)
    new_weights = (
        weights.astype(jnp.float32) * (1.0 - muon_rate * muon_decay)
        - muon_rate * muon_scale * orthogonal_update.astype(jnp.float32)
    ).astype(jnp.bfloat16)
    vector_clipped = clip_factor * vector_rows
    updated_first = 0.9 * first_moment + 0.1 * vector_clipped
    updated_second = 0.999 * second_moment + 0.001 * vector_clipped * vector_clipped
    adam_direction = updated_first / (jnp.sqrt(updated_second) + 1e-08)
    new_vectors = vectors * (1.0 - adam_rate * adam_decay) - adam_rate * adam_direction
    return (new_momentum[None], orthogonal_update, new_weights, adam_direction, new_vectors)


def solution(mesh):
    in_specs = (
        P("shard", "section", None, "tensor", None),
        P("shard", "section", None, "tensor"),
        P("section", None, ("tensor", "shard"), None),
        P("section", None, ("tensor", "shard"), None),
        P("section", None, ("tensor", "shard")),
        P("section", None, ("tensor", "shard")),
        P("section", None, ("tensor", "shard")),
    )
    out_specs = (
        P("section", None, ("tensor", "shard"), None),
        P("section", None, ("tensor", "shard"), None),
        P("section", None, ("tensor", "shard"), None),
        P("section", None, ("tensor", "shard")),
        P("section", None, ("tensor", "shard")),
    )
    return jax.shard_map(
        per_device, mesh=mesh, in_specs=in_specs, out_specs=out_specs, check_vma=False
    )
```

```python
import functools
import math

import jax
import jax.numpy as jnp
from jax import lax
from jax.experimental import pallas as pl
from jax.experimental.pallas import tpu as pltpu
from jax.sharding import PartitionSpec as P

D = 1024
NS_STEPS = 2


ns_first = 3.4445
ns_second = -4.775
ns_third = 2.0315
mom_beta = 0.95
max_norm = 1024.0
muon_rate = 0.02
muon_decay = 0.1
adam_rate = 0.001
adam_decay = 0.01

VECTOR_ROWS = 16
FIGURES = 16
MIB = 2**20
LANES = 128
MESH_AXES = ("shard", "tensor", "section")


def gram_of(blocks, gram_ref):
    width = blocks[0].shape[1]
    step = 256
    for start in range(0, width, step):
        total = None
        for block in blocks:
            whole = block[...]
            part = whole[:, start : start + step]
            product = lax.dot_general(
                whole, part, (((0,), (0,)), ((), ())), preferred_element_type=jnp.float32
            )
            rounded = product.astype(jnp.bfloat16).astype(jnp.float32)
            total = rounded if total is None else total + rounded
        gram_ref[:, start : start + step] = total.astype(jnp.bfloat16)


def polynomial(block, gram_ref):
    gram = gram_ref[...]
    first = jnp.dot(block, gram, preferred_element_type=jnp.float32).astype(jnp.bfloat16)
    second = jnp.dot(first, gram, preferred_element_type=jnp.float32)
    combined = (
        ns_first * block.astype(jnp.float32)
        + ns_second * first.astype(jnp.float32)
        + ns_third * second
    )
    return combined.astype(jnp.bfloat16)


def orthogonalize_kernel(count, pieces, *refs):
    height, width = refs[0].shape
    inputs = refs[: count * pieces]
    outputs = refs[count * pieces : count * pieces + pieces]
    gram_ref, start_ref, next_ref = refs[count * pieces + pieces :]
    for position in range(count):
        for piece in range(pieces):
            start_ref[position, piece * height : (piece + 1) * height, :] = inputs[
                position * pieces + piece
            ][...]
    current, other = start_ref, next_ref
    for iteration in range(NS_STEPS - 1):
        gram_of([current.at[position] for position in range(count)], gram_ref)
        for position in range(count):
            other[position] = polynomial(current[position], gram_ref)
        current, other = other, current
    gram_of([current.at[position] for position in range(count)], gram_ref)
    result = polynomial(current[0], gram_ref)
    for piece in range(pieces):
        outputs[piece][...] = result[piece * height : (piece + 1) * height, :]


def orthogonalize(blocks):
    count, pieces = len(blocks), len(blocks[0])
    height, width = blocks[0][0].shape
    return pl.pallas_call(
        functools.partial(orthogonalize_kernel, count, pieces),
        out_shape=[jax.ShapeDtypeStruct((height, width), jnp.bfloat16)] * pieces,
        scratch_shapes=[
            pltpu.VMEM((width, width), jnp.bfloat16),
            pltpu.VMEM((count, pieces * height, width), jnp.bfloat16),
            pltpu.VMEM((count, pieces * height, width), jnp.bfloat16),
        ],
        compiler_params=pltpu.CompilerParams(vmem_limit_bytes=32 * MIB),
    )(*[piece for block in blocks for piece in block])


def folded(array):
    line = jnp.sum(array, axis=0, keepdims=True)
    total = line[:, :LANES]
    for start in range(LANES, line.shape[1], LANES):
        total = total + line[:, start : start + LANES]
    return total


def slices_kernel(count, place_ref, grad_ref, *refs):
    outputs, semaphores = refs[:count], refs[count]
    copies = [
        pltpu.make_async_copy(
            grad_ref.at[:, place_ref[offset]], outputs[offset], semaphores.at[offset]
        )
        for offset in range(count)
    ]
    for copy in reversed(copies):
        copy.start()
    for copy in reversed(copies):
        copy.wait()


def row_slices(place, by_rows):
    matrix_count, shard_count, height, width = by_rows.shape
    return pl.pallas_call(
        functools.partial(slices_kernel, shard_count),
        out_shape=[jax.ShapeDtypeStruct((matrix_count, height, width), by_rows.dtype)]
        * shard_count,
        in_specs=[
            pl.BlockSpec(memory_space=pltpu.SMEM),
            pl.BlockSpec(memory_space=pltpu.HBM),
        ],
        out_specs=[pl.BlockSpec(memory_space=pltpu.VMEM)] * shard_count,
        scratch_shapes=[pltpu.SemaphoreType.DMA((shard_count,))],
    )(place, by_rows)


def sum_kernel(shard_count, place_ref, *refs):
    parts = refs[:shard_count]
    vector_parts, momentum_ref, grad_ref, vector_ref, figures_ref = refs[shard_count:]
    vector = jnp.sum(vector_parts[...].astype(jnp.float32), axis=0)
    vector_ref[...] = vector
    total = folded(vector * vector) * (1.0 / shard_count)
    squares, crosses, momentum_squares = [], [], []
    for matrix in range(momentum_ref.shape[0]):
        grad = parts[0][matrix].astype(jnp.float32)
        for part in parts[1:]:
            grad = grad + part[matrix].astype(jnp.float32)
        grad_ref[matrix] = grad
        old = momentum_ref[matrix]
        squares.append(folded(grad * grad))
        crosses.append(folded(grad * old))
        momentum_squares.append(folded(old * old))
        total = total + squares[-1]
    lines = squares + crosses + momentum_squares + [total]
    lines = lines + [jnp.zeros_like(total)] * (FIGURES - len(lines))
    tile = jnp.concatenate(lines, axis=0)
    sums = jnp.sum(tile, axis=1, keepdims=True)
    line_index = lax.broadcasted_iota(jnp.int32, tile.shape, 0)
    lane_index = lax.broadcasted_iota(jnp.int32, tile.shape, 1)
    line = jnp.sum(jnp.where(line_index == lane_index, sums, 0.0), axis=0, keepdims=True)
    total_only = jnp.where(lane_index[:1] == 3 * momentum_ref.shape[0], line, 0.0)
    for section in range(figures_ref.shape[1]):
        chosen = jnp.where(place_ref[shard_count] == section, line, total_only)
        figures_ref[:, section] = jnp.broadcast_to(
            chosen[None], (figures_ref.shape[0],) + line.shape
        )


def scale_kernel(matrix_count, place_ref, figures_ref, grad_ref, momentum_ref, *refs):
    outputs = refs[:matrix_count]
    clip_ref, new_momentum_ref = refs[matrix_count:]
    line = jnp.sum(figures_ref[...], axis=0)
    line_index = lax.broadcasted_iota(jnp.int32, (FIGURES, LANES), 0)
    lane_index = lax.broadcasted_iota(jnp.int32, (FIGURES, LANES), 1)
    sums = jnp.sum(jnp.where(line_index == lane_index, line, 0.0), axis=1, keepdims=True)
    total = sums[3 * matrix_count : 3 * matrix_count + 1]
    clip = jnp.minimum(1.0, max_norm / (jnp.sqrt(total) + 1e-06))
    clip_ref[...] = jnp.broadcast_to(clip, clip_ref.shape)
    grad_scale = (1.0 + mom_beta) * clip
    momentum_scale = mom_beta * mom_beta
    update_norm = (
        grad_scale * grad_scale * sums[:matrix_count]
        + 2.0 * grad_scale * momentum_scale * sums[matrix_count : 2 * matrix_count]
        + momentum_scale * momentum_scale * sums[2 * matrix_count : 3 * matrix_count]
    )
    inverse = 1.0 / (jnp.sqrt(jnp.maximum(update_norm, 0.0)) + 1e-07)
    position = lax.broadcasted_iota(jnp.int32, inverse.shape, 0)
    for place in range(matrix_count):
        matrix = place_ref[place]
        factor = jnp.sum(jnp.where(position == matrix, inverse, 0.0), axis=0, keepdims=True)
        clipped = clip * grad_ref[matrix]
        new_momentum = mom_beta * momentum_ref[matrix] + clipped
        new_momentum_ref[matrix] = new_momentum
        nesterov = clipped + mom_beta * new_momentum
        outputs[place][...] = (nesterov * factor).astype(jnp.bfloat16)


def end_kernel(matrix_count, place_ref, *refs):
    arrived = refs[:matrix_count]
    weights_ref, update_ref, new_weights_ref = refs[matrix_count:]
    step_size = muon_rate * (0.2 * math.sqrt(D))
    for place in range(matrix_count):
        matrix = place_ref[place]
        update = arrived[place][...]
        update_ref[matrix] = update
        new_weights_ref[matrix] = (
            weights_ref[matrix].astype(jnp.float32) * (1.0 - muon_rate * muon_decay)
            - step_size * update.astype(jnp.float32)
        ).astype(jnp.bfloat16)


def vectors_kernel(
    place_ref, clip_ref, sums_ref, vectors_ref, first_ref, second_ref, direction_ref, new_ref
):
    width = vectors_ref.shape[1]
    count = sums_ref.shape[1] // width
    rows = sums_ref[:, :width]
    for position in range(1, count):
        part = sums_ref[:, position * width : (position + 1) * width]
        rows = jnp.where(place_ref[0] == position, part, rows)
    clipped = clip_ref[0:1, 0:1] * rows
    updated_first = 0.9 * first_ref[...] + 0.1 * clipped
    updated_second = 0.999 * second_ref[...] + 0.001 * clipped * clipped
    direction = updated_first / (jnp.sqrt(updated_second) + 1e-08)
    direction_ref[...] = direction
    new_ref[...] = vectors_ref[...] * (1.0 - adam_rate * adam_decay) - adam_rate * direction


def on_device(kernel, scalars, operands, out_shape):
    return pl.pallas_call(
        kernel,
        out_shape=out_shape,
        in_specs=[pl.BlockSpec(memory_space=pltpu.SMEM)]
        + [pl.BlockSpec(memory_space=pltpu.VMEM)] * len(operands),
        compiler_params=pltpu.CompilerParams(vmem_limit_bytes=16 * MIB),
    )(scalars, *operands)


def swapped(array, axis, offset):
    pairs = [(i, i ^ offset) for i in range(lax.axis_size(axis))]
    return lax.ppermute(array, axis, pairs)


def after(array, earlier):
    return lax.optimization_barrier((array, earlier))[0]


def per_device(grad_parts, vector_grads, momentum, weights, vectors, first_moment, second_moment):
    shard_count = lax.axis_size("shard")
    tensor_count = lax.axis_size("tensor")
    section_count = lax.axis_size("section")
    _, matrix_count, local_height, width = momentum.shape
    if shard_count != matrix_count or shard_count != 4 or tensor_count != 4:
        return general_device(
            grad_parts, vector_grads, momentum, weights, vectors, first_moment, second_moment
        )
    vector_count, vector_width = vectors.shape[1:]
    own_momentum = momentum[0]
    position = jnp.arange(shard_count + 1, dtype=jnp.int32)
    place = jnp.where(
        position == shard_count,
        lax.axis_index("section").astype(jnp.int32),
        lax.axis_index("shard").astype(jnp.int32) ^ position,
    )

    by_rows = grad_parts.reshape(matrix_count, shard_count, local_height, width)
    parts = list(row_slices(place, by_rows))
    for offset in reversed(range(1, shard_count)):
        parts[offset] = swapped(parts[offset], "shard", offset)
    vector_parts = lax.all_to_all(
        jnp.broadcast_to(vector_grads[0], (shard_count, vector_count, vector_width * shard_count)),
        "shard",
        split_axis=0,
        concat_axis=0,
        tiled=True,
    )

    others = shard_count * tensor_count
    grad_rows, vector_whole, figures = on_device(
        functools.partial(sum_kernel, shard_count),
        place,
        parts + [vector_parts, own_momentum],
        [
            jax.ShapeDtypeStruct(own_momentum.shape, jnp.float32),
            jax.ShapeDtypeStruct(vector_parts.shape[1:], jnp.float32),
            jax.ShapeDtypeStruct((others, section_count, 1, LANES), jnp.float32),
        ],
    )
    figures = lax.all_to_all(
        figures.reshape(others * section_count, 1, LANES),
        MESH_AXES,
        split_axis=0,
        concat_axis=0,
        tiled=True,
    )
    *scaled, clip_tile, new_momentum = on_device(
        functools.partial(scale_kernel, matrix_count),
        place,
        [figures, grad_rows, own_momentum],
        [jax.ShapeDtypeStruct((local_height, width), jnp.bfloat16)] * matrix_count
        + [
            jax.ShapeDtypeStruct((8, LANES), jnp.float32),
            jax.ShapeDtypeStruct(own_momentum.shape, jnp.float32),
        ],
    )

    pieces = [scaled[0]] + [None] * 3
    for offset in (2, 3, 1):
        pieces[offset] = swapped(scaled[offset], "shard", offset)
    near, side, far = [None] * 4, [None] * 4, [None] * 4
    near[0] = swapped(pieces[0], "tensor", 1)
    side[0] = swapped(pieces[0], "tensor", 2)
    far[0] = swapped(near[0], "tensor", 2)
    near[1] = swapped(pieces[1], "tensor", 1)
    side[1] = swapped(after(pieces[1], side[0]), "tensor", 2)
    far[1] = swapped(side[1], "tensor", 1)
    near[2] = swapped(after(pieces[2], far[0]), "tensor", 1)
    side[2] = swapped(after(pieces[2], near[1]), "tensor", 2)
    far[2] = swapped(near[2], "tensor", 2)
    near[3] = swapped(after(pieces[3], far[1]), "tensor", 1)
    side[3] = swapped(after(pieces[3], side[2]), "tensor", 2)
    far[3] = swapped(side[3], "tensor", 1)
    results = orthogonalize([pieces, near, side, far])

    arrived = [
        swapped(results[offset], "shard", offset) if offset else results[0]
        for offset in range(shard_count)
    ]
    orthogonal_update, new_weights = on_device(
        functools.partial(end_kernel, matrix_count),
        place,
        arrived + [weights[0]],
        [jax.ShapeDtypeStruct(own_momentum.shape, jnp.bfloat16)] * 2,
    )

    adam_direction, new_vectors = on_device(
        vectors_kernel,
        place,
        [clip_tile, vector_whole, vectors[0], first_moment[0], second_moment[0]],
        [jax.ShapeDtypeStruct(vectors.shape[1:], jnp.float32)] * 2,
    )
    return (
        new_momentum[None],
        orthogonal_update[None],
        new_weights[None],
        adam_direction[None],
        new_vectors[None],
    )


def general_device(grad_parts, vector_grads, momentum, weights, vectors, first_moment, second_moment):
    shard_count = lax.axis_size("shard")
    tensor_count = lax.axis_size("tensor")
    section_count = lax.axis_size("section")
    shard_index = lax.axis_index("shard")
    _, matrix_count, local_height, width = momentum.shape
    vector_width = vectors.shape[2]
    own_momentum = momentum[0]

    rows = matrix_count * local_height
    by_target = (
        grad_parts.reshape(matrix_count, shard_count, local_height, width)
        .transpose(1, 0, 2, 3)
        .reshape(shard_count, rows, width)
    )
    vector_line = jnp.broadcast_to(
        vector_grads.reshape(1, 1, width), (shard_count, VECTOR_ROWS, width)
    )
    payload = jnp.concatenate([by_target, vector_line], axis=1)
    arrived = lax.all_to_all(payload, "shard", split_axis=0, concat_axis=0, tiled=True)
    grad_rows = jnp.sum(arrived[:, :rows].astype(jnp.float32), axis=0).reshape(
        matrix_count, local_height, width
    )
    vector_whole = jnp.sum(arrived[:, rows].astype(jnp.float32), axis=0).reshape(
        vectors.shape[1], vector_width * shard_count
    )
    vector_rows = lax.dynamic_slice_in_dim(
        vector_whole, shard_index * vector_width, vector_width, 1
    )

    grad_squares = jnp.sum(grad_rows * grad_rows, axis=(1, 2))
    cross = jnp.sum(grad_rows * own_momentum, axis=(1, 2))
    momentum_squares = jnp.sum(own_momentum * own_momentum, axis=(1, 2))
    own_total = jnp.sum(grad_squares) + jnp.sum(vector_rows * vector_rows)
    same_section = (
        jnp.arange(section_count) == lax.axis_index("section")
    ).astype(jnp.float32)[:, None]
    matrix_figures = jnp.concatenate([grad_squares, cross, momentum_squares])
    line = jnp.concatenate(
        [
            same_section * matrix_figures[None],
            jnp.broadcast_to(own_total, (section_count, 1)),
            jnp.zeros((section_count, 127 - 3 * matrix_count), jnp.float32),
        ],
        axis=1,
    )
    others = shard_count * tensor_count
    figures = jnp.broadcast_to(line[None, :, None, :], (others, section_count, 8, 128)).reshape(
        others * section_count, 8, 128
    )
    figures = lax.all_to_all(figures, MESH_AXES, split_axis=0, concat_axis=0, tiled=True)
    sums = jnp.sum(figures[:, 0, :], axis=0)
    grand_total = sums[3 * matrix_count]
    clip_factor = jnp.minimum(1.0, max_norm / (jnp.sqrt(grand_total) + 1e-06))
    grad_scale = (1.0 + mom_beta) * clip_factor
    momentum_scale = mom_beta * mom_beta
    update_norm = (
        grad_scale * grad_scale * sums[:matrix_count]
        + 2.0 * grad_scale * momentum_scale * sums[matrix_count : 2 * matrix_count]
        + momentum_scale * momentum_scale * sums[2 * matrix_count : 3 * matrix_count]
    )
    update_norm = jnp.maximum(update_norm, 0.0)[:, None, None]

    new_momentum = mom_beta * own_momentum + clip_factor * grad_rows
    nesterov = clip_factor * grad_rows + mom_beta * new_momentum
    scaled = (nesterov / (jnp.sqrt(update_norm) + 1e-07)).astype(jnp.bfloat16)

    owner_count = shard_count // matrix_count
    if owner_count == 1:
        row_block = lax.all_to_all(scaled, "shard", split_axis=0, concat_axis=0, tiled=True)
        row_block = row_block.reshape(shard_count * local_height, width)
    else:
        everything = lax.all_gather(scaled, "shard", axis=1, tiled=True)
        row_block = lax.dynamic_index_in_dim(
            everything, shard_index // owner_count, 0, keepdims=False
        )

    blocks = [row_block]
    for offset in range(1, tensor_count):
        pairs = [(i, i ^ offset) for i in range(tensor_count)]
        blocks.append(lax.ppermute(row_block, "tensor", pairs))
    (own_result,) = orthogonalize([[block] for block in blocks])

    if owner_count == 1:
        own_update = lax.all_to_all(
            own_result.reshape(shard_count, local_height, width),
            "shard",
            split_axis=0,
            concat_axis=0,
            tiled=True,
        )
    else:
        piece_length = local_height * width // owner_count
        split_rows = own_result.reshape(shard_count, owner_count, piece_length)
        returning = lax.dynamic_index_in_dim(
            split_rows, shard_index % owner_count, 1, keepdims=False
        )
        received = lax.all_to_all(returning, "shard", split_axis=0, concat_axis=0, tiled=True)
        own_update = received.reshape(matrix_count, local_height, width)
    orthogonal_update = own_update[None]
    muon_scale = 0.2 * math.sqrt(D)
    new_weights = (
        weights.astype(jnp.float32) * (1.0 - muon_rate * muon_decay)
        - muon_rate * muon_scale * orthogonal_update.astype(jnp.float32)
    ).astype(jnp.bfloat16)
    vector_clipped = clip_factor * vector_rows
    updated_first = 0.9 * first_moment + 0.1 * vector_clipped
    updated_second = 0.999 * second_moment + 0.001 * vector_clipped * vector_clipped
    adam_direction = updated_first / (jnp.sqrt(updated_second) + 1e-08)
    new_vectors = vectors * (1.0 - adam_rate * adam_decay) - adam_rate * adam_direction
    return (new_momentum[None], orthogonal_update, new_weights, adam_direction, new_vectors)


def solution(mesh):
    in_specs = (
        P("shard", "section", None, "tensor", None),
        P("shard", "section", None, "tensor"),
        P("section", None, ("tensor", "shard"), None),
        P("section", None, ("tensor", "shard"), None),
        P("section", None, ("tensor", "shard")),
        P("section", None, ("tensor", "shard")),
        P("section", None, ("tensor", "shard")),
    )
    out_specs = (
        P("section", None, ("tensor", "shard"), None),
        P("section", None, ("tensor", "shard"), None),
        P("section", None, ("tensor", "shard"), None),
        P("section", None, ("tensor", "shard")),
        P("section", None, ("tensor", "shard")),
    )
    return jax.shard_map(
        per_device, mesh=mesh, in_specs=in_specs, out_specs=out_specs, check_vma=False
    )
```

```python
import functools
import math

import jax
import jax.numpy as jnp
from jax import lax
from jax.experimental import pallas as pl
from jax.experimental.pallas import tpu as pltpu
from jax.sharding import PartitionSpec as P

D = 1024
NS_STEPS = 2


ns_first = 3.4445
ns_second = -4.775
ns_third = 2.0315
mom_beta = 0.95
max_norm = 1024.0
muon_rate = 0.02
muon_decay = 0.1
adam_rate = 0.001
adam_decay = 0.01

VECTOR_ROWS = 16
FIGURES = 16
MIB = 2**20
LANES = 128
MESH_AXES = ("shard", "tensor", "section")


def gram_of(blocks, gram_ref):
    width = blocks[0].shape[1]
    step = 256
    for start in range(0, width, step):
        stop = start + step
        total = None
        for block in blocks:
            whole = block[...]
            product = lax.dot_general(
                whole[:, :stop],
                whole[:, start:stop],
                (((0,), (0,)), ((), ())),
                preferred_element_type=jnp.float32,
            )
            rounded = product.astype(jnp.bfloat16).astype(jnp.float32)
            total = rounded if total is None else total + rounded
        gram_ref[:stop, start:stop] = total.astype(jnp.bfloat16)
        for above in range(0, start, step):
            tile = gram_ref[above : above + step, start:stop]
            gram_ref[start:stop, above : above + step] = tile.T


def polynomial(block, gram_ref):
    gram = gram_ref[...]
    first = jnp.dot(block, gram, preferred_element_type=jnp.float32).astype(jnp.bfloat16)
    second = jnp.dot(first, gram, preferred_element_type=jnp.float32)
    combined = (
        ns_first * block.astype(jnp.float32)
        + ns_second * first.astype(jnp.float32)
        + ns_third * second
    )
    return combined.astype(jnp.bfloat16)


def orthogonalize_kernel(count, pieces, *refs):
    height, width = refs[0].shape
    inputs = refs[: count * pieces]
    outputs = refs[count * pieces : count * pieces + pieces]
    gram_ref, start_ref, next_ref = refs[count * pieces + pieces :]
    for position in range(count):
        for piece in range(pieces):
            start_ref[position, piece * height : (piece + 1) * height, :] = inputs[
                position * pieces + piece
            ][...]
    current, other = start_ref, next_ref
    for iteration in range(NS_STEPS - 1):
        gram_of([current.at[position] for position in range(count)], gram_ref)
        for position in range(count):
            other[position] = polynomial(current[position], gram_ref)
        current, other = other, current
    gram_of([current.at[position] for position in range(count)], gram_ref)
    result = polynomial(current[0], gram_ref)
    for piece in range(pieces):
        outputs[piece][...] = result[piece * height : (piece + 1) * height, :]


def orthogonalize(blocks):
    count, pieces = len(blocks), len(blocks[0])
    height, width = blocks[0][0].shape
    return pl.pallas_call(
        functools.partial(orthogonalize_kernel, count, pieces),
        out_shape=[jax.ShapeDtypeStruct((height, width), jnp.bfloat16)] * pieces,
        scratch_shapes=[
            pltpu.VMEM((width, width), jnp.bfloat16),
            pltpu.VMEM((count, pieces * height, width), jnp.bfloat16),
            pltpu.VMEM((count, pieces * height, width), jnp.bfloat16),
        ],
        compiler_params=pltpu.CompilerParams(vmem_limit_bytes=32 * MIB),
    )(*[piece for block in blocks for piece in block])


def folded(array):
    line = jnp.sum(array, axis=0, keepdims=True)
    total = line[:, :LANES]
    for start in range(LANES, line.shape[1], LANES):
        total = total + line[:, start : start + LANES]
    return total


def slices_kernel(count, place_ref, grad_ref, *refs):
    outputs, semaphores = refs[:count], refs[count]
    copies = [
        pltpu.make_async_copy(
            grad_ref.at[:, place_ref[offset]], outputs[offset], semaphores.at[offset]
        )
        for offset in range(count)
    ]
    for copy in reversed(copies):
        copy.start()
    for copy in reversed(copies):
        copy.wait()


def row_slices(place, by_rows):
    matrix_count, shard_count, height, width = by_rows.shape
    return pl.pallas_call(
        functools.partial(slices_kernel, shard_count),
        out_shape=[jax.ShapeDtypeStruct((matrix_count, height, width), by_rows.dtype)]
        * shard_count,
        in_specs=[
            pl.BlockSpec(memory_space=pltpu.SMEM),
            pl.BlockSpec(memory_space=pltpu.HBM),
        ],
        out_specs=[pl.BlockSpec(memory_space=pltpu.VMEM)] * shard_count,
        scratch_shapes=[pltpu.SemaphoreType.DMA((shard_count,))],
        compiler_params=pltpu.CompilerParams(vmem_limit_bytes=4 * MIB),
    )(place, by_rows)


def sum_kernel(shard_count, place_ref, *refs):
    parts = refs[:shard_count]
    vector_parts, momentum_ref, grad_ref, vector_ref, figures_ref = refs[shard_count:]
    vector = jnp.sum(vector_parts[...].astype(jnp.float32), axis=0)
    vector_ref[...] = vector
    total = folded(vector * vector) * (1.0 / shard_count)
    squares, crosses, momentum_squares = [], [], []
    for matrix in range(momentum_ref.shape[0]):
        grad = parts[0][matrix].astype(jnp.float32)
        for part in parts[1:]:
            grad = grad + part[matrix].astype(jnp.float32)
        grad_ref[matrix] = grad
        old = momentum_ref[matrix]
        squares.append(folded(grad * grad))
        crosses.append(folded(grad * old))
        momentum_squares.append(folded(old * old))
        total = total + squares[-1]
    lines = squares + crosses + momentum_squares + [total]
    lines = lines + [jnp.zeros_like(total)] * (FIGURES - len(lines))
    tile = jnp.concatenate(lines, axis=0)
    sums = jnp.sum(tile, axis=1, keepdims=True)
    line_index = lax.broadcasted_iota(jnp.int32, tile.shape, 0)
    lane_index = lax.broadcasted_iota(jnp.int32, tile.shape, 1)
    line = jnp.sum(jnp.where(line_index == lane_index, sums, 0.0), axis=0, keepdims=True)
    total_only = jnp.where(lane_index[:1] == 3 * momentum_ref.shape[0], line, 0.0)
    for section in range(figures_ref.shape[1]):
        chosen = jnp.where(place_ref[shard_count] == section, line, total_only)
        figures_ref[:, section] = jnp.broadcast_to(
            chosen[None], (figures_ref.shape[0],) + line.shape
        )


def scale_kernel(matrix_count, place_ref, figures_ref, grad_ref, momentum_ref, *refs):
    outputs = refs[:matrix_count]
    clip_ref = refs[matrix_count]
    line = jnp.sum(figures_ref[...], axis=0)
    line_index = lax.broadcasted_iota(jnp.int32, (FIGURES, LANES), 0)
    lane_index = lax.broadcasted_iota(jnp.int32, (FIGURES, LANES), 1)
    sums = jnp.sum(jnp.where(line_index == lane_index, line, 0.0), axis=1, keepdims=True)
    total = sums[3 * matrix_count : 3 * matrix_count + 1]
    clip = jnp.minimum(1.0, max_norm / (jnp.sqrt(total) + 1e-06))
    clip_ref[...] = jnp.broadcast_to(clip, clip_ref.shape)
    grad_scale = (1.0 + mom_beta) * clip
    momentum_scale = mom_beta * mom_beta
    update_norm = (
        grad_scale * grad_scale * sums[:matrix_count]
        + 2.0 * grad_scale * momentum_scale * sums[matrix_count : 2 * matrix_count]
        + momentum_scale * momentum_scale * sums[2 * matrix_count : 3 * matrix_count]
    )
    inverse = 1.0 / (jnp.sqrt(jnp.maximum(update_norm, 0.0)) + 1e-07)
    position = lax.broadcasted_iota(jnp.int32, inverse.shape, 0)
    for place in range(matrix_count):
        matrix = place_ref[place]
        factor = jnp.sum(jnp.where(position == matrix, inverse, 0.0), axis=0, keepdims=True)
        clipped = clip * grad_ref[matrix]
        new_momentum = mom_beta * momentum_ref[matrix] + clipped
        nesterov = clipped + mom_beta * new_momentum
        outputs[place][...] = (nesterov * factor).astype(jnp.bfloat16)


def end_kernel(matrix_count, place_ref, *refs):
    arrived = refs[:matrix_count]
    weights_ref, update_ref, new_weights_ref = refs[matrix_count:]
    step_size = muon_rate * (0.2 * math.sqrt(D))
    for place in range(matrix_count):
        matrix = place_ref[place]
        update = arrived[place][...]
        update_ref[matrix] = update
        new_weights_ref[matrix] = (
            weights_ref[matrix].astype(jnp.float32) * (1.0 - muon_rate * muon_decay)
            - step_size * update.astype(jnp.float32)
        ).astype(jnp.bfloat16)


def state_kernel(
    place_ref,
    clip_ref,
    grad_ref,
    momentum_ref,
    sums_ref,
    vectors_ref,
    first_ref,
    second_ref,
    new_momentum_ref,
    direction_ref,
    new_ref,
):
    new_momentum_ref[...] = mom_beta * momentum_ref[...] + clip_ref[0:1, 0:1] * grad_ref[...]
    width = vectors_ref.shape[1]
    count = sums_ref.shape[1] // width
    rows = sums_ref[:, :width]
    for position in range(1, count):
        part = sums_ref[:, position * width : (position + 1) * width]
        rows = jnp.where(place_ref[0] == position, part, rows)
    clipped = clip_ref[0:1, 0:1] * rows
    updated_first = 0.9 * first_ref[...] + 0.1 * clipped
    updated_second = 0.999 * second_ref[...] + 0.001 * clipped * clipped
    direction = updated_first / (jnp.sqrt(updated_second) + 1e-08)
    direction_ref[...] = direction
    new_ref[...] = vectors_ref[...] * (1.0 - adam_rate * adam_decay) - adam_rate * direction


def on_device(kernel, scalars, operands, out_shape):
    return pl.pallas_call(
        kernel,
        out_shape=out_shape,
        in_specs=[pl.BlockSpec(memory_space=pltpu.SMEM)]
        + [pl.BlockSpec(memory_space=pltpu.VMEM)] * len(operands),
        compiler_params=pltpu.CompilerParams(vmem_limit_bytes=16 * MIB),
    )(scalars, *operands)


def swapped(array, axis, offset):
    pairs = [(i, i ^ offset) for i in range(lax.axis_size(axis))]
    return lax.ppermute(array, axis, pairs)


def after(array, earlier):
    return lax.optimization_barrier((array, earlier))[0]


def per_device(grad_parts, vector_grads, momentum, weights, vectors, first_moment, second_moment):
    shard_count = lax.axis_size("shard")
    tensor_count = lax.axis_size("tensor")
    section_count = lax.axis_size("section")
    _, matrix_count, local_height, width = momentum.shape
    if shard_count != matrix_count or shard_count != 4 or tensor_count != 4:
        return general_device(
            grad_parts, vector_grads, momentum, weights, vectors, first_moment, second_moment
        )
    vector_count, vector_width = vectors.shape[1:]
    own_momentum = momentum[0]
    position = jnp.arange(shard_count + 1, dtype=jnp.int32)
    place = jnp.where(
        position == shard_count,
        lax.axis_index("section").astype(jnp.int32),
        lax.axis_index("shard").astype(jnp.int32) ^ position,
    )

    by_rows = grad_parts.reshape(matrix_count, shard_count, local_height, width)
    parts = list(row_slices(place, by_rows))
    for offset in reversed(range(1, shard_count)):
        parts[offset] = swapped(parts[offset], "shard", offset)
    vector_parts = lax.all_to_all(
        jnp.broadcast_to(vector_grads[0], (shard_count, vector_count, vector_width * shard_count)),
        "shard",
        split_axis=0,
        concat_axis=0,
        tiled=True,
    )

    others = shard_count * tensor_count
    grad_rows, vector_whole, figures = on_device(
        functools.partial(sum_kernel, shard_count),
        place,
        parts + [vector_parts, own_momentum],
        [
            jax.ShapeDtypeStruct(own_momentum.shape, jnp.float32),
            jax.ShapeDtypeStruct(vector_parts.shape[1:], jnp.float32),
            jax.ShapeDtypeStruct((others, section_count, 1, LANES), jnp.float32),
        ],
    )
    figures = lax.all_to_all(
        figures.reshape(others * section_count, 1, LANES),
        MESH_AXES,
        split_axis=0,
        concat_axis=0,
        tiled=True,
    )
    *scaled, clip_tile = on_device(
        functools.partial(scale_kernel, matrix_count),
        place,
        [figures, grad_rows, own_momentum],
        [jax.ShapeDtypeStruct((local_height, width), jnp.bfloat16)] * matrix_count
        + [jax.ShapeDtypeStruct((8, LANES), jnp.float32)],
    )

    pieces = [scaled[0]] + [None] * 3
    for offset in (2, 3, 1):
        pieces[offset] = swapped(scaled[offset], "shard", offset)
    near, side, far = [None] * 4, [None] * 4, [None] * 4
    near[0] = swapped(pieces[0], "tensor", 1)
    side[0] = swapped(pieces[0], "tensor", 2)
    early = after(pieces[1], (near[0], side[0]))
    near[1] = swapped(early, "tensor", 1)
    side[1] = swapped(early, "tensor", 2)
    far[0] = swapped(near[0], "tensor", 2)
    far[1] = swapped(side[1], "tensor", 1)
    late = lax.optimization_barrier((pieces[2], pieces[3], near[1]))
    near[2] = swapped(late[0], "tensor", 1)
    side[2] = swapped(late[0], "tensor", 2)
    far[2] = swapped(near[2], "tensor", 2)
    near[3] = swapped(late[1], "tensor", 1)
    side[3] = swapped(late[1], "tensor", 2)
    far[3] = swapped(late[1], "tensor", 3)
    results = orthogonalize([pieces, near, side, far])

    arrived = [
        swapped(results[offset], "shard", offset) if offset else results[0]
        for offset in range(shard_count)
    ]
    orthogonal_update, new_weights = on_device(
        functools.partial(end_kernel, matrix_count),
        place,
        arrived + [weights[0]],
        [jax.ShapeDtypeStruct(own_momentum.shape, jnp.bfloat16)] * 2,
    )

    new_momentum, adam_direction, new_vectors = on_device(
        state_kernel,
        place,
        [
            after(clip_tile, results[0]),
            grad_rows,
            own_momentum,
            vector_whole,
            vectors[0],
            first_moment[0],
            second_moment[0],
        ],
        [jax.ShapeDtypeStruct(own_momentum.shape, jnp.float32)]
        + [jax.ShapeDtypeStruct(vectors.shape[1:], jnp.float32)] * 2,
    )
    return (
        new_momentum[None],
        orthogonal_update[None],
        new_weights[None],
        adam_direction[None],
        new_vectors[None],
    )


def general_device(grad_parts, vector_grads, momentum, weights, vectors, first_moment, second_moment):
    shard_count = lax.axis_size("shard")
    tensor_count = lax.axis_size("tensor")
    section_count = lax.axis_size("section")
    shard_index = lax.axis_index("shard")
    _, matrix_count, local_height, width = momentum.shape
    vector_width = vectors.shape[2]
    own_momentum = momentum[0]

    rows = matrix_count * local_height
    by_target = (
        grad_parts.reshape(matrix_count, shard_count, local_height, width)
        .transpose(1, 0, 2, 3)
        .reshape(shard_count, rows, width)
    )
    vector_line = jnp.broadcast_to(
        vector_grads.reshape(1, 1, width), (shard_count, VECTOR_ROWS, width)
    )
    payload = jnp.concatenate([by_target, vector_line], axis=1)
    arrived = lax.all_to_all(payload, "shard", split_axis=0, concat_axis=0, tiled=True)
    grad_rows = jnp.sum(arrived[:, :rows].astype(jnp.float32), axis=0).reshape(
        matrix_count, local_height, width
    )
    vector_whole = jnp.sum(arrived[:, rows].astype(jnp.float32), axis=0).reshape(
        vectors.shape[1], vector_width * shard_count
    )
    vector_rows = lax.dynamic_slice_in_dim(
        vector_whole, shard_index * vector_width, vector_width, 1
    )

    grad_squares = jnp.sum(grad_rows * grad_rows, axis=(1, 2))
    cross = jnp.sum(grad_rows * own_momentum, axis=(1, 2))
    momentum_squares = jnp.sum(own_momentum * own_momentum, axis=(1, 2))
    own_total = jnp.sum(grad_squares) + jnp.sum(vector_rows * vector_rows)
    same_section = (
        jnp.arange(section_count) == lax.axis_index("section")
    ).astype(jnp.float32)[:, None]
    matrix_figures = jnp.concatenate([grad_squares, cross, momentum_squares])
    line = jnp.concatenate(
        [
            same_section * matrix_figures[None],
            jnp.broadcast_to(own_total, (section_count, 1)),
            jnp.zeros((section_count, 127 - 3 * matrix_count), jnp.float32),
        ],
        axis=1,
    )
    others = shard_count * tensor_count
    figures = jnp.broadcast_to(line[None, :, None, :], (others, section_count, 8, 128)).reshape(
        others * section_count, 8, 128
    )
    figures = lax.all_to_all(figures, MESH_AXES, split_axis=0, concat_axis=0, tiled=True)
    sums = jnp.sum(figures[:, 0, :], axis=0)
    grand_total = sums[3 * matrix_count]
    clip_factor = jnp.minimum(1.0, max_norm / (jnp.sqrt(grand_total) + 1e-06))
    grad_scale = (1.0 + mom_beta) * clip_factor
    momentum_scale = mom_beta * mom_beta
    update_norm = (
        grad_scale * grad_scale * sums[:matrix_count]
        + 2.0 * grad_scale * momentum_scale * sums[matrix_count : 2 * matrix_count]
        + momentum_scale * momentum_scale * sums[2 * matrix_count : 3 * matrix_count]
    )
    update_norm = jnp.maximum(update_norm, 0.0)[:, None, None]

    new_momentum = mom_beta * own_momentum + clip_factor * grad_rows
    nesterov = clip_factor * grad_rows + mom_beta * new_momentum
    scaled = (nesterov / (jnp.sqrt(update_norm) + 1e-07)).astype(jnp.bfloat16)

    owner_count = shard_count // matrix_count
    if owner_count == 1:
        row_block = lax.all_to_all(scaled, "shard", split_axis=0, concat_axis=0, tiled=True)
        row_block = row_block.reshape(shard_count * local_height, width)
    else:
        everything = lax.all_gather(scaled, "shard", axis=1, tiled=True)
        row_block = lax.dynamic_index_in_dim(
            everything, shard_index // owner_count, 0, keepdims=False
        )

    blocks = [row_block]
    for offset in range(1, tensor_count):
        pairs = [(i, i ^ offset) for i in range(tensor_count)]
        blocks.append(lax.ppermute(row_block, "tensor", pairs))
    (own_result,) = orthogonalize([[block] for block in blocks])

    if owner_count == 1:
        own_update = lax.all_to_all(
            own_result.reshape(shard_count, local_height, width),
            "shard",
            split_axis=0,
            concat_axis=0,
            tiled=True,
        )
    else:
        piece_length = local_height * width // owner_count
        split_rows = own_result.reshape(shard_count, owner_count, piece_length)
        returning = lax.dynamic_index_in_dim(
            split_rows, shard_index % owner_count, 1, keepdims=False
        )
        received = lax.all_to_all(returning, "shard", split_axis=0, concat_axis=0, tiled=True)
        own_update = received.reshape(matrix_count, local_height, width)
    orthogonal_update = own_update[None]
    muon_scale = 0.2 * math.sqrt(D)
    new_weights = (
        weights.astype(jnp.float32) * (1.0 - muon_rate * muon_decay)
        - muon_rate * muon_scale * orthogonal_update.astype(jnp.float32)
    ).astype(jnp.bfloat16)
    vector_clipped = clip_factor * vector_rows
    updated_first = 0.9 * first_moment + 0.1 * vector_clipped
    updated_second = 0.999 * second_moment + 0.001 * vector_clipped * vector_clipped
    adam_direction = updated_first / (jnp.sqrt(updated_second) + 1e-08)
    new_vectors = vectors * (1.0 - adam_rate * adam_decay) - adam_rate * adam_direction
    return (new_momentum[None], orthogonal_update, new_weights, adam_direction, new_vectors)


def solution(mesh):
    in_specs = (
        P("shard", "section", None, "tensor", None),
        P("shard", "section", None, "tensor"),
        P("section", None, ("tensor", "shard"), None),
        P("section", None, ("tensor", "shard"), None),
        P("section", None, ("tensor", "shard")),
        P("section", None, ("tensor", "shard")),
        P("section", None, ("tensor", "shard")),
    )
    out_specs = (
        P("section", None, ("tensor", "shard"), None),
        P("section", None, ("tensor", "shard"), None),
        P("section", None, ("tensor", "shard"), None),
        P("section", None, ("tensor", "shard")),
        P("section", None, ("tensor", "shard")),
    )
    return jax.shard_map(
        per_device, mesh=mesh, in_specs=in_specs, out_specs=out_specs, check_vma=False
    )
```

```python
import functools
import math

import jax
import jax.numpy as jnp
from jax import lax
from jax.experimental import pallas as pl
from jax.experimental.pallas import tpu as pltpu
from jax.sharding import PartitionSpec as P

D = 1024
NS_STEPS = 2


ns_first = 3.4445
ns_second = -4.775
ns_third = 2.0315
mom_beta = 0.95
max_norm = 1024.0
muon_rate = 0.02
muon_decay = 0.1
adam_rate = 0.001
adam_decay = 0.01

VECTOR_ROWS = 16
FIGURES = 16
MIB = 2**20
LANES = 128
MESH_AXES = ("shard", "tensor", "section")


def gram_of(blocks, gram_ref):
    width = blocks[0].shape[1]
    step = 256
    for start in range(0, width, step):
        stop = start + step
        total = None
        for block in blocks:
            whole = block[...]
            product = lax.dot_general(
                whole[:, :stop],
                whole[:, start:stop],
                (((0,), (0,)), ((), ())),
                preferred_element_type=jnp.float32,
            )
            rounded = product.astype(jnp.bfloat16).astype(jnp.float32)
            total = rounded if total is None else total + rounded
        gram_ref[:stop, start:stop] = total.astype(jnp.bfloat16)
        for above in range(0, start, step):
            tile = gram_ref[above : above + step, start:stop]
            gram_ref[start:stop, above : above + step] = tile.T


def polynomial(block, gram_ref):
    gram = gram_ref[...]
    first = jnp.dot(block, gram, preferred_element_type=jnp.float32).astype(jnp.bfloat16)
    second = jnp.dot(first, gram, preferred_element_type=jnp.float32)
    combined = (
        ns_first * block.astype(jnp.float32)
        + ns_second * first.astype(jnp.float32)
        + ns_third * second
    )
    return combined.astype(jnp.bfloat16)


def orthogonalize_kernel(count, pieces, *refs):
    height, width = refs[0].shape
    inputs = refs[: count * pieces]
    outputs = refs[count * pieces : count * pieces + pieces]
    gram_ref, start_ref, next_ref = refs[count * pieces + pieces :]
    for position in range(count):
        for piece in range(pieces):
            start_ref[position, piece * height : (piece + 1) * height, :] = inputs[
                position * pieces + piece
            ][...]
    current, other = start_ref, next_ref
    for iteration in range(NS_STEPS - 1):
        gram_of([current.at[position] for position in range(count)], gram_ref)
        for position in range(count):
            other[position] = polynomial(current[position], gram_ref)
        current, other = other, current
    gram_of([current.at[position] for position in range(count)], gram_ref)
    result = polynomial(current[0], gram_ref)
    for piece in range(pieces):
        outputs[piece][...] = result[piece * height : (piece + 1) * height, :]


def orthogonalize(blocks):
    count, pieces = len(blocks), len(blocks[0])
    height, width = blocks[0][0].shape
    return pl.pallas_call(
        functools.partial(orthogonalize_kernel, count, pieces),
        out_shape=[jax.ShapeDtypeStruct((height, width), jnp.bfloat16)] * pieces,
        scratch_shapes=[
            pltpu.VMEM((width, width), jnp.bfloat16),
            pltpu.VMEM((count, pieces * height, width), jnp.bfloat16),
            pltpu.VMEM((count, pieces * height, width), jnp.bfloat16),
        ],
        compiler_params=pltpu.CompilerParams(vmem_limit_bytes=32 * MIB),
    )(*[piece for block in blocks for piece in block])


def folded(array):
    line = jnp.sum(array, axis=0, keepdims=True)
    total = line[:, :LANES]
    for start in range(LANES, line.shape[1], LANES):
        total = total + line[:, start : start + LANES]
    return total


def slices_kernel(count, place_ref, grad_ref, *refs):
    outputs, semaphores = refs[:count], refs[count]
    copies = [
        pltpu.make_async_copy(
            grad_ref.at[:, place_ref[offset]], outputs[offset], semaphores.at[offset]
        )
        for offset in range(count)
    ]
    for copy in reversed(copies):
        copy.start()
    for copy in reversed(copies):
        copy.wait()


def row_slices(place, by_rows):
    matrix_count, shard_count, height, width = by_rows.shape
    return pl.pallas_call(
        functools.partial(slices_kernel, shard_count),
        out_shape=[jax.ShapeDtypeStruct((matrix_count, height, width), by_rows.dtype)]
        * shard_count,
        in_specs=[
            pl.BlockSpec(memory_space=pltpu.SMEM),
            pl.BlockSpec(memory_space=pltpu.HBM),
        ],
        out_specs=[pl.BlockSpec(memory_space=pltpu.VMEM)] * shard_count,
        scratch_shapes=[pltpu.SemaphoreType.DMA((shard_count,))],
        compiler_params=pltpu.CompilerParams(vmem_limit_bytes=4 * MIB),
    )(place, by_rows)


def sum_kernel(shard_count, place_ref, *refs):
    parts = refs[:shard_count]
    vector_parts, momentum_ref, grad_ref, vector_ref, figures_ref = refs[shard_count:]
    vector = jnp.sum(vector_parts[...].astype(jnp.float32), axis=0)
    vector_ref[...] = vector
    total = folded(vector * vector) * (1.0 / shard_count)
    squares, crosses, momentum_squares = [], [], []
    for matrix in range(momentum_ref.shape[0]):
        grad = parts[0][matrix].astype(jnp.float32)
        for part in parts[1:]:
            grad = grad + part[matrix].astype(jnp.float32)
        grad_ref[matrix] = grad
        old = momentum_ref[matrix]
        squares.append(folded(grad * grad))
        crosses.append(folded(grad * old))
        momentum_squares.append(folded(old * old))
        total = total + squares[-1]
    lines = squares + crosses + momentum_squares + [total]
    lines = lines + [jnp.zeros_like(total)] * (FIGURES - len(lines))
    tile = jnp.concatenate(lines, axis=0)
    sums = jnp.sum(tile, axis=1, keepdims=True)
    line_index = lax.broadcasted_iota(jnp.int32, tile.shape, 0)
    lane_index = lax.broadcasted_iota(jnp.int32, tile.shape, 1)
    line = jnp.sum(jnp.where(line_index == lane_index, sums, 0.0), axis=0, keepdims=True)
    total_only = jnp.where(lane_index[:1] == 3 * momentum_ref.shape[0], line, 0.0)
    for section in range(figures_ref.shape[1]):
        chosen = jnp.where(place_ref[shard_count] == section, line, total_only)
        figures_ref[:, section] = jnp.broadcast_to(
            chosen[None], (figures_ref.shape[0],) + line.shape
        )


def scale_kernel(matrix_count, place_ref, figures_ref, grad_ref, momentum_ref, *refs):
    outputs = refs[:matrix_count]
    clip_ref = refs[matrix_count]
    line = jnp.sum(figures_ref[...], axis=0)
    line_index = lax.broadcasted_iota(jnp.int32, (FIGURES, LANES), 0)
    lane_index = lax.broadcasted_iota(jnp.int32, (FIGURES, LANES), 1)
    sums = jnp.sum(jnp.where(line_index == lane_index, line, 0.0), axis=1, keepdims=True)
    total = sums[3 * matrix_count : 3 * matrix_count + 1]
    clip = jnp.minimum(1.0, max_norm / (jnp.sqrt(total) + 1e-06))
    clip_ref[...] = jnp.broadcast_to(clip, clip_ref.shape)
    grad_scale = (1.0 + mom_beta) * clip
    momentum_scale = mom_beta * mom_beta
    update_norm = (
        grad_scale * grad_scale * sums[:matrix_count]
        + 2.0 * grad_scale * momentum_scale * sums[matrix_count : 2 * matrix_count]
        + momentum_scale * momentum_scale * sums[2 * matrix_count : 3 * matrix_count]
    )
    inverse = 1.0 / (jnp.sqrt(jnp.maximum(update_norm, 0.0)) + 1e-07)
    position = lax.broadcasted_iota(jnp.int32, inverse.shape, 0)
    for place in range(matrix_count):
        matrix = place_ref[place]
        factor = jnp.sum(jnp.where(position == matrix, inverse, 0.0), axis=0, keepdims=True)
        clipped = clip * grad_ref[matrix]
        new_momentum = mom_beta * momentum_ref[matrix] + clipped
        nesterov = clipped + mom_beta * new_momentum
        outputs[place][...] = (nesterov * factor).astype(jnp.bfloat16)


def end_kernel(offsets, place_ref, *refs):
    arrived = refs[: len(offsets)]
    weights_ref = refs[len(offsets)]
    update_ref, new_weights_ref, update_rows, weight_rows, semaphores = refs[-5:]
    step_size = muon_rate * (0.2 * math.sqrt(D))
    copies = []
    for slot, offset in enumerate(offsets):
        matrix = place_ref[offset]
        update = arrived[slot][...]
        update_rows[slot] = update
        weight_rows[slot] = (
            weights_ref[matrix].astype(jnp.float32) * (1.0 - muon_rate * muon_decay)
            - step_size * update.astype(jnp.float32)
        ).astype(jnp.bfloat16)
        for kind, (rows, target) in enumerate(
            ((update_rows, update_ref), (weight_rows, new_weights_ref))
        ):
            copies.append(
                pltpu.make_async_copy(
                    rows.at[slot], target.at[matrix], semaphores.at[2 * slot + kind]
                )
            )
            copies[-1].start()
    for copy in copies:
        copy.wait()


def finished(offsets, place, arrived, weights, partial=()):
    height, width = arrived[0].shape
    anywhere = pl.BlockSpec(memory_space=pltpu.HBM)
    return pl.pallas_call(
        functools.partial(end_kernel, offsets),
        out_shape=[jax.ShapeDtypeStruct(weights.shape, weights.dtype)] * 2,
        in_specs=[pl.BlockSpec(memory_space=pltpu.SMEM)]
        + [pl.BlockSpec(memory_space=pltpu.VMEM)] * (len(arrived) + 1)
        + [anywhere] * len(partial),
        out_specs=[anywhere] * 2,
        scratch_shapes=[
            pltpu.VMEM((len(offsets), height, width), weights.dtype),
            pltpu.VMEM((len(offsets), height, width), weights.dtype),
            pltpu.SemaphoreType.DMA((2 * len(offsets),)),
        ],
        input_output_aliases={len(arrived) + 2 + i: i for i in range(len(partial))},
        compiler_params=pltpu.CompilerParams(vmem_limit_bytes=8 * MIB),
    )(place, *arrived, weights, *partial)


def state_kernel(
    place_ref,
    clip_ref,
    grad_ref,
    momentum_ref,
    sums_ref,
    vectors_ref,
    first_ref,
    second_ref,
    new_momentum_ref,
    direction_ref,
    new_ref,
):
    new_momentum_ref[...] = mom_beta * momentum_ref[...] + clip_ref[0:1, 0:1] * grad_ref[...]
    width = vectors_ref.shape[1]
    count = sums_ref.shape[1] // width
    rows = sums_ref[:, :width]
    for position in range(1, count):
        part = sums_ref[:, position * width : (position + 1) * width]
        rows = jnp.where(place_ref[0] == position, part, rows)
    clipped = clip_ref[0:1, 0:1] * rows
    updated_first = 0.9 * first_ref[...] + 0.1 * clipped
    updated_second = 0.999 * second_ref[...] + 0.001 * clipped * clipped
    direction = updated_first / (jnp.sqrt(updated_second) + 1e-08)
    direction_ref[...] = direction
    new_ref[...] = vectors_ref[...] * (1.0 - adam_rate * adam_decay) - adam_rate * direction


def on_device(kernel, scalars, operands, out_shape):
    return pl.pallas_call(
        kernel,
        out_shape=out_shape,
        in_specs=[pl.BlockSpec(memory_space=pltpu.SMEM)]
        + [pl.BlockSpec(memory_space=pltpu.VMEM)] * len(operands),
        compiler_params=pltpu.CompilerParams(vmem_limit_bytes=16 * MIB),
    )(scalars, *operands)


def swapped(array, axis, offset):
    pairs = [(i, i ^ offset) for i in range(lax.axis_size(axis))]
    return lax.ppermute(array, axis, pairs)


def after(array, earlier):
    return lax.optimization_barrier((array, earlier))[0]


def per_device(grad_parts, vector_grads, momentum, weights, vectors, first_moment, second_moment):
    shard_count = lax.axis_size("shard")
    tensor_count = lax.axis_size("tensor")
    section_count = lax.axis_size("section")
    _, matrix_count, local_height, width = momentum.shape
    if shard_count != matrix_count or shard_count != 4 or tensor_count != 4:
        return general_device(
            grad_parts, vector_grads, momentum, weights, vectors, first_moment, second_moment
        )
    vector_count, vector_width = vectors.shape[1:]
    own_momentum = momentum[0]
    position = jnp.arange(shard_count + 1, dtype=jnp.int32)
    place = jnp.where(
        position == shard_count,
        lax.axis_index("section").astype(jnp.int32),
        lax.axis_index("shard").astype(jnp.int32) ^ position,
    )

    by_rows = grad_parts.reshape(matrix_count, shard_count, local_height, width)
    parts = list(row_slices(place, by_rows))
    for offset in reversed(range(1, shard_count)):
        parts[offset] = swapped(parts[offset], "shard", offset)
    vector_parts = lax.all_to_all(
        jnp.broadcast_to(vector_grads[0], (shard_count, vector_count, vector_width * shard_count)),
        "shard",
        split_axis=0,
        concat_axis=0,
        tiled=True,
    )

    others = shard_count * tensor_count
    grad_rows, vector_whole, figures = on_device(
        functools.partial(sum_kernel, shard_count),
        place,
        parts[::-1] + [vector_parts, own_momentum],
        [
            jax.ShapeDtypeStruct(own_momentum.shape, jnp.float32),
            jax.ShapeDtypeStruct(vector_parts.shape[1:], jnp.float32),
            jax.ShapeDtypeStruct((others, section_count, 1, LANES), jnp.float32),
        ],
    )
    figures = lax.all_to_all(
        figures.reshape(others * section_count, 1, LANES),
        MESH_AXES,
        split_axis=0,
        concat_axis=0,
        tiled=True,
    )
    *scaled, clip_tile = on_device(
        functools.partial(scale_kernel, matrix_count),
        place,
        [figures, grad_rows, own_momentum],
        [jax.ShapeDtypeStruct((local_height, width), jnp.bfloat16)] * matrix_count
        + [jax.ShapeDtypeStruct((8, LANES), jnp.float32)],
    )

    pieces = [scaled[0]] + [None] * 3
    for offset in (2, 3, 1):
        pieces[offset] = swapped(scaled[offset], "shard", offset)
    near, side, far = [None] * 4, [None] * 4, [None] * 4
    near[0] = swapped(pieces[0], "tensor", 1)
    side[0] = swapped(pieces[0], "tensor", 2)
    far[0] = swapped(near[0], "tensor", 2)
    near[1] = swapped(pieces[1], "tensor", 1)
    side[1] = swapped(after(pieces[1], near[0]), "tensor", 2)
    far[1] = swapped(side[1], "tensor", 1)
    near[2] = swapped(pieces[2], "tensor", 1)
    side[2] = swapped(after(pieces[2], side[0]), "tensor", 2)
    far[2] = swapped(near[2], "tensor", 2)
    near[3] = swapped(after(pieces[3], near[1]), "tensor", 1)
    side[3] = swapped(after(pieces[3], near[1]), "tensor", 2)
    far[3] = swapped(side[3], "tensor", 1)
    results = orthogonalize([pieces, near, side, far])

    returned = {
        offset: swapped(results[offset], "shard", offset)
        for offset in reversed(range(1, shard_count))
    }
    early = finished((0,), place, [results[0]], weights[0])
    orthogonal_update, new_weights = finished(
        (3, 2, 1), place, [returned[offset] for offset in (3, 2, 1)], weights[0], early
    )
    new_momentum, adam_direction, new_vectors = on_device(
        state_kernel,
        place,
        [
            after(clip_tile, results[0]),
            grad_rows,
            own_momentum,
            vector_whole,
            vectors[0],
            first_moment[0],
            second_moment[0],
        ],
        [jax.ShapeDtypeStruct(own_momentum.shape, jnp.float32)]
        + [jax.ShapeDtypeStruct(vectors.shape[1:], jnp.float32)] * 2,
    )
    return (
        new_momentum[None],
        orthogonal_update[None],
        new_weights[None],
        adam_direction[None],
        new_vectors[None],
    )


def general_device(grad_parts, vector_grads, momentum, weights, vectors, first_moment, second_moment):
    shard_count = lax.axis_size("shard")
    tensor_count = lax.axis_size("tensor")
    section_count = lax.axis_size("section")
    shard_index = lax.axis_index("shard")
    _, matrix_count, local_height, width = momentum.shape
    vector_width = vectors.shape[2]
    own_momentum = momentum[0]

    rows = matrix_count * local_height
    by_target = (
        grad_parts.reshape(matrix_count, shard_count, local_height, width)
        .transpose(1, 0, 2, 3)
        .reshape(shard_count, rows, width)
    )
    vector_line = jnp.broadcast_to(
        vector_grads.reshape(1, 1, width), (shard_count, VECTOR_ROWS, width)
    )
    payload = jnp.concatenate([by_target, vector_line], axis=1)
    arrived = lax.all_to_all(payload, "shard", split_axis=0, concat_axis=0, tiled=True)
    grad_rows = jnp.sum(arrived[:, :rows].astype(jnp.float32), axis=0).reshape(
        matrix_count, local_height, width
    )
    vector_whole = jnp.sum(arrived[:, rows].astype(jnp.float32), axis=0).reshape(
        vectors.shape[1], vector_width * shard_count
    )
    vector_rows = lax.dynamic_slice_in_dim(
        vector_whole, shard_index * vector_width, vector_width, 1
    )

    grad_squares = jnp.sum(grad_rows * grad_rows, axis=(1, 2))
    cross = jnp.sum(grad_rows * own_momentum, axis=(1, 2))
    momentum_squares = jnp.sum(own_momentum * own_momentum, axis=(1, 2))
    own_total = jnp.sum(grad_squares) + jnp.sum(vector_rows * vector_rows)
    same_section = (
        jnp.arange(section_count) == lax.axis_index("section")
    ).astype(jnp.float32)[:, None]
    matrix_figures = jnp.concatenate([grad_squares, cross, momentum_squares])
    line = jnp.concatenate(
        [
            same_section * matrix_figures[None],
            jnp.broadcast_to(own_total, (section_count, 1)),
            jnp.zeros((section_count, 127 - 3 * matrix_count), jnp.float32),
        ],
        axis=1,
    )
    others = shard_count * tensor_count
    figures = jnp.broadcast_to(line[None, :, None, :], (others, section_count, 8, 128)).reshape(
        others * section_count, 8, 128
    )
    figures = lax.all_to_all(figures, MESH_AXES, split_axis=0, concat_axis=0, tiled=True)
    sums = jnp.sum(figures[:, 0, :], axis=0)
    grand_total = sums[3 * matrix_count]
    clip_factor = jnp.minimum(1.0, max_norm / (jnp.sqrt(grand_total) + 1e-06))
    grad_scale = (1.0 + mom_beta) * clip_factor
    momentum_scale = mom_beta * mom_beta
    update_norm = (
        grad_scale * grad_scale * sums[:matrix_count]
        + 2.0 * grad_scale * momentum_scale * sums[matrix_count : 2 * matrix_count]
        + momentum_scale * momentum_scale * sums[2 * matrix_count : 3 * matrix_count]
    )
    update_norm = jnp.maximum(update_norm, 0.0)[:, None, None]

    new_momentum = mom_beta * own_momentum + clip_factor * grad_rows
    nesterov = clip_factor * grad_rows + mom_beta * new_momentum
    scaled = (nesterov / (jnp.sqrt(update_norm) + 1e-07)).astype(jnp.bfloat16)

    owner_count = shard_count // matrix_count
    if owner_count == 1:
        row_block = lax.all_to_all(scaled, "shard", split_axis=0, concat_axis=0, tiled=True)
        row_block = row_block.reshape(shard_count * local_height, width)
    else:
        everything = lax.all_gather(scaled, "shard", axis=1, tiled=True)
        row_block = lax.dynamic_index_in_dim(
            everything, shard_index // owner_count, 0, keepdims=False
        )

    blocks = [row_block]
    for offset in range(1, tensor_count):
        pairs = [(i, i ^ offset) for i in range(tensor_count)]
        blocks.append(lax.ppermute(row_block, "tensor", pairs))
    (own_result,) = orthogonalize([[block] for block in blocks])

    if owner_count == 1:
        own_update = lax.all_to_all(
            own_result.reshape(shard_count, local_height, width),
            "shard",
            split_axis=0,
            concat_axis=0,
            tiled=True,
        )
    else:
        piece_length = local_height * width // owner_count
        split_rows = own_result.reshape(shard_count, owner_count, piece_length)
        returning = lax.dynamic_index_in_dim(
            split_rows, shard_index % owner_count, 1, keepdims=False
        )
        received = lax.all_to_all(returning, "shard", split_axis=0, concat_axis=0, tiled=True)
        own_update = received.reshape(matrix_count, local_height, width)
    orthogonal_update = own_update[None]
    muon_scale = 0.2 * math.sqrt(D)
    new_weights = (
        weights.astype(jnp.float32) * (1.0 - muon_rate * muon_decay)
        - muon_rate * muon_scale * orthogonal_update.astype(jnp.float32)
    ).astype(jnp.bfloat16)
    vector_clipped = clip_factor * vector_rows
    updated_first = 0.9 * first_moment + 0.1 * vector_clipped
    updated_second = 0.999 * second_moment + 0.001 * vector_clipped * vector_clipped
    adam_direction = updated_first / (jnp.sqrt(updated_second) + 1e-08)
    new_vectors = vectors * (1.0 - adam_rate * adam_decay) - adam_rate * adam_direction
    return (new_momentum[None], orthogonal_update, new_weights, adam_direction, new_vectors)


def solution(mesh):
    in_specs = (
        P("shard", "section", None, "tensor", None),
        P("shard", "section", None, "tensor"),
        P("section", None, ("tensor", "shard"), None),
        P("section", None, ("tensor", "shard"), None),
        P("section", None, ("tensor", "shard")),
        P("section", None, ("tensor", "shard")),
        P("section", None, ("tensor", "shard")),
    )
    out_specs = (
        P("section", None, ("tensor", "shard"), None),
        P("section", None, ("tensor", "shard"), None),
        P("section", None, ("tensor", "shard"), None),
        P("section", None, ("tensor", "shard")),
        P("section", None, ("tensor", "shard")),
    )
    return jax.shard_map(
        per_device, mesh=mesh, in_specs=in_specs, out_specs=out_specs, check_vma=False
    )
```

```python
import functools
import math

import jax
import jax.numpy as jnp
from jax import lax
from jax.experimental import pallas as pl
from jax.experimental.pallas import tpu as pltpu
from jax.sharding import PartitionSpec as P

D = 1024
NS_STEPS = 2


ns_first = 3.4445
ns_second = -4.775
ns_third = 2.0315
mom_beta = 0.95
max_norm = 1024.0
muon_rate = 0.02
muon_decay = 0.1
adam_rate = 0.001
adam_decay = 0.01

VECTOR_ROWS = 16
FIGURES = 16
MIB = 2**20
LANES = 128
MESH_AXES = ("shard", "tensor", "section")


def gram_of(blocks, gram_ref):
    width = blocks[0].shape[1]
    step = 256
    for start in range(0, width, step):
        stop = start + step
        total = None
        for block in blocks:
            whole = block[...]
            product = lax.dot_general(
                whole[:, :stop],
                whole[:, start:stop],
                (((0,), (0,)), ((), ())),
                preferred_element_type=jnp.float32,
            )
            rounded = product.astype(jnp.bfloat16).astype(jnp.float32)
            total = rounded if total is None else total + rounded
        gram_ref[:stop, start:stop] = total.astype(jnp.bfloat16)
        for above in range(0, start, step):
            tile = gram_ref[above : above + step, start:stop]
            gram_ref[start:stop, above : above + step] = tile.T


def polynomial(block, gram_ref):
    gram = gram_ref[...]
    first = jnp.dot(block, gram, preferred_element_type=jnp.float32).astype(jnp.bfloat16)
    second = jnp.dot(first, gram, preferred_element_type=jnp.float32)
    combined = (
        ns_first * block.astype(jnp.float32)
        + ns_second * first.astype(jnp.float32)
        + ns_third * second
    )
    return combined.astype(jnp.bfloat16)


def orthogonalize_kernel(count, pieces, *refs):
    height, width = refs[0].shape
    inputs = refs[: count * pieces]
    outputs = refs[count * pieces : count * pieces + pieces]
    gram_ref, start_ref, next_ref = refs[count * pieces + pieces :]
    for position in range(count):
        for piece in range(pieces):
            start_ref[position, piece * height : (piece + 1) * height, :] = inputs[
                position * pieces + piece
            ][...]
    current, other = start_ref, next_ref
    for iteration in range(NS_STEPS - 1):
        gram_of([current.at[position] for position in range(count)], gram_ref)
        for position in range(count):
            other[position] = polynomial(current[position], gram_ref)
        current, other = other, current
    gram_of([current.at[position] for position in range(count)], gram_ref)
    result = polynomial(current[0], gram_ref)
    for piece in range(pieces):
        outputs[piece][...] = result[piece * height : (piece + 1) * height, :]


def orthogonalize(blocks):
    count, pieces = len(blocks), len(blocks[0])
    height, width = blocks[0][0].shape
    return pl.pallas_call(
        functools.partial(orthogonalize_kernel, count, pieces),
        out_shape=[jax.ShapeDtypeStruct((height, width), jnp.bfloat16)] * pieces,
        scratch_shapes=[
            pltpu.VMEM((width, width), jnp.bfloat16),
            pltpu.VMEM((count, pieces * height, width), jnp.bfloat16),
            pltpu.VMEM((count, pieces * height, width), jnp.bfloat16),
        ],
        compiler_params=pltpu.CompilerParams(vmem_limit_bytes=32 * MIB),
    )(*[piece for block in blocks for piece in block])


def folded(array):
    line = jnp.sum(array, axis=0, keepdims=True)
    total = line[:, :LANES]
    for start in range(LANES, line.shape[1], LANES):
        total = total + line[:, start : start + LANES]
    return total


def slices_kernel(count, place_ref, grad_ref, *refs):
    outputs, semaphores = refs[:count], refs[count]
    copies = [
        pltpu.make_async_copy(
            grad_ref.at[:, place_ref[offset]], outputs[offset], semaphores.at[offset]
        )
        for offset in range(count)
    ]
    for copy in reversed(copies):
        copy.start()
    for copy in reversed(copies):
        copy.wait()


def row_slices(place, by_rows):
    matrix_count, shard_count, height, width = by_rows.shape
    return pl.pallas_call(
        functools.partial(slices_kernel, shard_count),
        out_shape=[jax.ShapeDtypeStruct((matrix_count, height, width), by_rows.dtype)]
        * shard_count,
        in_specs=[
            pl.BlockSpec(memory_space=pltpu.SMEM),
            pl.BlockSpec(memory_space=pltpu.HBM),
        ],
        out_specs=[pl.BlockSpec(memory_space=pltpu.VMEM)] * shard_count,
        scratch_shapes=[pltpu.SemaphoreType.DMA((shard_count,))],
        compiler_params=pltpu.CompilerParams(vmem_limit_bytes=4 * MIB),
    )(place, by_rows)


def sum_kernel(shard_count, place_ref, *refs):
    parts = refs[:shard_count]
    vector_parts, momentum_ref, grad_ref, vector_ref, figures_ref = refs[shard_count:]
    vector = jnp.sum(vector_parts[...].astype(jnp.float32), axis=0)
    vector_ref[...] = vector
    total = folded(vector * vector) * (1.0 / shard_count)
    squares, crosses, momentum_squares = [], [], []
    for matrix in range(momentum_ref.shape[0]):
        grad = parts[0][matrix].astype(jnp.float32)
        for part in parts[1:]:
            grad = grad + part[matrix].astype(jnp.float32)
        grad_ref[matrix] = grad
        old = momentum_ref[matrix]
        squares.append(folded(grad * grad))
        crosses.append(folded(grad * old))
        momentum_squares.append(folded(old * old))
        total = total + squares[-1]
    lines = squares + crosses + momentum_squares + [total]
    lines = lines + [jnp.zeros_like(total)] * (FIGURES - len(lines))
    tile = jnp.concatenate(lines, axis=0)
    sums = jnp.sum(tile, axis=1, keepdims=True)
    line_index = lax.broadcasted_iota(jnp.int32, tile.shape, 0)
    lane_index = lax.broadcasted_iota(jnp.int32, tile.shape, 1)
    line = jnp.sum(jnp.where(line_index == lane_index, sums, 0.0), axis=0, keepdims=True)
    total_only = jnp.where(lane_index[:1] == 3 * momentum_ref.shape[0], line, 0.0)
    for section in range(figures_ref.shape[1]):
        chosen = jnp.where(place_ref[shard_count] == section, line, total_only)
        figures_ref[:, section] = jnp.broadcast_to(
            chosen[None], (figures_ref.shape[0],) + line.shape
        )


def scale_kernel(matrix_count, place_ref, figures_ref, grad_ref, momentum_ref, *refs):
    outputs = refs[:matrix_count]
    clip_ref = refs[matrix_count]
    line = jnp.sum(figures_ref[...], axis=0)
    line_index = lax.broadcasted_iota(jnp.int32, (FIGURES, LANES), 0)
    lane_index = lax.broadcasted_iota(jnp.int32, (FIGURES, LANES), 1)
    sums = jnp.sum(jnp.where(line_index == lane_index, line, 0.0), axis=1, keepdims=True)
    total = sums[3 * matrix_count : 3 * matrix_count + 1]
    clip = jnp.minimum(1.0, max_norm / (jnp.sqrt(total) + 1e-06))
    clip_ref[...] = jnp.broadcast_to(clip, clip_ref.shape)
    grad_scale = (1.0 + mom_beta) * clip
    momentum_scale = mom_beta * mom_beta
    update_norm = (
        grad_scale * grad_scale * sums[:matrix_count]
        + 2.0 * grad_scale * momentum_scale * sums[matrix_count : 2 * matrix_count]
        + momentum_scale * momentum_scale * sums[2 * matrix_count : 3 * matrix_count]
    )
    inverse = 1.0 / (jnp.sqrt(jnp.maximum(update_norm, 0.0)) + 1e-07)
    position = lax.broadcasted_iota(jnp.int32, inverse.shape, 0)
    for place in range(matrix_count):
        matrix = place_ref[place]
        factor = jnp.sum(jnp.where(position == matrix, inverse, 0.0), axis=0, keepdims=True)
        clipped = clip * grad_ref[matrix]
        new_momentum = mom_beta * momentum_ref[matrix] + clipped
        nesterov = clipped + mom_beta * new_momentum
        outputs[place][...] = (nesterov * factor).astype(jnp.bfloat16)


def end_kernel(offsets, place_ref, *refs):
    arrived = refs[: len(offsets)]
    weights_ref = refs[len(offsets)]
    update_ref, new_weights_ref, update_rows, weight_rows, semaphores = refs[-5:]
    step_size = muon_rate * (0.2 * math.sqrt(D))
    copies = []
    for slot, offset in enumerate(offsets):
        matrix = place_ref[offset]
        update = arrived[slot][...]
        update_rows[slot] = update
        weight_rows[slot] = (
            weights_ref[matrix].astype(jnp.float32) * (1.0 - muon_rate * muon_decay)
            - step_size * update.astype(jnp.float32)
        ).astype(jnp.bfloat16)
        for kind, (rows, target) in enumerate(
            ((update_rows, update_ref), (weight_rows, new_weights_ref))
        ):
            copies.append(
                pltpu.make_async_copy(
                    rows.at[slot], target.at[matrix], semaphores.at[2 * slot + kind]
                )
            )
            copies[-1].start()
    for copy in copies:
        copy.wait()


def finished(offsets, place, arrived, weights, partial=()):
    height, width = arrived[0].shape
    anywhere = pl.BlockSpec(memory_space=pltpu.HBM)
    return pl.pallas_call(
        functools.partial(end_kernel, offsets),
        out_shape=[jax.ShapeDtypeStruct(weights.shape, weights.dtype)] * 2,
        in_specs=[pl.BlockSpec(memory_space=pltpu.SMEM)]
        + [pl.BlockSpec(memory_space=pltpu.VMEM)] * (len(arrived) + 1)
        + [anywhere] * len(partial),
        out_specs=[anywhere] * 2,
        scratch_shapes=[
            pltpu.VMEM((len(offsets), height, width), weights.dtype),
            pltpu.VMEM((len(offsets), height, width), weights.dtype),
            pltpu.SemaphoreType.DMA((2 * len(offsets),)),
        ],
        input_output_aliases={len(arrived) + 2 + i: i for i in range(len(partial))},
        compiler_params=pltpu.CompilerParams(vmem_limit_bytes=8 * MIB),
    )(place, *arrived, weights, *partial)


def state_kernel(
    place_ref,
    clip_ref,
    grad_ref,
    momentum_ref,
    sums_ref,
    vectors_ref,
    first_ref,
    second_ref,
    new_momentum_ref,
    direction_ref,
    new_ref,
):
    new_momentum_ref[...] = mom_beta * momentum_ref[...] + clip_ref[0:1, 0:1] * grad_ref[...]
    width = vectors_ref.shape[1]
    count = sums_ref.shape[1] // width
    rows = sums_ref[:, :width]
    for position in range(1, count):
        part = sums_ref[:, position * width : (position + 1) * width]
        rows = jnp.where(place_ref[0] == position, part, rows)
    clipped = clip_ref[0:1, 0:1] * rows
    updated_first = 0.9 * first_ref[...] + 0.1 * clipped
    updated_second = 0.999 * second_ref[...] + 0.001 * clipped * clipped
    direction = updated_first / (jnp.sqrt(updated_second) + 1e-08)
    direction_ref[...] = direction
    new_ref[...] = vectors_ref[...] * (1.0 - adam_rate * adam_decay) - adam_rate * direction


def on_device(kernel, scalars, operands, out_shape):
    return pl.pallas_call(
        kernel,
        out_shape=out_shape,
        in_specs=[pl.BlockSpec(memory_space=pltpu.SMEM)]
        + [pl.BlockSpec(memory_space=pltpu.VMEM)] * len(operands),
        compiler_params=pltpu.CompilerParams(vmem_limit_bytes=16 * MIB),
    )(scalars, *operands)


def swapped(array, axis, offset):
    pairs = [(i, i ^ offset) for i in range(lax.axis_size(axis))]
    return lax.ppermute(array, axis, pairs)


def after(array, earlier):
    return lax.optimization_barrier((array, earlier))[0]


def per_device(grad_parts, vector_grads, momentum, weights, vectors, first_moment, second_moment):
    shard_count = lax.axis_size("shard")
    tensor_count = lax.axis_size("tensor")
    section_count = lax.axis_size("section")
    _, matrix_count, local_height, width = momentum.shape
    if shard_count != matrix_count or shard_count != 4 or tensor_count != 4:
        return general_device(
            grad_parts, vector_grads, momentum, weights, vectors, first_moment, second_moment
        )
    vector_count, vector_width = vectors.shape[1:]
    own_momentum = momentum[0]
    position = jnp.arange(shard_count + 1, dtype=jnp.int32)
    place = jnp.where(
        position == shard_count,
        lax.axis_index("section").astype(jnp.int32),
        lax.axis_index("shard").astype(jnp.int32) ^ position,
    )

    by_rows = grad_parts.reshape(matrix_count, shard_count, local_height, width)
    parts = list(row_slices(place, by_rows))
    for offset in reversed(range(1, shard_count)):
        parts[offset] = swapped(parts[offset], "shard", offset)
    vector_parts = lax.all_to_all(
        jnp.broadcast_to(vector_grads[0], (shard_count, vector_count, vector_width * shard_count)),
        "shard",
        split_axis=0,
        concat_axis=0,
        tiled=True,
    )

    others = shard_count * tensor_count
    grad_rows, vector_whole, figures = on_device(
        functools.partial(sum_kernel, shard_count),
        place,
        parts[::-1] + [vector_parts, own_momentum],
        [
            jax.ShapeDtypeStruct(own_momentum.shape, jnp.float32),
            jax.ShapeDtypeStruct(vector_parts.shape[1:], jnp.float32),
            jax.ShapeDtypeStruct((others, section_count, 1, LANES), jnp.float32),
        ],
    )
    figures = lax.all_to_all(
        figures.reshape(others * section_count, 1, LANES),
        MESH_AXES,
        split_axis=0,
        concat_axis=0,
        tiled=True,
    )
    *scaled, clip_tile = on_device(
        functools.partial(scale_kernel, matrix_count),
        place,
        [figures, grad_rows, own_momentum],
        [jax.ShapeDtypeStruct((local_height, width), jnp.bfloat16)] * matrix_count
        + [jax.ShapeDtypeStruct((8, LANES), jnp.float32)],
    )

    pieces = [scaled[0]] + [None] * 3
    for offset in (2, 3, 1):
        ready = after(scaled[offset], pieces[2]) if offset == 3 else scaled[offset]
        pieces[offset] = swapped(ready, "shard", offset)
    near, side, far = [None] * 4, [None] * 4, [None] * 4
    near[0] = swapped(pieces[0], "tensor", 1)
    side[0] = swapped(pieces[0], "tensor", 2)
    far[0] = swapped(near[0], "tensor", 2)
    near[1] = swapped(pieces[1], "tensor", 1)
    side[1] = swapped(pieces[1], "tensor", 2)
    far[1] = swapped(side[1], "tensor", 1)
    near[2] = swapped(pieces[2], "tensor", 1)
    side[2] = swapped(pieces[2], "tensor", 2)
    far[2] = swapped(near[2], "tensor", 2)
    near[3] = swapped(pieces[3], "tensor", 1)
    side[3] = swapped(pieces[3], "tensor", 2)
    far[3] = swapped(pieces[3], "tensor", 3)
    results = orthogonalize([pieces, near, side, far])

    returned = {
        offset: swapped(results[offset], "shard", offset)
        for offset in reversed(range(1, shard_count))
    }
    early = finished((0,), place, [results[0]], weights[0])
    orthogonal_update, new_weights = finished(
        (3, 2, 1), place, [returned[offset] for offset in (3, 2, 1)], weights[0], early
    )
    new_momentum, adam_direction, new_vectors = on_device(
        state_kernel,
        place,
        [
            after(clip_tile, results[0]),
            grad_rows,
            own_momentum,
            vector_whole,
            vectors[0],
            first_moment[0],
            second_moment[0],
        ],
        [jax.ShapeDtypeStruct(own_momentum.shape, jnp.float32)]
        + [jax.ShapeDtypeStruct(vectors.shape[1:], jnp.float32)] * 2,
    )
    return (
        new_momentum[None],
        orthogonal_update[None],
        new_weights[None],
        adam_direction[None],
        new_vectors[None],
    )


def general_device(grad_parts, vector_grads, momentum, weights, vectors, first_moment, second_moment):
    shard_count = lax.axis_size("shard")
    tensor_count = lax.axis_size("tensor")
    section_count = lax.axis_size("section")
    shard_index = lax.axis_index("shard")
    _, matrix_count, local_height, width = momentum.shape
    vector_width = vectors.shape[2]
    own_momentum = momentum[0]

    rows = matrix_count * local_height
    by_target = (
        grad_parts.reshape(matrix_count, shard_count, local_height, width)
        .transpose(1, 0, 2, 3)
        .reshape(shard_count, rows, width)
    )
    vector_line = jnp.broadcast_to(
        vector_grads.reshape(1, 1, width), (shard_count, VECTOR_ROWS, width)
    )
    payload = jnp.concatenate([by_target, vector_line], axis=1)
    arrived = lax.all_to_all(payload, "shard", split_axis=0, concat_axis=0, tiled=True)
    grad_rows = jnp.sum(arrived[:, :rows].astype(jnp.float32), axis=0).reshape(
        matrix_count, local_height, width
    )
    vector_whole = jnp.sum(arrived[:, rows].astype(jnp.float32), axis=0).reshape(
        vectors.shape[1], vector_width * shard_count
    )
    vector_rows = lax.dynamic_slice_in_dim(
        vector_whole, shard_index * vector_width, vector_width, 1
    )

    grad_squares = jnp.sum(grad_rows * grad_rows, axis=(1, 2))
    cross = jnp.sum(grad_rows * own_momentum, axis=(1, 2))
    momentum_squares = jnp.sum(own_momentum * own_momentum, axis=(1, 2))
    own_total = jnp.sum(grad_squares) + jnp.sum(vector_rows * vector_rows)
    same_section = (
        jnp.arange(section_count) == lax.axis_index("section")
    ).astype(jnp.float32)[:, None]
    matrix_figures = jnp.concatenate([grad_squares, cross, momentum_squares])
    line = jnp.concatenate(
        [
            same_section * matrix_figures[None],
            jnp.broadcast_to(own_total, (section_count, 1)),
            jnp.zeros((section_count, 127 - 3 * matrix_count), jnp.float32),
        ],
        axis=1,
    )
    others = shard_count * tensor_count
    figures = jnp.broadcast_to(line[None, :, None, :], (others, section_count, 8, 128)).reshape(
        others * section_count, 8, 128
    )
    figures = lax.all_to_all(figures, MESH_AXES, split_axis=0, concat_axis=0, tiled=True)
    sums = jnp.sum(figures[:, 0, :], axis=0)
    grand_total = sums[3 * matrix_count]
    clip_factor = jnp.minimum(1.0, max_norm / (jnp.sqrt(grand_total) + 1e-06))
    grad_scale = (1.0 + mom_beta) * clip_factor
    momentum_scale = mom_beta * mom_beta
    update_norm = (
        grad_scale * grad_scale * sums[:matrix_count]
        + 2.0 * grad_scale * momentum_scale * sums[matrix_count : 2 * matrix_count]
        + momentum_scale * momentum_scale * sums[2 * matrix_count : 3 * matrix_count]
    )
    update_norm = jnp.maximum(update_norm, 0.0)[:, None, None]

    new_momentum = mom_beta * own_momentum + clip_factor * grad_rows
    nesterov = clip_factor * grad_rows + mom_beta * new_momentum
    scaled = (nesterov / (jnp.sqrt(update_norm) + 1e-07)).astype(jnp.bfloat16)

    owner_count = shard_count // matrix_count
    if owner_count == 1:
        row_block = lax.all_to_all(scaled, "shard", split_axis=0, concat_axis=0, tiled=True)
        row_block = row_block.reshape(shard_count * local_height, width)
    else:
        everything = lax.all_gather(scaled, "shard", axis=1, tiled=True)
        row_block = lax.dynamic_index_in_dim(
            everything, shard_index // owner_count, 0, keepdims=False
        )

    blocks = [row_block]
    for offset in range(1, tensor_count):
        pairs = [(i, i ^ offset) for i in range(tensor_count)]
        blocks.append(lax.ppermute(row_block, "tensor", pairs))
    (own_result,) = orthogonalize([[block] for block in blocks])

    if owner_count == 1:
        own_update = lax.all_to_all(
            own_result.reshape(shard_count, local_height, width),
            "shard",
            split_axis=0,
            concat_axis=0,
            tiled=True,
        )
    else:
        piece_length = local_height * width // owner_count
        split_rows = own_result.reshape(shard_count, owner_count, piece_length)
        returning = lax.dynamic_index_in_dim(
            split_rows, shard_index % owner_count, 1, keepdims=False
        )
        received = lax.all_to_all(returning, "shard", split_axis=0, concat_axis=0, tiled=True)
        own_update = received.reshape(matrix_count, local_height, width)
    orthogonal_update = own_update[None]
    muon_scale = 0.2 * math.sqrt(D)
    new_weights = (
        weights.astype(jnp.float32) * (1.0 - muon_rate * muon_decay)
        - muon_rate * muon_scale * orthogonal_update.astype(jnp.float32)
    ).astype(jnp.bfloat16)
    vector_clipped = clip_factor * vector_rows
    updated_first = 0.9 * first_moment + 0.1 * vector_clipped
    updated_second = 0.999 * second_moment + 0.001 * vector_clipped * vector_clipped
    adam_direction = updated_first / (jnp.sqrt(updated_second) + 1e-08)
    new_vectors = vectors * (1.0 - adam_rate * adam_decay) - adam_rate * adam_direction
    return (new_momentum[None], orthogonal_update, new_weights, adam_direction, new_vectors)


def solution(mesh):
    in_specs = (
        P("shard", "section", None, "tensor", None),
        P("shard", "section", None, "tensor"),
        P("section", None, ("tensor", "shard"), None),
        P("section", None, ("tensor", "shard"), None),
        P("section", None, ("tensor", "shard")),
        P("section", None, ("tensor", "shard")),
        P("section", None, ("tensor", "shard")),
    )
    out_specs = (
        P("section", None, ("tensor", "shard"), None),
        P("section", None, ("tensor", "shard"), None),
        P("section", None, ("tensor", "shard"), None),
        P("section", None, ("tensor", "shard")),
        P("section", None, ("tensor", "shard")),
    )
    return jax.shard_map(
        per_device, mesh=mesh, in_specs=in_specs, out_specs=out_specs, check_vma=False
    )
```

```python
import functools
import math

import jax
import jax.numpy as jnp
from jax import lax
from jax.experimental import pallas as pl
from jax.experimental.pallas import tpu as pltpu
from jax.sharding import PartitionSpec as P

D = 1024
NS_STEPS = 2


ns_first = 3.4445
ns_second = -4.775
ns_third = 2.0315
mom_beta = 0.95
max_norm = 1024.0
muon_rate = 0.02
muon_decay = 0.1
adam_rate = 0.001
adam_decay = 0.01

VECTOR_ROWS = 16
FIGURES = 16
MIB = 2**20
LANES = 128
MESH_AXES = ("shard", "tensor", "section")


def gram_of(blocks, gram_ref):
    width = blocks[0].shape[1]
    step = 256
    for start in range(0, width, step):
        stop = start + step
        total = None
        for block in blocks:
            whole = block[...]
            product = lax.dot_general(
                whole[:, :stop],
                whole[:, start:stop],
                (((0,), (0,)), ((), ())),
                preferred_element_type=jnp.float32,
            )
            rounded = product.astype(jnp.bfloat16).astype(jnp.float32)
            total = rounded if total is None else total + rounded
        gram_ref[:stop, start:stop] = total.astype(jnp.bfloat16)
        for above in range(0, start, step):
            tile = gram_ref[above : above + step, start:stop]
            gram_ref[start:stop, above : above + step] = tile.T


def polynomial(block, gram_ref):
    gram = gram_ref[...]
    first = jnp.dot(block, gram, preferred_element_type=jnp.float32).astype(jnp.bfloat16)
    second = jnp.dot(first, gram, preferred_element_type=jnp.float32)
    combined = (
        ns_first * block.astype(jnp.float32)
        + ns_second * first.astype(jnp.float32)
        + ns_third * second
    )
    return combined.astype(jnp.bfloat16)


def orthogonalize_kernel(count, pieces, *refs):
    height, width = refs[0].shape
    inputs = refs[: count * pieces]
    outputs = refs[count * pieces : count * pieces + pieces]
    gram_ref, start_ref, next_ref = refs[count * pieces + pieces :]
    for position in range(count):
        for piece in range(pieces):
            start_ref[position, piece * height : (piece + 1) * height, :] = inputs[
                position * pieces + piece
            ][...]
    current, other = start_ref, next_ref
    for iteration in range(NS_STEPS - 1):
        gram_of([current.at[position] for position in range(count)], gram_ref)
        for position in range(count):
            other[position] = polynomial(current[position], gram_ref)
        current, other = other, current
    gram_of([current.at[position] for position in range(count)], gram_ref)
    result = polynomial(current[0], gram_ref)
    for piece in range(pieces):
        outputs[piece][...] = result[piece * height : (piece + 1) * height, :]


def orthogonalize(blocks):
    count, pieces = len(blocks), len(blocks[0])
    height, width = blocks[0][0].shape
    return pl.pallas_call(
        functools.partial(orthogonalize_kernel, count, pieces),
        out_shape=[jax.ShapeDtypeStruct((height, width), jnp.bfloat16)] * pieces,
        scratch_shapes=[
            pltpu.VMEM((width, width), jnp.bfloat16),
            pltpu.VMEM((count, pieces * height, width), jnp.bfloat16),
            pltpu.VMEM((count, pieces * height, width), jnp.bfloat16),
        ],
        compiler_params=pltpu.CompilerParams(vmem_limit_bytes=32 * MIB),
    )(*[piece for block in blocks for piece in block])


def folded(array):
    line = jnp.sum(array, axis=0, keepdims=True)
    total = line[:, :LANES]
    for start in range(LANES, line.shape[1], LANES):
        total = total + line[:, start : start + LANES]
    return total


def slices_kernel(count, place_ref, grad_ref, *refs):
    outputs, semaphores = refs[:count], refs[count]
    copies = [
        pltpu.make_async_copy(
            grad_ref.at[:, place_ref[offset]], outputs[offset], semaphores.at[offset]
        )
        for offset in range(count)
    ]
    for copy in reversed(copies):
        copy.start()
    for copy in reversed(copies):
        copy.wait()


def row_slices(place, by_rows):
    matrix_count, shard_count, height, width = by_rows.shape
    return pl.pallas_call(
        functools.partial(slices_kernel, shard_count),
        out_shape=[jax.ShapeDtypeStruct((matrix_count, height, width), by_rows.dtype)]
        * shard_count,
        in_specs=[
            pl.BlockSpec(memory_space=pltpu.SMEM),
            pl.BlockSpec(memory_space=pltpu.HBM),
        ],
        out_specs=[pl.BlockSpec(memory_space=pltpu.VMEM)] * shard_count,
        scratch_shapes=[pltpu.SemaphoreType.DMA((shard_count,))],
        compiler_params=pltpu.CompilerParams(vmem_limit_bytes=4 * MIB),
    )(place, by_rows)


def sum_kernel(shard_count, place_ref, *refs):
    parts = refs[:shard_count]
    vector_parts, momentum_ref, grad_ref, vector_ref, figures_ref = refs[shard_count:]
    vector = jnp.sum(vector_parts[...].astype(jnp.float32), axis=0)
    vector_ref[...] = vector
    total = folded(vector * vector) * (1.0 / shard_count)
    squares, crosses, momentum_squares = [], [], []
    for matrix in range(momentum_ref.shape[0]):
        grad = parts[0][matrix].astype(jnp.float32)
        for part in parts[1:]:
            grad = grad + part[matrix].astype(jnp.float32)
        grad_ref[matrix] = grad
        old = momentum_ref[matrix]
        squares.append(folded(grad * grad))
        crosses.append(folded(grad * old))
        momentum_squares.append(folded(old * old))
        total = total + squares[-1]
    lines = squares + crosses + momentum_squares + [total]
    lines = lines + [jnp.zeros_like(total)] * (FIGURES - len(lines))
    tile = jnp.concatenate(lines, axis=0)
    sums = jnp.sum(tile, axis=1, keepdims=True)
    line_index = lax.broadcasted_iota(jnp.int32, tile.shape, 0)
    lane_index = lax.broadcasted_iota(jnp.int32, tile.shape, 1)
    line = jnp.sum(jnp.where(line_index == lane_index, sums, 0.0), axis=0, keepdims=True)
    total_only = jnp.where(lane_index[:1] == 3 * momentum_ref.shape[0], line, 0.0)
    for section in range(figures_ref.shape[1]):
        chosen = jnp.where(place_ref[shard_count] == section, line, total_only)
        figures_ref[:, section] = jnp.broadcast_to(
            chosen[None], (figures_ref.shape[0],) + line.shape
        )


def scale_kernel(matrix_count, place_ref, figures_ref, grad_ref, momentum_ref, *refs):
    outputs = refs[:matrix_count]
    clip_ref = refs[matrix_count]
    line = jnp.sum(figures_ref[...], axis=0)
    line_index = lax.broadcasted_iota(jnp.int32, (FIGURES, LANES), 0)
    lane_index = lax.broadcasted_iota(jnp.int32, (FIGURES, LANES), 1)
    sums = jnp.sum(jnp.where(line_index == lane_index, line, 0.0), axis=1, keepdims=True)
    total = sums[3 * matrix_count : 3 * matrix_count + 1]
    clip = jnp.minimum(1.0, max_norm / (jnp.sqrt(total) + 1e-06))
    clip_ref[...] = jnp.broadcast_to(clip, clip_ref.shape)
    grad_scale = (1.0 + mom_beta) * clip
    momentum_scale = mom_beta * mom_beta
    update_norm = (
        grad_scale * grad_scale * sums[:matrix_count]
        + 2.0 * grad_scale * momentum_scale * sums[matrix_count : 2 * matrix_count]
        + momentum_scale * momentum_scale * sums[2 * matrix_count : 3 * matrix_count]
    )
    inverse = 1.0 / (jnp.sqrt(jnp.maximum(update_norm, 0.0)) + 1e-07)
    position = lax.broadcasted_iota(jnp.int32, inverse.shape, 0)
    for place in range(matrix_count):
        matrix = place_ref[place]
        factor = jnp.sum(jnp.where(position == matrix, inverse, 0.0), axis=0, keepdims=True)
        clipped = clip * grad_ref[matrix]
        new_momentum = mom_beta * momentum_ref[matrix] + clipped
        nesterov = clipped + mom_beta * new_momentum
        outputs[place][...] = (nesterov * factor).astype(jnp.bfloat16)


def end_kernel(offsets, place_ref, *refs):
    arrived = refs[: len(offsets)]
    weights_ref = refs[len(offsets)]
    update_ref, new_weights_ref, update_rows, weight_rows, semaphores = refs[-5:]
    step_size = muon_rate * (0.2 * math.sqrt(D))
    copies = []
    for slot, offset in enumerate(offsets):
        matrix = place_ref[offset]
        update = arrived[slot][...]
        update_rows[slot] = update
        weight_rows[slot] = (
            weights_ref[matrix].astype(jnp.float32) * (1.0 - muon_rate * muon_decay)
            - step_size * update.astype(jnp.float32)
        ).astype(jnp.bfloat16)
        for kind, (rows, target) in enumerate(
            ((update_rows, update_ref), (weight_rows, new_weights_ref))
        ):
            copies.append(
                pltpu.make_async_copy(
                    rows.at[slot], target.at[matrix], semaphores.at[2 * slot + kind]
                )
            )
            copies[-1].start()
    for copy in copies:
        copy.wait()


def finished(offsets, place, arrived, weights, partial=()):
    height, width = arrived[0].shape
    anywhere = pl.BlockSpec(memory_space=pltpu.HBM)
    return pl.pallas_call(
        functools.partial(end_kernel, offsets),
        out_shape=[jax.ShapeDtypeStruct(weights.shape, weights.dtype)] * 2,
        in_specs=[pl.BlockSpec(memory_space=pltpu.SMEM)]
        + [pl.BlockSpec(memory_space=pltpu.VMEM)] * (len(arrived) + 1)
        + [anywhere] * len(partial),
        out_specs=[anywhere] * 2,
        scratch_shapes=[
            pltpu.VMEM((len(offsets), height, width), weights.dtype),
            pltpu.VMEM((len(offsets), height, width), weights.dtype),
            pltpu.SemaphoreType.DMA((2 * len(offsets),)),
        ],
        input_output_aliases={len(arrived) + 2 + i: i for i in range(len(partial))},
        compiler_params=pltpu.CompilerParams(vmem_limit_bytes=8 * MIB),
    )(place, *arrived, weights, *partial)


def state_kernel(
    place_ref,
    clip_ref,
    grad_ref,
    momentum_ref,
    sums_ref,
    vectors_ref,
    first_ref,
    second_ref,
    new_momentum_ref,
    direction_ref,
    new_ref,
):
    new_momentum_ref[...] = mom_beta * momentum_ref[...] + clip_ref[0:1, 0:1] * grad_ref[...]
    width = vectors_ref.shape[1]
    count = sums_ref.shape[1] // width
    rows = sums_ref[:, :width]
    for position in range(1, count):
        part = sums_ref[:, position * width : (position + 1) * width]
        rows = jnp.where(place_ref[0] == position, part, rows)
    clipped = clip_ref[0:1, 0:1] * rows
    updated_first = 0.9 * first_ref[...] + 0.1 * clipped
    updated_second = 0.999 * second_ref[...] + 0.001 * clipped * clipped
    direction = updated_first / (jnp.sqrt(updated_second) + 1e-08)
    direction_ref[...] = direction
    new_ref[...] = vectors_ref[...] * (1.0 - adam_rate * adam_decay) - adam_rate * direction


def on_device(kernel, scalars, operands, out_shape):
    return pl.pallas_call(
        kernel,
        out_shape=out_shape,
        in_specs=[pl.BlockSpec(memory_space=pltpu.SMEM)]
        + [pl.BlockSpec(memory_space=pltpu.VMEM)] * len(operands),
        compiler_params=pltpu.CompilerParams(vmem_limit_bytes=16 * MIB),
    )(scalars, *operands)


def swapped(array, axis, offset):
    pairs = [(i, i ^ offset) for i in range(lax.axis_size(axis))]
    return lax.ppermute(array, axis, pairs)


def after(array, earlier):
    return lax.optimization_barrier((array, earlier))[0]


def per_device(grad_parts, vector_grads, momentum, weights, vectors, first_moment, second_moment):
    shard_count = lax.axis_size("shard")
    tensor_count = lax.axis_size("tensor")
    section_count = lax.axis_size("section")
    _, matrix_count, local_height, width = momentum.shape
    if shard_count != matrix_count or shard_count != 4 or tensor_count != 4:
        return general_device(
            grad_parts, vector_grads, momentum, weights, vectors, first_moment, second_moment
        )
    vector_count, vector_width = vectors.shape[1:]
    own_momentum = momentum[0]
    position = jnp.arange(shard_count + 1, dtype=jnp.int32)
    place = jnp.where(
        position == shard_count,
        lax.axis_index("section").astype(jnp.int32),
        lax.axis_index("shard").astype(jnp.int32) ^ position,
    )

    by_rows = grad_parts.reshape(matrix_count, shard_count, local_height, width)
    parts = list(row_slices(place, by_rows))
    for offset in reversed(range(1, shard_count)):
        parts[offset] = swapped(parts[offset], "shard", offset)
    vector_parts = lax.all_to_all(
        jnp.broadcast_to(vector_grads[0], (shard_count, vector_count, vector_width * shard_count)),
        "shard",
        split_axis=0,
        concat_axis=0,
        tiled=True,
    )

    others = shard_count * tensor_count
    grad_rows, vector_whole, figures = on_device(
        functools.partial(sum_kernel, shard_count),
        place,
        parts[::-1] + [vector_parts, own_momentum],
        [
            jax.ShapeDtypeStruct(own_momentum.shape, jnp.float32),
            jax.ShapeDtypeStruct(vector_parts.shape[1:], jnp.float32),
            jax.ShapeDtypeStruct((others, section_count, 1, LANES), jnp.float32),
        ],
    )
    figures = lax.all_to_all(
        figures.reshape(others * section_count, 1, LANES),
        MESH_AXES,
        split_axis=0,
        concat_axis=0,
        tiled=True,
    )
    *scaled, clip_tile = on_device(
        functools.partial(scale_kernel, matrix_count),
        place,
        [figures, grad_rows, own_momentum],
        [jax.ShapeDtypeStruct((local_height, width), jnp.bfloat16)] * matrix_count
        + [jax.ShapeDtypeStruct((8, LANES), jnp.float32)],
    )

    pieces = [scaled[0]] + [None] * 3
    for offset in (2, 1):
        pieces[offset] = swapped(scaled[offset], "shard", offset)
    near, side, far = [None] * 4, [None] * 4, [None] * 4
    near[0] = swapped(pieces[0], "tensor", 1)
    side[0] = swapped(pieces[0], "tensor", 2)
    far[0] = swapped(pieces[0], "tensor", 3)
    pieces[3] = swapped(after(scaled[3], near[0]), "shard", 3)
    near[1] = swapped(after(pieces[1], near[0]), "tensor", 1)
    side[1] = swapped(after(pieces[1], side[0]), "tensor", 2)
    far[1] = swapped(side[1], "tensor", 1)
    near[2] = swapped(after(pieces[2], far[0]), "tensor", 1)
    side[2] = swapped(after(pieces[2], far[0]), "tensor", 2)
    far[2] = swapped(near[2], "tensor", 2)
    near[3] = swapped(after(pieces[3], side[1]), "tensor", 1)
    side[3] = swapped(after(pieces[3], side[1]), "tensor", 2)
    far[3] = swapped(after(pieces[3], side[1]), "tensor", 3)
    results = orthogonalize([pieces, near, side, far])

    returned = {
        offset: swapped(results[offset], "shard", offset)
        for offset in reversed(range(1, shard_count))
    }
    early = finished((0,), place, [results[0]], weights[0])
    orthogonal_update, new_weights = finished(
        (3, 2, 1), place, [returned[offset] for offset in (3, 2, 1)], weights[0], early
    )
    new_momentum, adam_direction, new_vectors = on_device(
        state_kernel,
        place,
        [
            after(clip_tile, results[0]),
            grad_rows,
            own_momentum,
            vector_whole,
            vectors[0],
            first_moment[0],
            second_moment[0],
        ],
        [jax.ShapeDtypeStruct(own_momentum.shape, jnp.float32)]
        + [jax.ShapeDtypeStruct(vectors.shape[1:], jnp.float32)] * 2,
    )
    return (
        new_momentum[None],
        orthogonal_update[None],
        new_weights[None],
        adam_direction[None],
        new_vectors[None],
    )


def general_device(grad_parts, vector_grads, momentum, weights, vectors, first_moment, second_moment):
    shard_count = lax.axis_size("shard")
    tensor_count = lax.axis_size("tensor")
    section_count = lax.axis_size("section")
    shard_index = lax.axis_index("shard")
    _, matrix_count, local_height, width = momentum.shape
    vector_width = vectors.shape[2]
    own_momentum = momentum[0]

    rows = matrix_count * local_height
    by_target = (
        grad_parts.reshape(matrix_count, shard_count, local_height, width)
        .transpose(1, 0, 2, 3)
        .reshape(shard_count, rows, width)
    )
    vector_line = jnp.broadcast_to(
        vector_grads.reshape(1, 1, width), (shard_count, VECTOR_ROWS, width)
    )
    payload = jnp.concatenate([by_target, vector_line], axis=1)
    arrived = lax.all_to_all(payload, "shard", split_axis=0, concat_axis=0, tiled=True)
    grad_rows = jnp.sum(arrived[:, :rows].astype(jnp.float32), axis=0).reshape(
        matrix_count, local_height, width
    )
    vector_whole = jnp.sum(arrived[:, rows].astype(jnp.float32), axis=0).reshape(
        vectors.shape[1], vector_width * shard_count
    )
    vector_rows = lax.dynamic_slice_in_dim(
        vector_whole, shard_index * vector_width, vector_width, 1
    )

    grad_squares = jnp.sum(grad_rows * grad_rows, axis=(1, 2))
    cross = jnp.sum(grad_rows * own_momentum, axis=(1, 2))
    momentum_squares = jnp.sum(own_momentum * own_momentum, axis=(1, 2))
    own_total = jnp.sum(grad_squares) + jnp.sum(vector_rows * vector_rows)
    same_section = (
        jnp.arange(section_count) == lax.axis_index("section")
    ).astype(jnp.float32)[:, None]
    matrix_figures = jnp.concatenate([grad_squares, cross, momentum_squares])
    line = jnp.concatenate(
        [
            same_section * matrix_figures[None],
            jnp.broadcast_to(own_total, (section_count, 1)),
            jnp.zeros((section_count, 127 - 3 * matrix_count), jnp.float32),
        ],
        axis=1,
    )
    others = shard_count * tensor_count
    figures = jnp.broadcast_to(line[None, :, None, :], (others, section_count, 8, 128)).reshape(
        others * section_count, 8, 128
    )
    figures = lax.all_to_all(figures, MESH_AXES, split_axis=0, concat_axis=0, tiled=True)
    sums = jnp.sum(figures[:, 0, :], axis=0)
    grand_total = sums[3 * matrix_count]
    clip_factor = jnp.minimum(1.0, max_norm / (jnp.sqrt(grand_total) + 1e-06))
    grad_scale = (1.0 + mom_beta) * clip_factor
    momentum_scale = mom_beta * mom_beta
    update_norm = (
        grad_scale * grad_scale * sums[:matrix_count]
        + 2.0 * grad_scale * momentum_scale * sums[matrix_count : 2 * matrix_count]
        + momentum_scale * momentum_scale * sums[2 * matrix_count : 3 * matrix_count]
    )
    update_norm = jnp.maximum(update_norm, 0.0)[:, None, None]

    new_momentum = mom_beta * own_momentum + clip_factor * grad_rows
    nesterov = clip_factor * grad_rows + mom_beta * new_momentum
    scaled = (nesterov / (jnp.sqrt(update_norm) + 1e-07)).astype(jnp.bfloat16)

    owner_count = shard_count // matrix_count
    if owner_count == 1:
        row_block = lax.all_to_all(scaled, "shard", split_axis=0, concat_axis=0, tiled=True)
        row_block = row_block.reshape(shard_count * local_height, width)
    else:
        everything = lax.all_gather(scaled, "shard", axis=1, tiled=True)
        row_block = lax.dynamic_index_in_dim(
            everything, shard_index // owner_count, 0, keepdims=False
        )

    blocks = [row_block]
    for offset in range(1, tensor_count):
        pairs = [(i, i ^ offset) for i in range(tensor_count)]
        blocks.append(lax.ppermute(row_block, "tensor", pairs))
    (own_result,) = orthogonalize([[block] for block in blocks])

    if owner_count == 1:
        own_update = lax.all_to_all(
            own_result.reshape(shard_count, local_height, width),
            "shard",
            split_axis=0,
            concat_axis=0,
            tiled=True,
        )
    else:
        piece_length = local_height * width // owner_count
        split_rows = own_result.reshape(shard_count, owner_count, piece_length)
        returning = lax.dynamic_index_in_dim(
            split_rows, shard_index % owner_count, 1, keepdims=False
        )
        received = lax.all_to_all(returning, "shard", split_axis=0, concat_axis=0, tiled=True)
        own_update = received.reshape(matrix_count, local_height, width)
    orthogonal_update = own_update[None]
    muon_scale = 0.2 * math.sqrt(D)
    new_weights = (
        weights.astype(jnp.float32) * (1.0 - muon_rate * muon_decay)
        - muon_rate * muon_scale * orthogonal_update.astype(jnp.float32)
    ).astype(jnp.bfloat16)
    vector_clipped = clip_factor * vector_rows
    updated_first = 0.9 * first_moment + 0.1 * vector_clipped
    updated_second = 0.999 * second_moment + 0.001 * vector_clipped * vector_clipped
    adam_direction = updated_first / (jnp.sqrt(updated_second) + 1e-08)
    new_vectors = vectors * (1.0 - adam_rate * adam_decay) - adam_rate * adam_direction
    return (new_momentum[None], orthogonal_update, new_weights, adam_direction, new_vectors)


def solution(mesh):
    in_specs = (
        P("shard", "section", None, "tensor", None),
        P("shard", "section", None, "tensor"),
        P("section", None, ("tensor", "shard"), None),
        P("section", None, ("tensor", "shard"), None),
        P("section", None, ("tensor", "shard")),
        P("section", None, ("tensor", "shard")),
        P("section", None, ("tensor", "shard")),
    )
    out_specs = (
        P("section", None, ("tensor", "shard"), None),
        P("section", None, ("tensor", "shard"), None),
        P("section", None, ("tensor", "shard"), None),
        P("section", None, ("tensor", "shard")),
        P("section", None, ("tensor", "shard")),
    )
    return jax.shard_map(
        per_device, mesh=mesh, in_specs=in_specs, out_specs=out_specs, check_vma=False
    )
```

```python
import functools
import math

import jax
import jax.numpy as jnp
from jax import lax
from jax.experimental import pallas as pl
from jax.experimental.pallas import tpu as pltpu
from jax.sharding import PartitionSpec as P

D = 1024
NS_STEPS = 2


ns_first = 3.4445
ns_second = -4.775
ns_third = 2.0315
mom_beta = 0.95
max_norm = 1024.0
muon_rate = 0.02
muon_decay = 0.1
adam_rate = 0.001
adam_decay = 0.01

VECTOR_ROWS = 16
FIGURES = 16
MIB = 2**20
LANES = 128
MESH_AXES = ("shard", "tensor", "section")
TURNS = ((0, 2, 1, 3), (0, 1, 2, 3))


def gram_of(blocks, gram_ref):
    width = blocks[0].shape[1]
    step = 256
    for start in range(0, width, step):
        stop = start + step
        total = None
        for block in blocks:
            whole = block[...]
            product = lax.dot_general(
                whole[:, :stop],
                whole[:, start:stop],
                (((0,), (0,)), ((), ())),
                preferred_element_type=jnp.float32,
            )
            rounded = product.astype(jnp.bfloat16).astype(jnp.float32)
            total = rounded if total is None else total + rounded
        gram_ref[:stop, start:stop] = total.astype(jnp.bfloat16)
        for above in range(0, start, step):
            tile = gram_ref[above : above + step, start:stop]
            gram_ref[start:stop, above : above + step] = tile.T


def polynomial(block, gram_ref):
    gram = gram_ref[...]
    first = jnp.dot(block, gram, preferred_element_type=jnp.float32).astype(jnp.bfloat16)
    second = jnp.dot(first, gram, preferred_element_type=jnp.float32)
    combined = (
        ns_first * block.astype(jnp.float32)
        + ns_second * first.astype(jnp.float32)
        + ns_third * second
    )
    return combined.astype(jnp.bfloat16)


def orthogonalize_kernel(count, pieces, *refs):
    height, width = refs[0].shape
    inputs = refs[: count * pieces]
    outputs = refs[count * pieces : count * pieces + pieces]
    gram_ref, start_ref, next_ref = refs[count * pieces + pieces :]
    for position in range(count):
        for piece in range(pieces):
            start_ref[position, piece * height : (piece + 1) * height, :] = inputs[
                position * pieces + piece
            ][...]
    current, other = start_ref, next_ref
    for iteration in range(NS_STEPS - 1):
        gram_of([current.at[position] for position in range(count)], gram_ref)
        for position in range(count):
            other[position] = polynomial(current[position], gram_ref)
        current, other = other, current
    gram_of([current.at[position] for position in range(count)], gram_ref)
    result = polynomial(current[0], gram_ref)
    for piece in range(pieces):
        outputs[piece][...] = result[piece * height : (piece + 1) * height, :]


def orthogonalize(blocks):
    count, pieces = len(blocks), len(blocks[0])
    height, width = blocks[0][0].shape
    return pl.pallas_call(
        functools.partial(orthogonalize_kernel, count, pieces),
        out_shape=[jax.ShapeDtypeStruct((height, width), jnp.bfloat16)] * pieces,
        scratch_shapes=[
            pltpu.VMEM((width, width), jnp.bfloat16),
            pltpu.VMEM((count, pieces * height, width), jnp.bfloat16),
            pltpu.VMEM((count, pieces * height, width), jnp.bfloat16),
        ],
        compiler_params=pltpu.CompilerParams(vmem_limit_bytes=32 * MIB),
    )(*[piece for block in blocks for piece in block])


def folded(array):
    line = jnp.sum(array, axis=0, keepdims=True)
    total = line[:, :LANES]
    for start in range(LANES, line.shape[1], LANES):
        total = total + line[:, start : start + LANES]
    return total


def slices_kernel(count, place_ref, grad_ref, *refs):
    outputs, semaphores = refs[:count], refs[count]
    copies = [
        pltpu.make_async_copy(
            grad_ref.at[:, place_ref[offset]], outputs[offset], semaphores.at[offset]
        )
        for offset in range(count)
    ]
    for copy in reversed(copies):
        copy.start()
    for copy in reversed(copies):
        copy.wait()


def row_slices(place, by_rows):
    matrix_count, shard_count, height, width = by_rows.shape
    return pl.pallas_call(
        functools.partial(slices_kernel, shard_count),
        out_shape=[jax.ShapeDtypeStruct((matrix_count, height, width), by_rows.dtype)]
        * shard_count,
        in_specs=[
            pl.BlockSpec(memory_space=pltpu.SMEM),
            pl.BlockSpec(memory_space=pltpu.HBM),
        ],
        out_specs=[pl.BlockSpec(memory_space=pltpu.VMEM)] * shard_count,
        scratch_shapes=[pltpu.SemaphoreType.DMA((shard_count,))],
        compiler_params=pltpu.CompilerParams(vmem_limit_bytes=4 * MIB),
    )(place, by_rows)


def sum_kernel(shard_count, place_ref, *refs):
    parts = refs[:shard_count]
    vector_parts, momentum_ref, grad_ref, vector_ref, figures_ref = refs[shard_count:]
    vector = jnp.sum(vector_parts[...].astype(jnp.float32), axis=0)
    vector_ref[...] = vector
    total = folded(vector * vector) * (1.0 / shard_count)
    squares, crosses, momentum_squares = [], [], []
    for matrix in range(momentum_ref.shape[0]):
        grad = parts[0][matrix].astype(jnp.float32)
        for part in parts[1:]:
            grad = grad + part[matrix].astype(jnp.float32)
        grad_ref[matrix] = grad
        old = momentum_ref[matrix]
        squares.append(folded(grad * grad))
        crosses.append(folded(grad * old))
        momentum_squares.append(folded(old * old))
        total = total + squares[-1]
    lines = squares + crosses + momentum_squares + [total]
    lines = lines + [jnp.zeros_like(total)] * (FIGURES - len(lines))
    tile = jnp.concatenate(lines, axis=0)
    sums = jnp.sum(tile, axis=1, keepdims=True)
    line_index = lax.broadcasted_iota(jnp.int32, tile.shape, 0)
    lane_index = lax.broadcasted_iota(jnp.int32, tile.shape, 1)
    line = jnp.sum(jnp.where(line_index == lane_index, sums, 0.0), axis=0, keepdims=True)
    total_only = jnp.where(lane_index[:1] == 3 * momentum_ref.shape[0], line, 0.0)
    for section in range(figures_ref.shape[1]):
        chosen = jnp.where(place_ref[shard_count] == section, line, total_only)
        figures_ref[:, section] = jnp.broadcast_to(
            chosen[None], (figures_ref.shape[0],) + line.shape
        )


def scale_kernel(matrix_count, place_ref, figures_ref, grad_ref, momentum_ref, *refs):
    outputs = refs[:matrix_count]
    clip_ref = refs[matrix_count]
    line = jnp.sum(figures_ref[...], axis=0)
    line_index = lax.broadcasted_iota(jnp.int32, (FIGURES, LANES), 0)
    lane_index = lax.broadcasted_iota(jnp.int32, (FIGURES, LANES), 1)
    sums = jnp.sum(jnp.where(line_index == lane_index, line, 0.0), axis=1, keepdims=True)
    total = sums[3 * matrix_count : 3 * matrix_count + 1]
    clip = jnp.minimum(1.0, max_norm / (jnp.sqrt(total) + 1e-06))
    clip_ref[...] = jnp.broadcast_to(clip, clip_ref.shape)
    grad_scale = (1.0 + mom_beta) * clip
    momentum_scale = mom_beta * mom_beta
    update_norm = (
        grad_scale * grad_scale * sums[:matrix_count]
        + 2.0 * grad_scale * momentum_scale * sums[matrix_count : 2 * matrix_count]
        + momentum_scale * momentum_scale * sums[2 * matrix_count : 3 * matrix_count]
    )
    inverse = 1.0 / (jnp.sqrt(jnp.maximum(update_norm, 0.0)) + 1e-07)
    position = lax.broadcasted_iota(jnp.int32, inverse.shape, 0)
    for place in range(matrix_count):
        matrix = place_ref[matrix_count + 1 + place]
        factor = jnp.sum(jnp.where(position == matrix, inverse, 0.0), axis=0, keepdims=True)
        clipped = clip * grad_ref[matrix]
        new_momentum = mom_beta * momentum_ref[matrix] + clipped
        nesterov = clipped + mom_beta * new_momentum
        outputs[place][...] = (nesterov * factor).astype(jnp.bfloat16)


def end_kernel(offsets, place_ref, *refs):
    arrived = refs[: len(offsets)]
    weights_ref = refs[len(offsets)]
    update_ref, new_weights_ref, update_rows, weight_rows, semaphores = refs[-5:]
    step_size = muon_rate * (0.2 * math.sqrt(D))
    copies = []
    for slot, offset in enumerate(offsets):
        matrix = place_ref[weights_ref.shape[0] + 1 + offset]
        update = arrived[slot][...]
        update_rows[slot] = update
        weight_rows[slot] = (
            weights_ref[matrix].astype(jnp.float32) * (1.0 - muon_rate * muon_decay)
            - step_size * update.astype(jnp.float32)
        ).astype(jnp.bfloat16)
        for kind, (rows, target) in enumerate(
            ((update_rows, update_ref), (weight_rows, new_weights_ref))
        ):
            copies.append(
                pltpu.make_async_copy(
                    rows.at[slot], target.at[matrix], semaphores.at[2 * slot + kind]
                )
            )
            copies[-1].start()
    for copy in copies:
        copy.wait()


def finished(offsets, place, arrived, weights, partial=()):
    height, width = arrived[0].shape
    anywhere = pl.BlockSpec(memory_space=pltpu.HBM)
    return pl.pallas_call(
        functools.partial(end_kernel, offsets),
        out_shape=[jax.ShapeDtypeStruct(weights.shape, weights.dtype)] * 2,
        in_specs=[pl.BlockSpec(memory_space=pltpu.SMEM)]
        + [pl.BlockSpec(memory_space=pltpu.VMEM)] * (len(arrived) + 1)
        + [anywhere] * len(partial),
        out_specs=[anywhere] * 2,
        scratch_shapes=[
            pltpu.VMEM((len(offsets), height, width), weights.dtype),
            pltpu.VMEM((len(offsets), height, width), weights.dtype),
            pltpu.SemaphoreType.DMA((2 * len(offsets),)),
        ],
        input_output_aliases={len(arrived) + 2 + i: i for i in range(len(partial))},
        compiler_params=pltpu.CompilerParams(vmem_limit_bytes=8 * MIB),
    )(place, *arrived, weights, *partial)


def state_kernel(
    place_ref,
    clip_ref,
    grad_ref,
    momentum_ref,
    sums_ref,
    vectors_ref,
    first_ref,
    second_ref,
    new_momentum_ref,
    direction_ref,
    new_ref,
):
    new_momentum_ref[...] = mom_beta * momentum_ref[...] + clip_ref[0:1, 0:1] * grad_ref[...]
    width = vectors_ref.shape[1]
    count = sums_ref.shape[1] // width
    rows = sums_ref[:, :width]
    for position in range(1, count):
        part = sums_ref[:, position * width : (position + 1) * width]
        rows = jnp.where(place_ref[0] == position, part, rows)
    clipped = clip_ref[0:1, 0:1] * rows
    updated_first = 0.9 * first_ref[...] + 0.1 * clipped
    updated_second = 0.999 * second_ref[...] + 0.001 * clipped * clipped
    direction = updated_first / (jnp.sqrt(updated_second) + 1e-08)
    direction_ref[...] = direction
    new_ref[...] = vectors_ref[...] * (1.0 - adam_rate * adam_decay) - adam_rate * direction


def on_device(kernel, scalars, operands, out_shape):
    return pl.pallas_call(
        kernel,
        out_shape=out_shape,
        in_specs=[pl.BlockSpec(memory_space=pltpu.SMEM)]
        + [pl.BlockSpec(memory_space=pltpu.VMEM)] * len(operands),
        compiler_params=pltpu.CompilerParams(vmem_limit_bytes=16 * MIB),
    )(scalars, *operands)


def swapped(array, axis, offset):
    pairs = [(i, i ^ offset) for i in range(lax.axis_size(axis))]
    return lax.ppermute(array, axis, pairs)


def traded(array, slot):
    sections = lax.axis_size("section")
    pairs = [
        (shard * sections + section, (shard ^ TURNS[section % 2][slot]) * sections + section)
        for shard in range(lax.axis_size("shard"))
        for section in range(sections)
    ]
    return lax.ppermute(array, ("shard", "section"), pairs)


def after(array, earlier):
    return lax.optimization_barrier((array, earlier))[0]


def per_device(grad_parts, vector_grads, momentum, weights, vectors, first_moment, second_moment):
    shard_count = lax.axis_size("shard")
    tensor_count = lax.axis_size("tensor")
    section_count = lax.axis_size("section")
    _, matrix_count, local_height, width = momentum.shape
    if shard_count != matrix_count or shard_count != 4 or tensor_count != 4:
        return general_device(
            grad_parts, vector_grads, momentum, weights, vectors, first_moment, second_moment
        )
    vector_count, vector_width = vectors.shape[1:]
    own_momentum = momentum[0]
    position = jnp.arange(2 * shard_count + 1, dtype=jnp.int32)
    section_index = lax.axis_index("section").astype(jnp.int32)
    slot = position - shard_count - 1
    swap = (slot == 1) | (slot == 2)
    offset = jnp.where(swap & (section_index % 2 == 0), 3 - slot, slot)
    place = jnp.where(
        position == shard_count,
        section_index,
        lax.axis_index("shard").astype(jnp.int32)
        ^ jnp.where(position < shard_count, position, offset),
    )

    by_rows = grad_parts.reshape(matrix_count, shard_count, local_height, width)
    parts = list(row_slices(place, by_rows))
    for offset in reversed(range(1, shard_count)):
        parts[offset] = swapped(parts[offset], "shard", offset)
    vector_parts = lax.all_to_all(
        jnp.broadcast_to(vector_grads[0], (shard_count, vector_count, vector_width * shard_count)),
        "shard",
        split_axis=0,
        concat_axis=0,
        tiled=True,
    )

    others = shard_count * tensor_count
    grad_rows, vector_whole, figures = on_device(
        functools.partial(sum_kernel, shard_count),
        place,
        parts[::-1] + [vector_parts, own_momentum],
        [
            jax.ShapeDtypeStruct(own_momentum.shape, jnp.float32),
            jax.ShapeDtypeStruct(vector_parts.shape[1:], jnp.float32),
            jax.ShapeDtypeStruct((others, section_count, 1, LANES), jnp.float32),
        ],
    )
    figures = lax.all_to_all(
        figures.reshape(others * section_count, 1, LANES),
        MESH_AXES,
        split_axis=0,
        concat_axis=0,
        tiled=True,
    )
    *scaled, clip_tile = on_device(
        functools.partial(scale_kernel, matrix_count),
        place,
        [figures, grad_rows, own_momentum],
        [jax.ShapeDtypeStruct((local_height, width), jnp.bfloat16)] * matrix_count
        + [jax.ShapeDtypeStruct((8, LANES), jnp.float32)],
    )

    pieces = [scaled[0]] + [None] * 3
    pieces[1] = traded(scaled[1], 1)
    near, side, far = [None] * 4, [None] * 4, [None] * 4
    near[0] = swapped(pieces[0], "tensor", 1)
    side[0] = swapped(pieces[0], "tensor", 2)
    far[0] = swapped(pieces[0], "tensor", 3)
    pieces[2] = traded(after(scaled[2], pieces[1]), 2)
    pieces[3] = traded(after(scaled[3], side[0]), 3)
    near[1] = swapped(after(pieces[1], near[0]), "tensor", 1)
    side[1] = swapped(after(pieces[1], side[0]), "tensor", 2)
    far[1] = swapped(side[1], "tensor", 1)
    near[2] = swapped(pieces[2], "tensor", 1)
    side[2] = swapped(after(pieces[2], near[1]), "tensor", 2)
    far[2] = swapped(near[2], "tensor", 2)
    near[3] = swapped(after(pieces[3], (side[1], near[1])), "tensor", 1)
    side[3] = swapped(after(pieces[3], (side[1], near[1])), "tensor", 2)
    far[3] = swapped(after(pieces[3], (side[1], near[1])), "tensor", 3)
    results = orthogonalize([pieces, near, side, far])

    returned = {
        offset: traded(results[offset], offset)
        for offset in reversed(range(1, shard_count))
    }
    early = finished((0,), place, [results[0]], weights[0])
    orthogonal_update, new_weights = finished(
        (3, 2, 1), place, [returned[offset] for offset in (3, 2, 1)], weights[0], early
    )
    new_momentum, adam_direction, new_vectors = on_device(
        state_kernel,
        place,
        [
            after(clip_tile, results[0]),
            grad_rows,
            own_momentum,
            vector_whole,
            vectors[0],
            first_moment[0],
            second_moment[0],
        ],
        [jax.ShapeDtypeStruct(own_momentum.shape, jnp.float32)]
        + [jax.ShapeDtypeStruct(vectors.shape[1:], jnp.float32)] * 2,
    )
    return (
        new_momentum[None],
        orthogonal_update[None],
        new_weights[None],
        adam_direction[None],
        new_vectors[None],
    )


def general_device(grad_parts, vector_grads, momentum, weights, vectors, first_moment, second_moment):
    shard_count = lax.axis_size("shard")
    tensor_count = lax.axis_size("tensor")
    section_count = lax.axis_size("section")
    shard_index = lax.axis_index("shard")
    _, matrix_count, local_height, width = momentum.shape
    vector_width = vectors.shape[2]
    own_momentum = momentum[0]

    rows = matrix_count * local_height
    by_target = (
        grad_parts.reshape(matrix_count, shard_count, local_height, width)
        .transpose(1, 0, 2, 3)
        .reshape(shard_count, rows, width)
    )
    vector_line = jnp.broadcast_to(
        vector_grads.reshape(1, 1, width), (shard_count, VECTOR_ROWS, width)
    )
    payload = jnp.concatenate([by_target, vector_line], axis=1)
    arrived = lax.all_to_all(payload, "shard", split_axis=0, concat_axis=0, tiled=True)
    grad_rows = jnp.sum(arrived[:, :rows].astype(jnp.float32), axis=0).reshape(
        matrix_count, local_height, width
    )
    vector_whole = jnp.sum(arrived[:, rows].astype(jnp.float32), axis=0).reshape(
        vectors.shape[1], vector_width * shard_count
    )
    vector_rows = lax.dynamic_slice_in_dim(
        vector_whole, shard_index * vector_width, vector_width, 1
    )

    grad_squares = jnp.sum(grad_rows * grad_rows, axis=(1, 2))
    cross = jnp.sum(grad_rows * own_momentum, axis=(1, 2))
    momentum_squares = jnp.sum(own_momentum * own_momentum, axis=(1, 2))
    own_total = jnp.sum(grad_squares) + jnp.sum(vector_rows * vector_rows)
    same_section = (
        jnp.arange(section_count) == lax.axis_index("section")
    ).astype(jnp.float32)[:, None]
    matrix_figures = jnp.concatenate([grad_squares, cross, momentum_squares])
    line = jnp.concatenate(
        [
            same_section * matrix_figures[None],
            jnp.broadcast_to(own_total, (section_count, 1)),
            jnp.zeros((section_count, 127 - 3 * matrix_count), jnp.float32),
        ],
        axis=1,
    )
    others = shard_count * tensor_count
    figures = jnp.broadcast_to(line[None, :, None, :], (others, section_count, 8, 128)).reshape(
        others * section_count, 8, 128
    )
    figures = lax.all_to_all(figures, MESH_AXES, split_axis=0, concat_axis=0, tiled=True)
    sums = jnp.sum(figures[:, 0, :], axis=0)
    grand_total = sums[3 * matrix_count]
    clip_factor = jnp.minimum(1.0, max_norm / (jnp.sqrt(grand_total) + 1e-06))
    grad_scale = (1.0 + mom_beta) * clip_factor
    momentum_scale = mom_beta * mom_beta
    update_norm = (
        grad_scale * grad_scale * sums[:matrix_count]
        + 2.0 * grad_scale * momentum_scale * sums[matrix_count : 2 * matrix_count]
        + momentum_scale * momentum_scale * sums[2 * matrix_count : 3 * matrix_count]
    )
    update_norm = jnp.maximum(update_norm, 0.0)[:, None, None]

    new_momentum = mom_beta * own_momentum + clip_factor * grad_rows
    nesterov = clip_factor * grad_rows + mom_beta * new_momentum
    scaled = (nesterov / (jnp.sqrt(update_norm) + 1e-07)).astype(jnp.bfloat16)

    owner_count = shard_count // matrix_count
    if owner_count == 1:
        row_block = lax.all_to_all(scaled, "shard", split_axis=0, concat_axis=0, tiled=True)
        row_block = row_block.reshape(shard_count * local_height, width)
    else:
        everything = lax.all_gather(scaled, "shard", axis=1, tiled=True)
        row_block = lax.dynamic_index_in_dim(
            everything, shard_index // owner_count, 0, keepdims=False
        )

    blocks = [row_block]
    for offset in range(1, tensor_count):
        pairs = [(i, i ^ offset) for i in range(tensor_count)]
        blocks.append(lax.ppermute(row_block, "tensor", pairs))
    (own_result,) = orthogonalize([[block] for block in blocks])

    if owner_count == 1:
        own_update = lax.all_to_all(
            own_result.reshape(shard_count, local_height, width),
            "shard",
            split_axis=0,
            concat_axis=0,
            tiled=True,
        )
    else:
        piece_length = local_height * width // owner_count
        split_rows = own_result.reshape(shard_count, owner_count, piece_length)
        returning = lax.dynamic_index_in_dim(
            split_rows, shard_index % owner_count, 1, keepdims=False
        )
        received = lax.all_to_all(returning, "shard", split_axis=0, concat_axis=0, tiled=True)
        own_update = received.reshape(matrix_count, local_height, width)
    orthogonal_update = own_update[None]
    muon_scale = 0.2 * math.sqrt(D)
    new_weights = (
        weights.astype(jnp.float32) * (1.0 - muon_rate * muon_decay)
        - muon_rate * muon_scale * orthogonal_update.astype(jnp.float32)
    ).astype(jnp.bfloat16)
    vector_clipped = clip_factor * vector_rows
    updated_first = 0.9 * first_moment + 0.1 * vector_clipped
    updated_second = 0.999 * second_moment + 0.001 * vector_clipped * vector_clipped
    adam_direction = updated_first / (jnp.sqrt(updated_second) + 1e-08)
    new_vectors = vectors * (1.0 - adam_rate * adam_decay) - adam_rate * adam_direction
    return (new_momentum[None], orthogonal_update, new_weights, adam_direction, new_vectors)


def solution(mesh):
    in_specs = (
        P("shard", "section", None, "tensor", None),
        P("shard", "section", None, "tensor"),
        P("section", None, ("tensor", "shard"), None),
        P("section", None, ("tensor", "shard"), None),
        P("section", None, ("tensor", "shard")),
        P("section", None, ("tensor", "shard")),
        P("section", None, ("tensor", "shard")),
    )
    out_specs = (
        P("section", None, ("tensor", "shard"), None),
        P("section", None, ("tensor", "shard"), None),
        P("section", None, ("tensor", "shard"), None),
        P("section", None, ("tensor", "shard")),
        P("section", None, ("tensor", "shard")),
    )
    return jax.shard_map(
        per_device, mesh=mesh, in_specs=in_specs, out_specs=out_specs, check_vma=False
    )
```

```python
import functools
import math

import jax
import jax.numpy as jnp
from jax import lax
from jax.experimental import pallas as pl
from jax.experimental.pallas import tpu as pltpu
from jax.sharding import PartitionSpec as P

D = 1024
NS_STEPS = 2


ns_first = 3.4445
ns_second = -4.775
ns_third = 2.0315
mom_beta = 0.95
max_norm = 1024.0
muon_rate = 0.02
muon_decay = 0.1
adam_rate = 0.001
adam_decay = 0.01

VECTOR_ROWS = 16
FIGURES = 16
MIB = 2**20
LANES = 128
MESH_AXES = ("shard", "tensor", "section")


def gram_of(blocks, gram_ref):
    width = blocks[0].shape[1]
    step = 256
    for start in range(0, width, step):
        stop = start + step
        total = None
        for block in blocks:
            whole = block[...]
            product = lax.dot_general(
                whole[:, :stop],
                whole[:, start:stop],
                (((0,), (0,)), ((), ())),
                preferred_element_type=jnp.float32,
            )
            rounded = product.astype(jnp.bfloat16).astype(jnp.float32)
            total = rounded if total is None else total + rounded
        gram_ref[:stop, start:stop] = total.astype(jnp.bfloat16)
        for above in range(0, start, step):
            tile = gram_ref[above : above + step, start:stop]
            gram_ref[start:stop, above : above + step] = tile.T


def polynomial(block, gram_ref):
    gram = gram_ref[...]
    first = jnp.dot(block, gram, preferred_element_type=jnp.float32).astype(jnp.bfloat16)
    second = jnp.dot(first, gram, preferred_element_type=jnp.float32)
    combined = (
        ns_first * block.astype(jnp.float32)
        + ns_second * first.astype(jnp.float32)
        + ns_third * second
    )
    return combined.astype(jnp.bfloat16)


def orthogonalize_kernel(count, pieces, *refs):
    height, width = refs[0].shape
    inputs = refs[: count * pieces]
    outputs = refs[count * pieces : count * pieces + pieces]
    gram_ref, start_ref, next_ref = refs[count * pieces + pieces :]
    block = pieces * height
    rows = count * block
    chunk = 2 * block if count % 2 == 0 else block
    for position, piece_ref in enumerate(inputs):
        start_ref[position * height : (position + 1) * height, :] = piece_ref[...]
    current, other = start_ref, next_ref
    for iteration in range(NS_STEPS):
        gram_of([current.at[start : start + block] for start in range(0, rows, block)], gram_ref)
        if iteration + 1 < NS_STEPS:
            for start in range(0, rows, chunk):
                other[start : start + chunk, :] = polynomial(
                    current[start : start + chunk, :], gram_ref
                )
            current, other = other, current
    result = polynomial(current[:block, :], gram_ref)
    for piece in range(pieces):
        outputs[piece][...] = result[piece * height : (piece + 1) * height, :]


def orthogonalize(blocks):
    count, pieces = len(blocks), len(blocks[0])
    height, width = blocks[0][0].shape
    return pl.pallas_call(
        functools.partial(orthogonalize_kernel, count, pieces),
        out_shape=[jax.ShapeDtypeStruct((height, width), jnp.bfloat16)] * pieces,
        scratch_shapes=[
            pltpu.VMEM((width, width), jnp.bfloat16),
            pltpu.VMEM((count * pieces * height, width), jnp.bfloat16),
            pltpu.VMEM((count * pieces * height, width), jnp.bfloat16),
        ],
        compiler_params=pltpu.CompilerParams(vmem_limit_bytes=32 * MIB),
    )(*[piece for block in blocks for piece in block])


def folded(array):
    line = jnp.sum(array, axis=0, keepdims=True)
    total = line[:, :LANES]
    for start in range(LANES, line.shape[1], LANES):
        total = total + line[:, start : start + LANES]
    return total


def slices_kernel(count, place_ref, grad_ref, *refs):
    outputs, semaphores = refs[:count], refs[count]
    copies = [
        pltpu.make_async_copy(
            grad_ref.at[:, place_ref[offset]], outputs[offset], semaphores.at[offset]
        )
        for offset in range(count)
    ]
    for copy in reversed(copies):
        copy.start()
    for copy in reversed(copies):
        copy.wait()


def row_slices(place, by_rows):
    matrix_count, shard_count, height, width = by_rows.shape
    return pl.pallas_call(
        functools.partial(slices_kernel, shard_count),
        out_shape=[pltpu.VMEM((matrix_count, height, width), by_rows.dtype)] * shard_count,
        in_specs=[
            pl.BlockSpec(memory_space=pltpu.SMEM),
            pl.BlockSpec(memory_space=pltpu.HBM),
        ],
        out_specs=[pl.BlockSpec(memory_space=pltpu.VMEM)] * shard_count,
        scratch_shapes=[pltpu.SemaphoreType.DMA((shard_count,))],
        compiler_params=pltpu.CompilerParams(vmem_limit_bytes=60 * MIB),
    )(place, by_rows)


def sum_kernel(shard_count, place_ref, *refs):
    parts = refs[:shard_count]
    vector_parts, momentum_ref, grad_ref, vector_ref, figures_ref = refs[shard_count:]
    vector = jnp.sum(vector_parts[...].astype(jnp.float32), axis=0)
    vector_ref[...] = vector
    total = folded(vector * vector) * (1.0 / shard_count)
    squares, crosses, momentum_squares = [], [], []
    for matrix in range(momentum_ref.shape[0]):
        grad = parts[0][matrix].astype(jnp.float32)
        for part in parts[1:]:
            grad = grad + part[matrix].astype(jnp.float32)
        grad_ref[matrix] = grad
        old = momentum_ref[matrix]
        squares.append(folded(grad * grad))
        crosses.append(folded(grad * old))
        momentum_squares.append(folded(old * old))
        total = total + squares[-1]
    lines = squares + crosses + momentum_squares + [total]
    lines = lines + [jnp.zeros_like(total)] * (FIGURES - len(lines))
    tile = jnp.concatenate(lines, axis=0)
    sums = jnp.sum(tile, axis=1, keepdims=True)
    line_index = lax.broadcasted_iota(jnp.int32, tile.shape, 0)
    lane_index = lax.broadcasted_iota(jnp.int32, tile.shape, 1)
    line = jnp.sum(jnp.where(line_index == lane_index, sums, 0.0), axis=0, keepdims=True)
    total_only = jnp.where(lane_index[:1] == 3 * momentum_ref.shape[0], line, 0.0)
    for section in range(figures_ref.shape[1]):
        chosen = jnp.where(place_ref[shard_count] == section, line, total_only)
        figures_ref[:, section] = jnp.broadcast_to(
            chosen[None], (figures_ref.shape[0],) + line.shape
        )


def scale_kernel(matrix_count, place_ref, figures_ref, grad_ref, momentum_ref, *refs):
    outputs = refs[:matrix_count]
    clip_ref = refs[matrix_count]
    line = jnp.sum(figures_ref[...], axis=0)
    line_index = lax.broadcasted_iota(jnp.int32, (FIGURES, LANES), 0)
    lane_index = lax.broadcasted_iota(jnp.int32, (FIGURES, LANES), 1)
    sums = jnp.sum(jnp.where(line_index == lane_index, line, 0.0), axis=1, keepdims=True)
    total = sums[3 * matrix_count : 3 * matrix_count + 1]
    clip = jnp.minimum(1.0, max_norm / (jnp.sqrt(total) + 1e-06))
    clip_ref[...] = jnp.broadcast_to(clip, clip_ref.shape)
    grad_scale = (1.0 + mom_beta) * clip
    momentum_scale = mom_beta * mom_beta
    update_norm = (
        grad_scale * grad_scale * sums[:matrix_count]
        + 2.0 * grad_scale * momentum_scale * sums[matrix_count : 2 * matrix_count]
        + momentum_scale * momentum_scale * sums[2 * matrix_count : 3 * matrix_count]
    )
    inverse = 1.0 / (jnp.sqrt(jnp.maximum(update_norm, 0.0)) + 1e-07)
    position = lax.broadcasted_iota(jnp.int32, inverse.shape, 0)
    for place in range(matrix_count):
        matrix = place_ref[place]
        factor = jnp.sum(jnp.where(position == matrix, inverse, 0.0), axis=0, keepdims=True)
        clipped = clip * grad_ref[matrix]
        new_momentum = mom_beta * momentum_ref[matrix] + clipped
        nesterov = clipped + mom_beta * new_momentum
        outputs[place][...] = (nesterov * factor).astype(jnp.bfloat16)


def end_kernel(offsets, place_ref, *refs):
    arrived = refs[: len(offsets)]
    weights_ref = refs[len(offsets)]
    update_ref, new_weights_ref, update_rows, weight_rows, semaphores = refs[-5:]
    step_size = muon_rate * (0.2 * math.sqrt(D))
    copies = []
    for slot, offset in enumerate(offsets):
        matrix = place_ref[offset]
        update = arrived[slot][...]
        update_rows[slot] = update
        weight_rows[slot] = (
            weights_ref[matrix].astype(jnp.float32) * (1.0 - muon_rate * muon_decay)
            - step_size * update.astype(jnp.float32)
        ).astype(jnp.bfloat16)
        for kind, (rows, target) in enumerate(
            ((update_rows, update_ref), (weight_rows, new_weights_ref))
        ):
            copies.append(
                pltpu.make_async_copy(
                    rows.at[slot], target.at[matrix], semaphores.at[2 * slot + kind]
                )
            )
            copies[-1].start()
    for copy in copies:
        copy.wait()


def finished(offsets, place, arrived, weights, partial=()):
    height, width = arrived[0].shape
    anywhere = pl.BlockSpec(memory_space=pltpu.HBM)
    return pl.pallas_call(
        functools.partial(end_kernel, offsets),
        out_shape=[jax.ShapeDtypeStruct(weights.shape, weights.dtype)] * 2,
        in_specs=[pl.BlockSpec(memory_space=pltpu.SMEM)]
        + [pl.BlockSpec(memory_space=pltpu.VMEM)] * (len(arrived) + 1)
        + [anywhere] * len(partial),
        out_specs=[anywhere] * 2,
        scratch_shapes=[
            pltpu.VMEM((len(offsets), height, width), weights.dtype),
            pltpu.VMEM((len(offsets), height, width), weights.dtype),
            pltpu.SemaphoreType.DMA((2 * len(offsets),)),
        ],
        input_output_aliases={len(arrived) + 2 + i: i for i in range(len(partial))},
        compiler_params=pltpu.CompilerParams(vmem_limit_bytes=8 * MIB),
    )(place, *arrived, weights, *partial)


def state_kernel(
    place_ref,
    clip_ref,
    grad_ref,
    momentum_ref,
    sums_ref,
    vectors_ref,
    first_ref,
    second_ref,
    new_momentum_ref,
    direction_ref,
    new_ref,
):
    new_momentum_ref[...] = mom_beta * momentum_ref[...] + clip_ref[0:1, 0:1] * grad_ref[...]
    width = vectors_ref.shape[1]
    count = sums_ref.shape[1] // width
    rows = sums_ref[:, :width]
    for position in range(1, count):
        part = sums_ref[:, position * width : (position + 1) * width]
        rows = jnp.where(place_ref[0] == position, part, rows)
    clipped = clip_ref[0:1, 0:1] * rows
    updated_first = 0.9 * first_ref[...] + 0.1 * clipped
    updated_second = 0.999 * second_ref[...] + 0.001 * clipped * clipped
    direction = updated_first / (jnp.sqrt(updated_second) + 1e-08)
    direction_ref[...] = direction
    new_ref[...] = vectors_ref[...] * (1.0 - adam_rate * adam_decay) - adam_rate * direction


def on_device(kernel, scalars, operands, out_shape):
    return pl.pallas_call(
        kernel,
        out_shape=out_shape,
        in_specs=[pl.BlockSpec(memory_space=pltpu.SMEM)]
        + [pl.BlockSpec(memory_space=pltpu.VMEM)] * len(operands),
        compiler_params=pltpu.CompilerParams(vmem_limit_bytes=16 * MIB),
    )(scalars, *operands)


def swapped(array, axis, offset):
    pairs = [(i, i ^ offset) for i in range(lax.axis_size(axis))]
    return lax.ppermute(array, axis, pairs)


def after(array, earlier):
    return lax.optimization_barrier((array, earlier))[0]


def per_device(grad_parts, vector_grads, momentum, weights, vectors, first_moment, second_moment):
    shard_count = lax.axis_size("shard")
    tensor_count = lax.axis_size("tensor")
    section_count = lax.axis_size("section")
    _, matrix_count, local_height, width = momentum.shape
    if shard_count != matrix_count or shard_count != 4 or tensor_count != 4:
        return general_device(
            grad_parts, vector_grads, momentum, weights, vectors, first_moment, second_moment
        )
    vector_count, vector_width = vectors.shape[1:]
    own_momentum = momentum[0]
    position = jnp.arange(shard_count + 1, dtype=jnp.int32)
    place = jnp.where(
        position == shard_count,
        lax.axis_index("section").astype(jnp.int32),
        lax.axis_index("shard").astype(jnp.int32) ^ position,
    )

    by_rows = grad_parts.reshape(matrix_count, shard_count, local_height, width)
    parts = list(row_slices(place, by_rows))
    for offset in reversed(range(1, shard_count)):
        parts[offset] = swapped(parts[offset], "shard", offset)
    vector_parts = lax.all_to_all(
        jnp.broadcast_to(vector_grads[0], (shard_count, vector_count, vector_width * shard_count)),
        "shard",
        split_axis=0,
        concat_axis=0,
        tiled=True,
    )

    others = shard_count * tensor_count
    grad_rows, vector_whole, figures = on_device(
        functools.partial(sum_kernel, shard_count),
        place,
        parts[::-1] + [vector_parts, own_momentum],
        [
            jax.ShapeDtypeStruct(own_momentum.shape, jnp.float32),
            jax.ShapeDtypeStruct(vector_parts.shape[1:], jnp.float32),
            jax.ShapeDtypeStruct((others, section_count, 1, LANES), jnp.float32),
        ],
    )
    figures = lax.all_to_all(
        figures.reshape(others * section_count, 1, LANES),
        MESH_AXES,
        split_axis=0,
        concat_axis=0,
        tiled=True,
    )
    *scaled, clip_tile = on_device(
        functools.partial(scale_kernel, matrix_count),
        place,
        [figures, grad_rows, own_momentum],
        [jax.ShapeDtypeStruct((local_height, width), jnp.bfloat16)] * matrix_count
        + [jax.ShapeDtypeStruct((8, LANES), jnp.float32)],
    )

    pieces = [scaled[0]] + [None] * 3
    for offset in (2, 3, 1):
        ready = after(scaled[offset], pieces[2]) if offset == 3 else scaled[offset]
        pieces[offset] = swapped(ready, "shard", offset)
    near, side, far = [None] * 4, [None] * 4, [None] * 4
    near[0] = swapped(pieces[0], "tensor", 1)
    side[0] = swapped(pieces[0], "tensor", 2)
    far[0] = swapped(near[0], "tensor", 2)
    near[1] = swapped(pieces[1], "tensor", 1)
    side[1] = swapped(pieces[1], "tensor", 2)
    far[1] = swapped(side[1], "tensor", 1)
    near[2] = swapped(pieces[2], "tensor", 1)
    side[2] = swapped(pieces[2], "tensor", 2)
    far[2] = swapped(near[2], "tensor", 2)
    near[3] = swapped(pieces[3], "tensor", 1)
    side[3] = swapped(pieces[3], "tensor", 2)
    far[3] = swapped(pieces[3], "tensor", 3)
    results = orthogonalize([pieces, near, side, far])

    returned = {
        offset: swapped(results[offset], "shard", offset)
        for offset in reversed(range(1, shard_count))
    }
    early = finished((0,), place, [results[0]], weights[0])
    orthogonal_update, new_weights = finished(
        (3, 2, 1), place, [returned[offset] for offset in (3, 2, 1)], weights[0], early
    )
    new_momentum, adam_direction, new_vectors = on_device(
        state_kernel,
        place,
        [
            after(clip_tile, results[0]),
            grad_rows,
            own_momentum,
            vector_whole,
            vectors[0],
            first_moment[0],
            second_moment[0],
        ],
        [jax.ShapeDtypeStruct(own_momentum.shape, jnp.float32)]
        + [jax.ShapeDtypeStruct(vectors.shape[1:], jnp.float32)] * 2,
    )
    return (
        new_momentum[None],
        orthogonal_update[None],
        new_weights[None],
        adam_direction[None],
        new_vectors[None],
    )


def general_device(grad_parts, vector_grads, momentum, weights, vectors, first_moment, second_moment):
    shard_count = lax.axis_size("shard")
    tensor_count = lax.axis_size("tensor")
    section_count = lax.axis_size("section")
    shard_index = lax.axis_index("shard")
    _, matrix_count, local_height, width = momentum.shape
    vector_width = vectors.shape[2]
    own_momentum = momentum[0]

    rows = matrix_count * local_height
    by_target = (
        grad_parts.reshape(matrix_count, shard_count, local_height, width)
        .transpose(1, 0, 2, 3)
        .reshape(shard_count, rows, width)
    )
    vector_line = jnp.broadcast_to(
        vector_grads.reshape(1, 1, width), (shard_count, VECTOR_ROWS, width)
    )
    payload = jnp.concatenate([by_target, vector_line], axis=1)
    arrived = lax.all_to_all(payload, "shard", split_axis=0, concat_axis=0, tiled=True)
    grad_rows = jnp.sum(arrived[:, :rows].astype(jnp.float32), axis=0).reshape(
        matrix_count, local_height, width
    )
    vector_whole = jnp.sum(arrived[:, rows].astype(jnp.float32), axis=0).reshape(
        vectors.shape[1], vector_width * shard_count
    )
    vector_rows = lax.dynamic_slice_in_dim(
        vector_whole, shard_index * vector_width, vector_width, 1
    )

    grad_squares = jnp.sum(grad_rows * grad_rows, axis=(1, 2))
    cross = jnp.sum(grad_rows * own_momentum, axis=(1, 2))
    momentum_squares = jnp.sum(own_momentum * own_momentum, axis=(1, 2))
    own_total = jnp.sum(grad_squares) + jnp.sum(vector_rows * vector_rows)
    same_section = (
        jnp.arange(section_count) == lax.axis_index("section")
    ).astype(jnp.float32)[:, None]
    matrix_figures = jnp.concatenate([grad_squares, cross, momentum_squares])
    line = jnp.concatenate(
        [
            same_section * matrix_figures[None],
            jnp.broadcast_to(own_total, (section_count, 1)),
            jnp.zeros((section_count, 127 - 3 * matrix_count), jnp.float32),
        ],
        axis=1,
    )
    others = shard_count * tensor_count
    figures = jnp.broadcast_to(line[None, :, None, :], (others, section_count, 8, 128)).reshape(
        others * section_count, 8, 128
    )
    figures = lax.all_to_all(figures, MESH_AXES, split_axis=0, concat_axis=0, tiled=True)
    sums = jnp.sum(figures[:, 0, :], axis=0)
    grand_total = sums[3 * matrix_count]
    clip_factor = jnp.minimum(1.0, max_norm / (jnp.sqrt(grand_total) + 1e-06))
    grad_scale = (1.0 + mom_beta) * clip_factor
    momentum_scale = mom_beta * mom_beta
    update_norm = (
        grad_scale * grad_scale * sums[:matrix_count]
        + 2.0 * grad_scale * momentum_scale * sums[matrix_count : 2 * matrix_count]
        + momentum_scale * momentum_scale * sums[2 * matrix_count : 3 * matrix_count]
    )
    update_norm = jnp.maximum(update_norm, 0.0)[:, None, None]

    new_momentum = mom_beta * own_momentum + clip_factor * grad_rows
    nesterov = clip_factor * grad_rows + mom_beta * new_momentum
    scaled = (nesterov / (jnp.sqrt(update_norm) + 1e-07)).astype(jnp.bfloat16)

    owner_count = shard_count // matrix_count
    if owner_count == 1:
        row_block = lax.all_to_all(scaled, "shard", split_axis=0, concat_axis=0, tiled=True)
        row_block = row_block.reshape(shard_count * local_height, width)
    else:
        everything = lax.all_gather(scaled, "shard", axis=1, tiled=True)
        row_block = lax.dynamic_index_in_dim(
            everything, shard_index // owner_count, 0, keepdims=False
        )

    blocks = [row_block]
    for offset in range(1, tensor_count):
        pairs = [(i, i ^ offset) for i in range(tensor_count)]
        blocks.append(lax.ppermute(row_block, "tensor", pairs))
    (own_result,) = orthogonalize([[block] for block in blocks])

    if owner_count == 1:
        own_update = lax.all_to_all(
            own_result.reshape(shard_count, local_height, width),
            "shard",
            split_axis=0,
            concat_axis=0,
            tiled=True,
        )
    else:
        piece_length = local_height * width // owner_count
        split_rows = own_result.reshape(shard_count, owner_count, piece_length)
        returning = lax.dynamic_index_in_dim(
            split_rows, shard_index % owner_count, 1, keepdims=False
        )
        received = lax.all_to_all(returning, "shard", split_axis=0, concat_axis=0, tiled=True)
        own_update = received.reshape(matrix_count, local_height, width)
    orthogonal_update = own_update[None]
    muon_scale = 0.2 * math.sqrt(D)
    new_weights = (
        weights.astype(jnp.float32) * (1.0 - muon_rate * muon_decay)
        - muon_rate * muon_scale * orthogonal_update.astype(jnp.float32)
    ).astype(jnp.bfloat16)
    vector_clipped = clip_factor * vector_rows
    updated_first = 0.9 * first_moment + 0.1 * vector_clipped
    updated_second = 0.999 * second_moment + 0.001 * vector_clipped * vector_clipped
    adam_direction = updated_first / (jnp.sqrt(updated_second) + 1e-08)
    new_vectors = vectors * (1.0 - adam_rate * adam_decay) - adam_rate * adam_direction
    return (new_momentum[None], orthogonal_update, new_weights, adam_direction, new_vectors)


def solution(mesh):
    in_specs = (
        P("shard", "section", None, "tensor", None),
        P("shard", "section", None, "tensor"),
        P("section", None, ("tensor", "shard"), None),
        P("section", None, ("tensor", "shard"), None),
        P("section", None, ("tensor", "shard")),
        P("section", None, ("tensor", "shard")),
        P("section", None, ("tensor", "shard")),
    )
    out_specs = (
        P("section", None, ("tensor", "shard"), None),
        P("section", None, ("tensor", "shard"), None),
        P("section", None, ("tensor", "shard"), None),
        P("section", None, ("tensor", "shard")),
        P("section", None, ("tensor", "shard")),
    )
    return jax.shard_map(
        per_device, mesh=mesh, in_specs=in_specs, out_specs=out_specs, check_vma=False
    )
```

```python
import functools
import math

import jax
import jax.numpy as jnp
from jax import lax
from jax.experimental import pallas as pl
from jax.experimental.pallas import tpu as pltpu
from jax.sharding import PartitionSpec as P

D = 1024
NS_STEPS = 2


ns_first = 3.4445
ns_second = -4.775
ns_third = 2.0315
mom_beta = 0.95
max_norm = 1024.0
muon_rate = 0.02
muon_decay = 0.1
adam_rate = 0.001
adam_decay = 0.01

VECTOR_ROWS = 16
FIGURES = 16
MIB = 2**20
LANES = 128
MESH_AXES = ("shard", "tensor", "section")


def gram_of(blocks, gram_ref):
    width = blocks[0].shape[1]
    step = 256
    for start in range(0, width, step):
        stop = start + step
        total = None
        for block in blocks:
            whole = block[...]
            product = lax.dot_general(
                whole[:, :stop],
                whole[:, start:stop],
                (((0,), (0,)), ((), ())),
                preferred_element_type=jnp.float32,
            )
            rounded = product.astype(jnp.bfloat16).astype(jnp.float32)
            total = rounded if total is None else total + rounded
        gram_ref[:stop, start:stop] = total.astype(jnp.bfloat16)
        for above in range(0, start, step):
            tile = gram_ref[above : above + step, start:stop]
            gram_ref[start:stop, above : above + step] = tile.T


def polynomial(block, gram_ref):
    gram = gram_ref[...]
    first = jnp.dot(block, gram, preferred_element_type=jnp.float32).astype(jnp.bfloat16)
    second = jnp.dot(first, gram, preferred_element_type=jnp.float32)
    combined = (
        ns_first * block.astype(jnp.float32)
        + ns_second * first.astype(jnp.float32)
        + ns_third * second
    )
    return combined.astype(jnp.bfloat16)


def orthogonalize_kernel(count, pieces, *refs):
    height, width = refs[0].shape
    inputs = refs[: count * pieces]
    outputs = refs[count * pieces : count * pieces + pieces]
    gram_ref, start_ref, next_ref = refs[count * pieces + pieces :]
    block = pieces * height
    rows = count * block
    chunk = 2 * block if count % 2 == 0 else block
    for position, piece_ref in enumerate(inputs):
        start_ref[position * height : (position + 1) * height, :] = piece_ref[...]
    current, other = start_ref, next_ref
    for iteration in range(NS_STEPS):
        gram_of([current.at[start : start + block] for start in range(0, rows, block)], gram_ref)
        if iteration + 1 < NS_STEPS:
            for start in range(0, rows, chunk):
                other[start : start + chunk, :] = polynomial(
                    current[start : start + chunk, :], gram_ref
                )
            current, other = other, current
    result = polynomial(current[:block, :], gram_ref)
    for piece in range(pieces):
        outputs[piece][...] = result[piece * height : (piece + 1) * height, :]


def orthogonalize(blocks):
    count, pieces = len(blocks), len(blocks[0])
    height, width = blocks[0][0].shape
    return pl.pallas_call(
        functools.partial(orthogonalize_kernel, count, pieces),
        out_shape=[jax.ShapeDtypeStruct((height, width), jnp.bfloat16)] * pieces,
        scratch_shapes=[
            pltpu.VMEM((width, width), jnp.bfloat16),
            pltpu.VMEM((count * pieces * height, width), jnp.bfloat16),
            pltpu.VMEM((count * pieces * height, width), jnp.bfloat16),
        ],
        compiler_params=pltpu.CompilerParams(vmem_limit_bytes=32 * MIB),
    )(*[piece for block in blocks for piece in block])


def folded(array):
    line = jnp.sum(array, axis=0, keepdims=True)
    total = line[:, :LANES]
    for start in range(LANES, line.shape[1], LANES):
        total = total + line[:, start : start + LANES]
    return total


def slices_kernel(offsets, place_ref, grad_ref, *refs):
    outputs, semaphores = refs[: len(offsets)], refs[len(offsets)]
    copies = [
        pltpu.make_async_copy(grad_ref.at[:, place_ref[offset]], output, semaphores.at[slot])
        for slot, (offset, output) in enumerate(zip(offsets, outputs))
    ]
    for copy in copies:
        copy.start()
    for copy in copies:
        copy.wait()


def row_slices(offsets, place, by_rows):
    matrix_count, shard_count, height, width = by_rows.shape
    slices = pl.pallas_call(
        functools.partial(slices_kernel, offsets),
        out_shape=[pltpu.VMEM((matrix_count, height, width), by_rows.dtype)] * len(offsets),
        in_specs=[
            pl.BlockSpec(memory_space=pltpu.SMEM),
            pl.BlockSpec(memory_space=pltpu.HBM),
        ],
        out_specs=[pl.BlockSpec(memory_space=pltpu.VMEM)] * len(offsets),
        scratch_shapes=[pltpu.SemaphoreType.DMA((len(offsets),))],
        compiler_params=pltpu.CompilerParams(vmem_limit_bytes=60 * MIB),
    )(place, by_rows)
    return dict(zip(offsets, slices))


def sum_kernel(shard_count, place_ref, *refs):
    parts = refs[:shard_count]
    vector_parts, momentum_ref, grad_ref, vector_ref, figures_ref = refs[shard_count:]
    vector = jnp.sum(vector_parts[...].astype(jnp.float32), axis=0)
    vector_ref[...] = vector
    total = folded(vector * vector) * (1.0 / shard_count)
    squares, crosses, momentum_squares = [], [], []
    for matrix in range(momentum_ref.shape[0]):
        grad = parts[0][matrix].astype(jnp.float32)
        for part in parts[1:]:
            grad = grad + part[matrix].astype(jnp.float32)
        grad_ref[matrix] = grad
        old = momentum_ref[matrix]
        squares.append(folded(grad * grad))
        crosses.append(folded(grad * old))
        momentum_squares.append(folded(old * old))
        total = total + squares[-1]
    lines = squares + crosses + momentum_squares + [total]
    lines = lines + [jnp.zeros_like(total)] * (FIGURES - len(lines))
    tile = jnp.concatenate(lines, axis=0)
    sums = jnp.sum(tile, axis=1, keepdims=True)
    line_index = lax.broadcasted_iota(jnp.int32, tile.shape, 0)
    lane_index = lax.broadcasted_iota(jnp.int32, tile.shape, 1)
    line = jnp.sum(jnp.where(line_index == lane_index, sums, 0.0), axis=0, keepdims=True)
    total_only = jnp.where(lane_index[:1] == 3 * momentum_ref.shape[0], line, 0.0)
    for section in range(figures_ref.shape[1]):
        chosen = jnp.where(place_ref[shard_count] == section, line, total_only)
        figures_ref[:, section] = jnp.broadcast_to(
            chosen[None], (figures_ref.shape[0],) + line.shape
        )


def spread_kernel(place_ref, figures_ref, out_ref):
    line = jnp.sum(figures_ref[...], axis=0)
    out_ref[...] = jnp.broadcast_to(line[None], out_ref.shape)


def scale_kernel(matrix_count, place_ref, figures_ref, grad_ref, momentum_ref, *refs):
    outputs = refs[:matrix_count]
    clip_ref = refs[matrix_count]
    line = jnp.sum(figures_ref[...], axis=0)
    line_index = lax.broadcasted_iota(jnp.int32, (FIGURES, LANES), 0)
    lane_index = lax.broadcasted_iota(jnp.int32, (FIGURES, LANES), 1)
    sums = jnp.sum(jnp.where(line_index == lane_index, line, 0.0), axis=1, keepdims=True)
    total = sums[3 * matrix_count : 3 * matrix_count + 1]
    clip = jnp.minimum(1.0, max_norm / (jnp.sqrt(total) + 1e-06))
    clip_ref[...] = jnp.broadcast_to(clip, clip_ref.shape)
    grad_scale = (1.0 + mom_beta) * clip
    momentum_scale = mom_beta * mom_beta
    update_norm = (
        grad_scale * grad_scale * sums[:matrix_count]
        + 2.0 * grad_scale * momentum_scale * sums[matrix_count : 2 * matrix_count]
        + momentum_scale * momentum_scale * sums[2 * matrix_count : 3 * matrix_count]
    )
    inverse = 1.0 / (jnp.sqrt(jnp.maximum(update_norm, 0.0)) + 1e-07)
    position = lax.broadcasted_iota(jnp.int32, inverse.shape, 0)
    for place in range(matrix_count):
        matrix = place_ref[place]
        factor = jnp.sum(jnp.where(position == matrix, inverse, 0.0), axis=0, keepdims=True)
        clipped = clip * grad_ref[matrix]
        new_momentum = mom_beta * momentum_ref[matrix] + clipped
        nesterov = clipped + mom_beta * new_momentum
        outputs[place][...] = (nesterov * factor).astype(jnp.bfloat16)


def end_kernel(offsets, place_ref, *refs):
    arrived = refs[: len(offsets)]
    weights_ref = refs[len(offsets)]
    update_ref, new_weights_ref, update_rows, weight_rows, semaphores = refs[-5:]
    step_size = muon_rate * (0.2 * math.sqrt(D))
    copies = []
    for slot, offset in enumerate(offsets):
        matrix = place_ref[offset]
        update = arrived[slot][...]
        update_rows[slot] = update
        weight_rows[slot] = (
            weights_ref[matrix].astype(jnp.float32) * (1.0 - muon_rate * muon_decay)
            - step_size * update.astype(jnp.float32)
        ).astype(jnp.bfloat16)
        for kind, (rows, target) in enumerate(
            ((update_rows, update_ref), (weight_rows, new_weights_ref))
        ):
            copies.append(
                pltpu.make_async_copy(
                    rows.at[slot], target.at[matrix], semaphores.at[2 * slot + kind]
                )
            )
            copies[-1].start()
    for copy in copies:
        copy.wait()


def finished(offsets, place, arrived, weights, partial=()):
    height, width = arrived[0].shape
    anywhere = pl.BlockSpec(memory_space=pltpu.HBM)
    return pl.pallas_call(
        functools.partial(end_kernel, offsets),
        out_shape=[jax.ShapeDtypeStruct(weights.shape, weights.dtype)] * 2,
        in_specs=[pl.BlockSpec(memory_space=pltpu.SMEM)]
        + [pl.BlockSpec(memory_space=pltpu.VMEM)] * (len(arrived) + 1)
        + [anywhere] * len(partial),
        out_specs=[anywhere] * 2,
        scratch_shapes=[
            pltpu.VMEM((len(offsets), height, width), weights.dtype),
            pltpu.VMEM((len(offsets), height, width), weights.dtype),
            pltpu.SemaphoreType.DMA((2 * len(offsets),)),
        ],
        input_output_aliases={len(arrived) + 2 + i: i for i in range(len(partial))},
        compiler_params=pltpu.CompilerParams(vmem_limit_bytes=8 * MIB),
    )(place, *arrived, weights, *partial)


def state_kernel(
    place_ref,
    clip_ref,
    grad_ref,
    momentum_ref,
    sums_ref,
    vectors_ref,
    first_ref,
    second_ref,
    new_momentum_ref,
    direction_ref,
    new_ref,
):
    new_momentum_ref[...] = mom_beta * momentum_ref[...] + clip_ref[0:1, 0:1] * grad_ref[...]
    width = vectors_ref.shape[1]
    count = sums_ref.shape[1] // width
    rows = sums_ref[:, :width]
    for position in range(1, count):
        part = sums_ref[:, position * width : (position + 1) * width]
        rows = jnp.where(place_ref[0] == position, part, rows)
    clipped = clip_ref[0:1, 0:1] * rows
    updated_first = 0.9 * first_ref[...] + 0.1 * clipped
    updated_second = 0.999 * second_ref[...] + 0.001 * clipped * clipped
    direction = updated_first / (jnp.sqrt(updated_second) + 1e-08)
    direction_ref[...] = direction
    new_ref[...] = vectors_ref[...] * (1.0 - adam_rate * adam_decay) - adam_rate * direction


def on_device(kernel, scalars, operands, out_shape):
    return pl.pallas_call(
        kernel,
        out_shape=out_shape,
        in_specs=[pl.BlockSpec(memory_space=pltpu.SMEM)]
        + [pl.BlockSpec(memory_space=pltpu.VMEM)] * len(operands),
        compiler_params=pltpu.CompilerParams(vmem_limit_bytes=16 * MIB),
    )(scalars, *operands)


def swapped(array, axis, offset):
    pairs = [(i, i ^ offset) for i in range(lax.axis_size(axis))]
    return lax.ppermute(array, axis, pairs)


def after(array, earlier):
    return lax.optimization_barrier((array, earlier))[0]


def per_device(grad_parts, vector_grads, momentum, weights, vectors, first_moment, second_moment):
    shard_count = lax.axis_size("shard")
    tensor_count = lax.axis_size("tensor")
    section_count = lax.axis_size("section")
    _, matrix_count, local_height, width = momentum.shape
    if shard_count != matrix_count or shard_count != 4 or tensor_count != 4:
        return general_device(
            grad_parts, vector_grads, momentum, weights, vectors, first_moment, second_moment
        )
    vector_count, vector_width = vectors.shape[1:]
    own_momentum = momentum[0]
    position = jnp.arange(shard_count + 1, dtype=jnp.int32)
    place = jnp.where(
        position == shard_count,
        lax.axis_index("section").astype(jnp.int32),
        lax.axis_index("shard").astype(jnp.int32) ^ position,
    )

    by_rows = grad_parts.reshape(matrix_count, shard_count, local_height, width)
    parts = row_slices((3, 2), place, by_rows)
    parts.update(row_slices((1, 0), after(place, parts[3]), by_rows))
    for offset in reversed(range(1, shard_count)):
        parts[offset] = swapped(parts[offset], "shard", offset)
    vector_parts = lax.all_to_all(
        jnp.broadcast_to(vector_grads[0], (shard_count, vector_count, vector_width * shard_count)),
        "shard",
        split_axis=0,
        concat_axis=0,
        tiled=True,
    )

    grad_rows, vector_whole, figures = on_device(
        functools.partial(sum_kernel, shard_count),
        place,
        [parts[offset] for offset in (3, 2, 1, 0)] + [vector_parts, own_momentum],
        [
            jax.ShapeDtypeStruct(own_momentum.shape, jnp.float32),
            jax.ShapeDtypeStruct(vector_parts.shape[1:], jnp.float32),
            jax.ShapeDtypeStruct((tensor_count, section_count, 1, LANES), jnp.float32),
        ],
    )
    figures = lax.all_to_all(
        figures.reshape(tensor_count * section_count, 1, LANES),
        ("tensor", "section"),
        split_axis=0,
        concat_axis=0,
        tiled=True,
    )
    figures = on_device(
        spread_kernel,
        place,
        [figures],
        jax.ShapeDtypeStruct((shard_count, 1, LANES), jnp.float32),
    )
    figures = lax.all_to_all(figures, "shard", split_axis=0, concat_axis=0, tiled=True)
    *scaled, clip_tile = on_device(
        functools.partial(scale_kernel, matrix_count),
        place,
        [figures, grad_rows, own_momentum],
        [jax.ShapeDtypeStruct((local_height, width), jnp.bfloat16)] * matrix_count
        + [jax.ShapeDtypeStruct((8, LANES), jnp.float32)],
    )

    pieces = [scaled[0]] + [None] * 3
    for offset in (2, 3, 1):
        ready = after(scaled[offset], pieces[2]) if offset == 3 else scaled[offset]
        pieces[offset] = swapped(ready, "shard", offset)
    near, side, far = [None] * 4, [None] * 4, [None] * 4
    near[0] = swapped(pieces[0], "tensor", 1)
    side[0] = swapped(pieces[0], "tensor", 2)
    far[0] = swapped(near[0], "tensor", 2)
    near[1] = swapped(pieces[1], "tensor", 1)
    side[1] = swapped(pieces[1], "tensor", 2)
    far[1] = swapped(side[1], "tensor", 1)
    near[2] = swapped(pieces[2], "tensor", 1)
    side[2] = swapped(pieces[2], "tensor", 2)
    far[2] = swapped(near[2], "tensor", 2)
    near[3] = swapped(pieces[3], "tensor", 1)
    side[3] = swapped(pieces[3], "tensor", 2)
    far[3] = swapped(pieces[3], "tensor", 3)
    results = orthogonalize([pieces, near, side, far])

    returned = {
        offset: swapped(results[offset], "shard", offset)
        for offset in reversed(range(1, shard_count))
    }
    early = finished((0,), place, [results[0]], weights[0])
    orthogonal_update, new_weights = finished(
        (3, 2, 1), place, [returned[offset] for offset in (3, 2, 1)], weights[0], early
    )
    new_momentum, adam_direction, new_vectors = on_device(
        state_kernel,
        place,
        [
            after(clip_tile, results[0]),
            grad_rows,
            own_momentum,
            vector_whole,
            vectors[0],
            first_moment[0],
            second_moment[0],
        ],
        [jax.ShapeDtypeStruct(own_momentum.shape, jnp.float32)]
        + [jax.ShapeDtypeStruct(vectors.shape[1:], jnp.float32)] * 2,
    )
    return (
        new_momentum[None],
        orthogonal_update[None],
        new_weights[None],
        adam_direction[None],
        new_vectors[None],
    )


def general_device(grad_parts, vector_grads, momentum, weights, vectors, first_moment, second_moment):
    shard_count = lax.axis_size("shard")
    tensor_count = lax.axis_size("tensor")
    section_count = lax.axis_size("section")
    shard_index = lax.axis_index("shard")
    _, matrix_count, local_height, width = momentum.shape
    vector_width = vectors.shape[2]
    own_momentum = momentum[0]

    rows = matrix_count * local_height
    by_target = (
        grad_parts.reshape(matrix_count, shard_count, local_height, width)
        .transpose(1, 0, 2, 3)
        .reshape(shard_count, rows, width)
    )
    vector_line = jnp.broadcast_to(
        vector_grads.reshape(1, 1, width), (shard_count, VECTOR_ROWS, width)
    )
    payload = jnp.concatenate([by_target, vector_line], axis=1)
    arrived = lax.all_to_all(payload, "shard", split_axis=0, concat_axis=0, tiled=True)
    grad_rows = jnp.sum(arrived[:, :rows].astype(jnp.float32), axis=0).reshape(
        matrix_count, local_height, width
    )
    vector_whole = jnp.sum(arrived[:, rows].astype(jnp.float32), axis=0).reshape(
        vectors.shape[1], vector_width * shard_count
    )
    vector_rows = lax.dynamic_slice_in_dim(
        vector_whole, shard_index * vector_width, vector_width, 1
    )

    grad_squares = jnp.sum(grad_rows * grad_rows, axis=(1, 2))
    cross = jnp.sum(grad_rows * own_momentum, axis=(1, 2))
    momentum_squares = jnp.sum(own_momentum * own_momentum, axis=(1, 2))
    own_total = jnp.sum(grad_squares) + jnp.sum(vector_rows * vector_rows)
    same_section = (
        jnp.arange(section_count) == lax.axis_index("section")
    ).astype(jnp.float32)[:, None]
    matrix_figures = jnp.concatenate([grad_squares, cross, momentum_squares])
    line = jnp.concatenate(
        [
            same_section * matrix_figures[None],
            jnp.broadcast_to(own_total, (section_count, 1)),
            jnp.zeros((section_count, 127 - 3 * matrix_count), jnp.float32),
        ],
        axis=1,
    )
    others = shard_count * tensor_count
    figures = jnp.broadcast_to(line[None, :, None, :], (others, section_count, 8, 128)).reshape(
        others * section_count, 8, 128
    )
    figures = lax.all_to_all(figures, MESH_AXES, split_axis=0, concat_axis=0, tiled=True)
    sums = jnp.sum(figures[:, 0, :], axis=0)
    grand_total = sums[3 * matrix_count]
    clip_factor = jnp.minimum(1.0, max_norm / (jnp.sqrt(grand_total) + 1e-06))
    grad_scale = (1.0 + mom_beta) * clip_factor
    momentum_scale = mom_beta * mom_beta
    update_norm = (
        grad_scale * grad_scale * sums[:matrix_count]
        + 2.0 * grad_scale * momentum_scale * sums[matrix_count : 2 * matrix_count]
        + momentum_scale * momentum_scale * sums[2 * matrix_count : 3 * matrix_count]
    )
    update_norm = jnp.maximum(update_norm, 0.0)[:, None, None]

    new_momentum = mom_beta * own_momentum + clip_factor * grad_rows
    nesterov = clip_factor * grad_rows + mom_beta * new_momentum
    scaled = (nesterov / (jnp.sqrt(update_norm) + 1e-07)).astype(jnp.bfloat16)

    owner_count = shard_count // matrix_count
    if owner_count == 1:
        row_block = lax.all_to_all(scaled, "shard", split_axis=0, concat_axis=0, tiled=True)
        row_block = row_block.reshape(shard_count * local_height, width)
    else:
        everything = lax.all_gather(scaled, "shard", axis=1, tiled=True)
        row_block = lax.dynamic_index_in_dim(
            everything, shard_index // owner_count, 0, keepdims=False
        )

    blocks = [row_block]
    for offset in range(1, tensor_count):
        pairs = [(i, i ^ offset) for i in range(tensor_count)]
        blocks.append(lax.ppermute(row_block, "tensor", pairs))
    (own_result,) = orthogonalize([[block] for block in blocks])

    if owner_count == 1:
        own_update = lax.all_to_all(
            own_result.reshape(shard_count, local_height, width),
            "shard",
            split_axis=0,
            concat_axis=0,
            tiled=True,
        )
    else:
        piece_length = local_height * width // owner_count
        split_rows = own_result.reshape(shard_count, owner_count, piece_length)
        returning = lax.dynamic_index_in_dim(
            split_rows, shard_index % owner_count, 1, keepdims=False
        )
        received = lax.all_to_all(returning, "shard", split_axis=0, concat_axis=0, tiled=True)
        own_update = received.reshape(matrix_count, local_height, width)
    orthogonal_update = own_update[None]
    muon_scale = 0.2 * math.sqrt(D)
    new_weights = (
        weights.astype(jnp.float32) * (1.0 - muon_rate * muon_decay)
        - muon_rate * muon_scale * orthogonal_update.astype(jnp.float32)
    ).astype(jnp.bfloat16)
    vector_clipped = clip_factor * vector_rows
    updated_first = 0.9 * first_moment + 0.1 * vector_clipped
    updated_second = 0.999 * second_moment + 0.001 * vector_clipped * vector_clipped
    adam_direction = updated_first / (jnp.sqrt(updated_second) + 1e-08)
    new_vectors = vectors * (1.0 - adam_rate * adam_decay) - adam_rate * adam_direction
    return (new_momentum[None], orthogonal_update, new_weights, adam_direction, new_vectors)


def solution(mesh):
    in_specs = (
        P("shard", "section", None, "tensor", None),
        P("shard", "section", None, "tensor"),
        P("section", None, ("tensor", "shard"), None),
        P("section", None, ("tensor", "shard"), None),
        P("section", None, ("tensor", "shard")),
        P("section", None, ("tensor", "shard")),
        P("section", None, ("tensor", "shard")),
    )
    out_specs = (
        P("section", None, ("tensor", "shard"), None),
        P("section", None, ("tensor", "shard"), None),
        P("section", None, ("tensor", "shard"), None),
        P("section", None, ("tensor", "shard")),
        P("section", None, ("tensor", "shard")),
    )
    return jax.shard_map(
        per_device, mesh=mesh, in_specs=in_specs, out_specs=out_specs, check_vma=False
    )
```

```python
import functools
import math

import jax
import jax.numpy as jnp
from jax import lax
from jax.experimental import pallas as pl
from jax.experimental.pallas import tpu as pltpu
from jax.sharding import PartitionSpec as P

D = 1024
NS_STEPS = 2


ns_first = 3.4445
ns_second = -4.775
ns_third = 2.0315
mom_beta = 0.95
max_norm = 1024.0
muon_rate = 0.02
muon_decay = 0.1
adam_rate = 0.001
adam_decay = 0.01

VECTOR_ROWS = 16
FIGURES = 16
MIB = 2**20
LANES = 128
MESH_AXES = ("shard", "tensor", "section")


def gram_of(blocks, gram_ref, ready_ref=None):
    width = blocks[0].shape[1]
    step = 256
    for start in range(0, width, step):
        stop = start + step
        total = None if ready_ref is None else ready_ref[:stop, start:stop].astype(jnp.float32)
        for block in blocks:
            whole = block[...]
            product = lax.dot_general(
                whole[:, :stop],
                whole[:, start:stop],
                (((0,), (0,)), ((), ())),
                preferred_element_type=jnp.float32,
            )
            rounded = product.astype(jnp.bfloat16).astype(jnp.float32)
            total = rounded if total is None else total + rounded
        gram_ref[:stop, start:stop] = total.astype(jnp.bfloat16)
        for above in range(0, start, step):
            tile = gram_ref[above : above + step, start:stop]
            gram_ref[start:stop, above : above + step] = tile.T


def polynomial(block, gram_ref):
    gram = gram_ref[...]
    first = jnp.dot(block, gram, preferred_element_type=jnp.float32).astype(jnp.bfloat16)
    second = jnp.dot(first, gram, preferred_element_type=jnp.float32)
    combined = (
        ns_first * block.astype(jnp.float32)
        + ns_second * first.astype(jnp.float32)
        + ns_third * second
    )
    return combined.astype(jnp.bfloat16)


def block_gram_kernel(*refs):
    pieces, (gram_ref, rows_ref) = refs[:-2], refs[-2:]
    height = pieces[0].shape[0]
    for position, piece_ref in enumerate(pieces):
        rows_ref[position * height : (position + 1) * height, :] = piece_ref[...]
    whole = rows_ref[...]
    step = 256
    for start in range(0, whole.shape[1], step):
        stop = start + step
        gram_ref[:stop, start:stop] = lax.dot_general(
            whole[:, :stop],
            whole[:, start:stop],
            (((0,), (0,)), ((), ())),
            preferred_element_type=jnp.float32,
        ).astype(jnp.bfloat16)


def block_gram(pieces):
    height, width = pieces[0].shape
    return pl.pallas_call(
        block_gram_kernel,
        out_shape=jax.ShapeDtypeStruct((width, width), jnp.bfloat16),
        scratch_shapes=[pltpu.VMEM((len(pieces) * height, width), jnp.bfloat16)],
        compiler_params=pltpu.CompilerParams(vmem_limit_bytes=16 * MIB),
    )(*pieces)


def orthogonalize_kernel(count, pieces, *refs):
    height, width = refs[0].shape
    inputs = refs[: count * pieces]
    ready_ref = refs[count * pieces]
    outputs = refs[count * pieces + 1 : count * pieces + 1 + pieces]
    gram_ref, start_ref, next_ref = refs[count * pieces + 1 + pieces :]
    block = pieces * height
    rows = count * block
    chunk = 2 * block if count % 2 == 0 else block
    for position, piece_ref in enumerate(inputs):
        start_ref[position * height : (position + 1) * height, :] = piece_ref[...]
    current, other = start_ref, next_ref
    for iteration in range(NS_STEPS):
        blocks = [current.at[start : start + block] for start in range(0, rows, block)]
        if iteration == 0:
            gram_of(blocks[1:], gram_ref, ready_ref)
        else:
            gram_of(blocks, gram_ref)
        if iteration + 1 < NS_STEPS:
            for start in range(0, rows, chunk):
                other[start : start + chunk, :] = polynomial(
                    current[start : start + chunk, :], gram_ref
                )
            current, other = other, current
    result = polynomial(current[:block, :], gram_ref)
    for piece in range(pieces):
        outputs[piece][...] = result[piece * height : (piece + 1) * height, :]


def orthogonalize(blocks, own_gram):
    count, pieces = len(blocks), len(blocks[0])
    height, width = blocks[0][0].shape
    return pl.pallas_call(
        functools.partial(orthogonalize_kernel, count, pieces),
        out_shape=[jax.ShapeDtypeStruct((height, width), jnp.bfloat16)] * pieces,
        scratch_shapes=[
            pltpu.VMEM((width, width), jnp.bfloat16),
            pltpu.VMEM((count * pieces * height, width), jnp.bfloat16),
            pltpu.VMEM((count * pieces * height, width), jnp.bfloat16),
        ],
        compiler_params=pltpu.CompilerParams(vmem_limit_bytes=32 * MIB),
    )(*[piece for block in blocks for piece in block], own_gram)


def folded(array):
    line = jnp.sum(array, axis=0, keepdims=True)
    total = line[:, :LANES]
    for start in range(LANES, line.shape[1], LANES):
        total = total + line[:, start : start + LANES]
    return total


def slices_kernel(count, place_ref, grad_ref, *refs):
    outputs, semaphores = refs[:count], refs[count]
    copies = [
        pltpu.make_async_copy(
            grad_ref.at[:, place_ref[offset]], outputs[offset], semaphores.at[offset]
        )
        for offset in range(count)
    ]
    for copy in reversed(copies):
        copy.start()
    for copy in reversed(copies):
        copy.wait()


def row_slices(place, by_rows):
    matrix_count, shard_count, height, width = by_rows.shape
    return pl.pallas_call(
        functools.partial(slices_kernel, shard_count),
        out_shape=[jax.ShapeDtypeStruct((matrix_count, height, width), by_rows.dtype)] * shard_count,
        in_specs=[
            pl.BlockSpec(memory_space=pltpu.SMEM),
            pl.BlockSpec(memory_space=pltpu.HBM),
        ],
        out_specs=[pl.BlockSpec(memory_space=pltpu.VMEM)] * shard_count,
        scratch_shapes=[pltpu.SemaphoreType.DMA((shard_count,))],
        compiler_params=pltpu.CompilerParams(vmem_limit_bytes=4 * MIB),
    )(place, by_rows)


def sum_kernel(shard_count, place_ref, *refs):
    parts = refs[:shard_count]
    vector_parts, momentum_ref, grad_ref, vector_ref, figures_ref = refs[shard_count:]
    vector = jnp.sum(vector_parts[...].astype(jnp.float32), axis=0)
    vector_ref[...] = vector
    total = folded(vector * vector) * (1.0 / shard_count)
    squares, crosses, momentum_squares = [], [], []
    for matrix in range(momentum_ref.shape[0]):
        grad = parts[0][matrix].astype(jnp.float32)
        for part in parts[1:]:
            grad = grad + part[matrix].astype(jnp.float32)
        grad_ref[matrix] = grad
        old = momentum_ref[matrix]
        squares.append(folded(grad * grad))
        crosses.append(folded(grad * old))
        momentum_squares.append(folded(old * old))
        total = total + squares[-1]
    lines = squares + crosses + momentum_squares + [total]
    lines = lines + [jnp.zeros_like(total)] * (FIGURES - len(lines))
    tile = jnp.concatenate(lines, axis=0)
    sums = jnp.sum(tile, axis=1, keepdims=True)
    line_index = lax.broadcasted_iota(jnp.int32, tile.shape, 0)
    lane_index = lax.broadcasted_iota(jnp.int32, tile.shape, 1)
    line = jnp.sum(jnp.where(line_index == lane_index, sums, 0.0), axis=0, keepdims=True)
    total_only = jnp.where(lane_index[:1] == 3 * momentum_ref.shape[0], line, 0.0)
    for section in range(figures_ref.shape[1]):
        chosen = jnp.where(place_ref[shard_count] == section, line, total_only)
        figures_ref[:, section] = jnp.broadcast_to(
            chosen[None], (figures_ref.shape[0],) + line.shape
        )


def scale_kernel(matrix_count, place_ref, figures_ref, grad_ref, momentum_ref, *refs):
    outputs = refs[:matrix_count]
    clip_ref = refs[matrix_count]
    line = jnp.sum(figures_ref[...], axis=0)
    line_index = lax.broadcasted_iota(jnp.int32, (FIGURES, LANES), 0)
    lane_index = lax.broadcasted_iota(jnp.int32, (FIGURES, LANES), 1)
    sums = jnp.sum(jnp.where(line_index == lane_index, line, 0.0), axis=1, keepdims=True)
    total = sums[3 * matrix_count : 3 * matrix_count + 1]
    clip = jnp.minimum(1.0, max_norm / (jnp.sqrt(total) + 1e-06))
    clip_ref[...] = jnp.broadcast_to(clip, clip_ref.shape)
    grad_scale = (1.0 + mom_beta) * clip
    momentum_scale = mom_beta * mom_beta
    update_norm = (
        grad_scale * grad_scale * sums[:matrix_count]
        + 2.0 * grad_scale * momentum_scale * sums[matrix_count : 2 * matrix_count]
        + momentum_scale * momentum_scale * sums[2 * matrix_count : 3 * matrix_count]
    )
    inverse = 1.0 / (jnp.sqrt(jnp.maximum(update_norm, 0.0)) + 1e-07)
    position = lax.broadcasted_iota(jnp.int32, inverse.shape, 0)
    for place in range(matrix_count):
        matrix = place_ref[place]
        factor = jnp.sum(jnp.where(position == matrix, inverse, 0.0), axis=0, keepdims=True)
        clipped = clip * grad_ref[matrix]
        new_momentum = mom_beta * momentum_ref[matrix] + clipped
        nesterov = clipped + mom_beta * new_momentum
        outputs[place][...] = (nesterov * factor).astype(jnp.bfloat16)


def end_kernel(offsets, place_ref, *refs):
    arrived = refs[: len(offsets)]
    weights_ref = refs[len(offsets)]
    update_ref, new_weights_ref, update_rows, weight_rows, semaphores = refs[-5:]
    step_size = muon_rate * (0.2 * math.sqrt(D))
    copies = []
    for slot, offset in enumerate(offsets):
        matrix = place_ref[offset]
        update = arrived[slot][...]
        update_rows[slot] = update
        weight_rows[slot] = (
            weights_ref[matrix].astype(jnp.float32) * (1.0 - muon_rate * muon_decay)
            - step_size * update.astype(jnp.float32)
        ).astype(jnp.bfloat16)
        for kind, (rows, target) in enumerate(
            ((update_rows, update_ref), (weight_rows, new_weights_ref))
        ):
            copies.append(
                pltpu.make_async_copy(
                    rows.at[slot], target.at[matrix], semaphores.at[2 * slot + kind]
                )
            )
            copies[-1].start()
    for copy in copies:
        copy.wait()


def finished(offsets, place, arrived, weights, partial=()):
    height, width = arrived[0].shape
    anywhere = pl.BlockSpec(memory_space=pltpu.HBM)
    return pl.pallas_call(
        functools.partial(end_kernel, offsets),
        out_shape=[jax.ShapeDtypeStruct(weights.shape, weights.dtype)] * 2,
        in_specs=[pl.BlockSpec(memory_space=pltpu.SMEM)]
        + [pl.BlockSpec(memory_space=pltpu.VMEM)] * (len(arrived) + 1)
        + [anywhere] * len(partial),
        out_specs=[anywhere] * 2,
        scratch_shapes=[
            pltpu.VMEM((len(offsets), height, width), weights.dtype),
            pltpu.VMEM((len(offsets), height, width), weights.dtype),
            pltpu.SemaphoreType.DMA((2 * len(offsets),)),
        ],
        input_output_aliases={len(arrived) + 2 + i: i for i in range(len(partial))},
        compiler_params=pltpu.CompilerParams(vmem_limit_bytes=8 * MIB),
    )(place, *arrived, weights, *partial)


def state_kernel(
    place_ref,
    clip_ref,
    grad_ref,
    momentum_ref,
    sums_ref,
    vectors_ref,
    first_ref,
    second_ref,
    new_momentum_ref,
    direction_ref,
    new_ref,
):
    new_momentum_ref[...] = mom_beta * momentum_ref[...] + clip_ref[0:1, 0:1] * grad_ref[...]
    width = vectors_ref.shape[1]
    count = sums_ref.shape[1] // width
    rows = sums_ref[:, :width]
    for position in range(1, count):
        part = sums_ref[:, position * width : (position + 1) * width]
        rows = jnp.where(place_ref[0] == position, part, rows)
    clipped = clip_ref[0:1, 0:1] * rows
    updated_first = 0.9 * first_ref[...] + 0.1 * clipped
    updated_second = 0.999 * second_ref[...] + 0.001 * clipped * clipped
    direction = updated_first / (jnp.sqrt(updated_second) + 1e-08)
    direction_ref[...] = direction
    new_ref[...] = vectors_ref[...] * (1.0 - adam_rate * adam_decay) - adam_rate * direction


def on_device(kernel, scalars, operands, out_shape):
    return pl.pallas_call(
        kernel,
        out_shape=out_shape,
        in_specs=[pl.BlockSpec(memory_space=pltpu.SMEM)]
        + [pl.BlockSpec(memory_space=pltpu.VMEM)] * len(operands),
        compiler_params=pltpu.CompilerParams(vmem_limit_bytes=16 * MIB),
    )(scalars, *operands)


def swapped(array, axis, offset):
    pairs = [(i, i ^ offset) for i in range(lax.axis_size(axis))]
    return lax.ppermute(array, axis, pairs)


def after(array, earlier):
    return lax.optimization_barrier((array, earlier))[0]


def per_device(grad_parts, vector_grads, momentum, weights, vectors, first_moment, second_moment):
    shard_count = lax.axis_size("shard")
    tensor_count = lax.axis_size("tensor")
    section_count = lax.axis_size("section")
    _, matrix_count, local_height, width = momentum.shape
    if shard_count != matrix_count or shard_count != 4 or tensor_count != 4:
        return general_device(
            grad_parts, vector_grads, momentum, weights, vectors, first_moment, second_moment
        )
    vector_count, vector_width = vectors.shape[1:]
    own_momentum = momentum[0]
    position = jnp.arange(shard_count + 1, dtype=jnp.int32)
    place = jnp.where(
        position == shard_count,
        lax.axis_index("section").astype(jnp.int32),
        lax.axis_index("shard").astype(jnp.int32) ^ position,
    )

    by_rows = grad_parts.reshape(matrix_count, shard_count, local_height, width)
    parts = list(row_slices(place, by_rows))
    for offset in reversed(range(1, shard_count)):
        parts[offset] = swapped(parts[offset], "shard", offset)
    vector_parts = lax.all_to_all(
        jnp.broadcast_to(vector_grads[0], (shard_count, vector_count, vector_width * shard_count)),
        "shard",
        split_axis=0,
        concat_axis=0,
        tiled=True,
    )

    others = shard_count * tensor_count
    grad_rows, vector_whole, figures = on_device(
        functools.partial(sum_kernel, shard_count),
        place,
        parts[::-1] + [vector_parts, own_momentum],
        [
            jax.ShapeDtypeStruct(own_momentum.shape, jnp.float32),
            jax.ShapeDtypeStruct(vector_parts.shape[1:], jnp.float32),
            jax.ShapeDtypeStruct((others, section_count, 1, LANES), jnp.float32),
        ],
    )
    figures = lax.all_to_all(
        figures.reshape(others * section_count, 1, LANES),
        MESH_AXES,
        split_axis=0,
        concat_axis=0,
        tiled=True,
    )
    *scaled, clip_tile = on_device(
        functools.partial(scale_kernel, matrix_count),
        place,
        [figures, grad_rows, own_momentum],
        [jax.ShapeDtypeStruct((local_height, width), jnp.bfloat16)] * matrix_count
        + [jax.ShapeDtypeStruct((8, LANES), jnp.float32)],
    )

    pieces = [scaled[0]] + [None] * 3
    for offset in (2, 3, 1):
        ready = after(scaled[offset], pieces[2]) if offset == 3 else scaled[offset]
        pieces[offset] = swapped(ready, "shard", offset)
    near, side, far = [None] * 4, [None] * 4, [None] * 4
    near[0] = swapped(pieces[0], "tensor", 1)
    side[0] = swapped(pieces[0], "tensor", 2)
    far[0] = swapped(near[0], "tensor", 2)
    near[1] = swapped(pieces[1], "tensor", 1)
    side[1] = swapped(pieces[1], "tensor", 2)
    far[1] = swapped(side[1], "tensor", 1)
    near[2] = swapped(pieces[2], "tensor", 1)
    side[2] = swapped(pieces[2], "tensor", 2)
    far[2] = swapped(near[2], "tensor", 2)
    near[3] = swapped(pieces[3], "tensor", 1)
    side[3] = swapped(pieces[3], "tensor", 2)
    far[3] = swapped(pieces[3], "tensor", 3)
    own_gram = block_gram(pieces[:3] + [after(pieces[3], far[1])])
    results = orthogonalize([pieces, near, side, far], own_gram)

    returned = {
        offset: swapped(results[offset], "shard", offset)
        for offset in reversed(range(1, shard_count))
    }
    early = finished((0,), place, [results[0]], weights[0])
    orthogonal_update, new_weights = finished(
        (3, 2, 1), place, [returned[offset] for offset in (3, 2, 1)], weights[0], early
    )
    new_momentum, adam_direction, new_vectors = on_device(
        state_kernel,
        place,
        [
            after(clip_tile, results[0]),
            grad_rows,
            own_momentum,
            vector_whole,
            vectors[0],
            first_moment[0],
            second_moment[0],
        ],
        [jax.ShapeDtypeStruct(own_momentum.shape, jnp.float32)]
        + [jax.ShapeDtypeStruct(vectors.shape[1:], jnp.float32)] * 2,
    )
    return (
        new_momentum[None],
        orthogonal_update[None],
        new_weights[None],
        adam_direction[None],
        new_vectors[None],
    )


def general_device(grad_parts, vector_grads, momentum, weights, vectors, first_moment, second_moment):
    shard_count = lax.axis_size("shard")
    tensor_count = lax.axis_size("tensor")
    section_count = lax.axis_size("section")
    shard_index = lax.axis_index("shard")
    _, matrix_count, local_height, width = momentum.shape
    vector_width = vectors.shape[2]
    own_momentum = momentum[0]

    rows = matrix_count * local_height
    by_target = (
        grad_parts.reshape(matrix_count, shard_count, local_height, width)
        .transpose(1, 0, 2, 3)
        .reshape(shard_count, rows, width)
    )
    vector_line = jnp.broadcast_to(
        vector_grads.reshape(1, 1, width), (shard_count, VECTOR_ROWS, width)
    )
    payload = jnp.concatenate([by_target, vector_line], axis=1)
    arrived = lax.all_to_all(payload, "shard", split_axis=0, concat_axis=0, tiled=True)
    grad_rows = jnp.sum(arrived[:, :rows].astype(jnp.float32), axis=0).reshape(
        matrix_count, local_height, width
    )
    vector_whole = jnp.sum(arrived[:, rows].astype(jnp.float32), axis=0).reshape(
        vectors.shape[1], vector_width * shard_count
    )
    vector_rows = lax.dynamic_slice_in_dim(
        vector_whole, shard_index * vector_width, vector_width, 1
    )

    grad_squares = jnp.sum(grad_rows * grad_rows, axis=(1, 2))
    cross = jnp.sum(grad_rows * own_momentum, axis=(1, 2))
    momentum_squares = jnp.sum(own_momentum * own_momentum, axis=(1, 2))
    own_total = jnp.sum(grad_squares) + jnp.sum(vector_rows * vector_rows)
    same_section = (
        jnp.arange(section_count) == lax.axis_index("section")
    ).astype(jnp.float32)[:, None]
    matrix_figures = jnp.concatenate([grad_squares, cross, momentum_squares])
    line = jnp.concatenate(
        [
            same_section * matrix_figures[None],
            jnp.broadcast_to(own_total, (section_count, 1)),
            jnp.zeros((section_count, 127 - 3 * matrix_count), jnp.float32),
        ],
        axis=1,
    )
    others = shard_count * tensor_count
    figures = jnp.broadcast_to(line[None, :, None, :], (others, section_count, 8, 128)).reshape(
        others * section_count, 8, 128
    )
    figures = lax.all_to_all(figures, MESH_AXES, split_axis=0, concat_axis=0, tiled=True)
    sums = jnp.sum(figures[:, 0, :], axis=0)
    grand_total = sums[3 * matrix_count]
    clip_factor = jnp.minimum(1.0, max_norm / (jnp.sqrt(grand_total) + 1e-06))
    grad_scale = (1.0 + mom_beta) * clip_factor
    momentum_scale = mom_beta * mom_beta
    update_norm = (
        grad_scale * grad_scale * sums[:matrix_count]
        + 2.0 * grad_scale * momentum_scale * sums[matrix_count : 2 * matrix_count]
        + momentum_scale * momentum_scale * sums[2 * matrix_count : 3 * matrix_count]
    )
    update_norm = jnp.maximum(update_norm, 0.0)[:, None, None]

    new_momentum = mom_beta * own_momentum + clip_factor * grad_rows
    nesterov = clip_factor * grad_rows + mom_beta * new_momentum
    scaled = (nesterov / (jnp.sqrt(update_norm) + 1e-07)).astype(jnp.bfloat16)

    owner_count = shard_count // matrix_count
    if owner_count == 1:
        row_block = lax.all_to_all(scaled, "shard", split_axis=0, concat_axis=0, tiled=True)
        row_block = row_block.reshape(shard_count * local_height, width)
    else:
        everything = lax.all_gather(scaled, "shard", axis=1, tiled=True)
        row_block = lax.dynamic_index_in_dim(
            everything, shard_index // owner_count, 0, keepdims=False
        )

    blocks = [row_block]
    for offset in range(1, tensor_count):
        pairs = [(i, i ^ offset) for i in range(tensor_count)]
        blocks.append(lax.ppermute(row_block, "tensor", pairs))
    (own_result,) = orthogonalize([[block] for block in blocks], block_gram(blocks[:1]))

    if owner_count == 1:
        own_update = lax.all_to_all(
            own_result.reshape(shard_count, local_height, width),
            "shard",
            split_axis=0,
            concat_axis=0,
            tiled=True,
        )
    else:
        piece_length = local_height * width // owner_count
        split_rows = own_result.reshape(shard_count, owner_count, piece_length)
        returning = lax.dynamic_index_in_dim(
            split_rows, shard_index % owner_count, 1, keepdims=False
        )
        received = lax.all_to_all(returning, "shard", split_axis=0, concat_axis=0, tiled=True)
        own_update = received.reshape(matrix_count, local_height, width)
    orthogonal_update = own_update[None]
    muon_scale = 0.2 * math.sqrt(D)
    new_weights = (
        weights.astype(jnp.float32) * (1.0 - muon_rate * muon_decay)
        - muon_rate * muon_scale * orthogonal_update.astype(jnp.float32)
    ).astype(jnp.bfloat16)
    vector_clipped = clip_factor * vector_rows
    updated_first = 0.9 * first_moment + 0.1 * vector_clipped
    updated_second = 0.999 * second_moment + 0.001 * vector_clipped * vector_clipped
    adam_direction = updated_first / (jnp.sqrt(updated_second) + 1e-08)
    new_vectors = vectors * (1.0 - adam_rate * adam_decay) - adam_rate * adam_direction
    return (new_momentum[None], orthogonal_update, new_weights, adam_direction, new_vectors)


def solution(mesh):
    in_specs = (
        P("shard", "section", None, "tensor", None),
        P("shard", "section", None, "tensor"),
        P("section", None, ("tensor", "shard"), None),
        P("section", None, ("tensor", "shard"), None),
        P("section", None, ("tensor", "shard")),
        P("section", None, ("tensor", "shard")),
        P("section", None, ("tensor", "shard")),
    )
    out_specs = (
        P("section", None, ("tensor", "shard"), None),
        P("section", None, ("tensor", "shard"), None),
        P("section", None, ("tensor", "shard"), None),
        P("section", None, ("tensor", "shard")),
        P("section", None, ("tensor", "shard")),
    )
    return jax.shard_map(
        per_device, mesh=mesh, in_specs=in_specs, out_specs=out_specs, check_vma=False
    )
```

```python
import functools
import math

import jax
import jax.numpy as jnp
from jax import lax
from jax.experimental import pallas as pl
from jax.experimental.pallas import tpu as pltpu
from jax.sharding import PartitionSpec as P

D = 1024
NS_STEPS = 2


ns_first = 3.4445
ns_second = -4.775
ns_third = 2.0315
mom_beta = 0.95
max_norm = 1024.0
muon_rate = 0.02
muon_decay = 0.1
adam_rate = 0.001
adam_decay = 0.01

VECTOR_ROWS = 16
FIGURES = 16
MIB = 2**20
LANES = 128
MESH_AXES = ("shard", "tensor", "section")


def gram_of(blocks, gram_ref, ready_ref=None):
    width = blocks[0].shape[1]
    step = 256
    turned = [block[...].T for block in blocks]
    for start in range(0, width, step):
        stop = start + step
        total = None if ready_ref is None else ready_ref[:stop, start:stop].astype(jnp.float32)
        for block, columns in zip(blocks, turned):
            product = jnp.dot(
                columns[:stop], block[:, start:stop], preferred_element_type=jnp.float32
            )
            rounded = product.astype(jnp.bfloat16).astype(jnp.float32)
            total = rounded if total is None else total + rounded
        gram_ref[:stop, start:stop] = total.astype(jnp.bfloat16)
        for above in range(0, start, step):
            tile = gram_ref[above : above + step, start:stop]
            gram_ref[start:stop, above : above + step] = tile.T


def polynomial(block, gram_ref):
    gram = gram_ref[...]
    first = jnp.dot(block, gram, preferred_element_type=jnp.float32).astype(jnp.bfloat16)
    second = jnp.dot(first, gram, preferred_element_type=jnp.float32)
    combined = (
        ns_first * block.astype(jnp.float32)
        + ns_second * first.astype(jnp.float32)
        + ns_third * second
    )
    return combined.astype(jnp.bfloat16)


def block_gram_kernel(*refs):
    pieces, (gram_ref, rows_ref) = refs[:-2], refs[-2:]
    height = pieces[0].shape[0]
    for position, piece_ref in enumerate(pieces):
        rows_ref[position * height : (position + 1) * height, :] = piece_ref[...]
    whole = rows_ref[...]
    step = 256
    for start in range(0, whole.shape[1], step):
        stop = start + step
        gram_ref[:stop, start:stop] = lax.dot_general(
            whole[:, :stop],
            whole[:, start:stop],
            (((0,), (0,)), ((), ())),
            preferred_element_type=jnp.float32,
        ).astype(jnp.bfloat16)


def block_gram(pieces):
    height, width = pieces[0].shape
    return pl.pallas_call(
        block_gram_kernel,
        out_shape=jax.ShapeDtypeStruct((width, width), jnp.bfloat16),
        scratch_shapes=[pltpu.VMEM((len(pieces) * height, width), jnp.bfloat16)],
        compiler_params=pltpu.CompilerParams(vmem_limit_bytes=16 * MIB),
    )(*pieces)


def orthogonalize_kernel(count, pieces, *refs):
    height, width = refs[0].shape
    inputs = refs[: count * pieces]
    ready_ref = refs[count * pieces]
    outputs = refs[count * pieces + 1 : count * pieces + 1 + pieces]
    gram_ref, start_ref, next_ref = refs[count * pieces + 1 + pieces :]
    block = pieces * height
    rows = count * block
    chunk = 2 * block if count % 2 == 0 else block
    for position, piece_ref in enumerate(inputs):
        start_ref[position * height : (position + 1) * height, :] = piece_ref[...]
    current, other = start_ref, next_ref
    for iteration in range(NS_STEPS):
        blocks = [current.at[start : start + block] for start in range(0, rows, block)]
        if iteration == 0:
            gram_of(blocks[1:], gram_ref, ready_ref)
        else:
            gram_of(blocks, gram_ref)
        if iteration + 1 < NS_STEPS:
            for start in range(0, rows, chunk):
                other[start : start + chunk, :] = polynomial(
                    current[start : start + chunk, :], gram_ref
                )
            current, other = other, current
    result = polynomial(current[:block, :], gram_ref)
    for piece in range(pieces):
        outputs[piece][...] = result[piece * height : (piece + 1) * height, :]


def orthogonalize(blocks, own_gram):
    count, pieces = len(blocks), len(blocks[0])
    height, width = blocks[0][0].shape
    return pl.pallas_call(
        functools.partial(orthogonalize_kernel, count, pieces),
        out_shape=[jax.ShapeDtypeStruct((height, width), jnp.bfloat16)] * pieces,
        scratch_shapes=[
            pltpu.VMEM((width, width), jnp.bfloat16),
            pltpu.VMEM((count * pieces * height, width), jnp.bfloat16),
            pltpu.VMEM((count * pieces * height, width), jnp.bfloat16),
        ],
        compiler_params=pltpu.CompilerParams(vmem_limit_bytes=32 * MIB),
    )(*[piece for block in blocks for piece in block], own_gram)


def folded(array):
    line = jnp.sum(array, axis=0, keepdims=True)
    total = line[:, :LANES]
    for start in range(LANES, line.shape[1], LANES):
        total = total + line[:, start : start + LANES]
    return total


def slices_kernel(count, place_ref, grad_ref, *refs):
    outputs, semaphores = refs[:count], refs[count]
    copies = [
        pltpu.make_async_copy(
            grad_ref.at[:, place_ref[offset]], outputs[offset], semaphores.at[offset]
        )
        for offset in range(count)
    ]
    for copy in reversed(copies):
        copy.start()
    for copy in reversed(copies):
        copy.wait()


def row_slices(place, by_rows):
    matrix_count, shard_count, height, width = by_rows.shape
    return pl.pallas_call(
        functools.partial(slices_kernel, shard_count),
        out_shape=[jax.ShapeDtypeStruct((matrix_count, height, width), by_rows.dtype)] * shard_count,
        in_specs=[
            pl.BlockSpec(memory_space=pltpu.SMEM),
            pl.BlockSpec(memory_space=pltpu.HBM),
        ],
        out_specs=[pl.BlockSpec(memory_space=pltpu.VMEM)] * shard_count,
        scratch_shapes=[pltpu.SemaphoreType.DMA((shard_count,))],
        compiler_params=pltpu.CompilerParams(vmem_limit_bytes=4 * MIB),
    )(place, by_rows)


def sum_kernel(shard_count, place_ref, *refs):
    parts = refs[:shard_count]
    vector_parts, momentum_ref, grad_ref, vector_ref, figures_ref = refs[shard_count:]
    vector = jnp.sum(vector_parts[...].astype(jnp.float32), axis=0)
    vector_ref[...] = vector
    total = folded(vector * vector) * (1.0 / shard_count)
    squares, crosses, momentum_squares = [], [], []
    for matrix in range(momentum_ref.shape[0]):
        grad = parts[0][matrix].astype(jnp.float32)
        for part in parts[1:]:
            grad = grad + part[matrix].astype(jnp.float32)
        grad_ref[matrix] = grad
        old = momentum_ref[matrix]
        squares.append(folded(grad * grad))
        crosses.append(folded(grad * old))
        momentum_squares.append(folded(old * old))
        total = total + squares[-1]
    lines = squares + crosses + momentum_squares + [total]
    lines = lines + [jnp.zeros_like(total)] * (FIGURES - len(lines))
    tile = jnp.concatenate(lines, axis=0)
    sums = jnp.sum(tile, axis=1, keepdims=True)
    line_index = lax.broadcasted_iota(jnp.int32, tile.shape, 0)
    lane_index = lax.broadcasted_iota(jnp.int32, tile.shape, 1)
    line = jnp.sum(jnp.where(line_index == lane_index, sums, 0.0), axis=0, keepdims=True)
    total_only = jnp.where(lane_index[:1] == 3 * momentum_ref.shape[0], line, 0.0)
    for section in range(figures_ref.shape[1]):
        chosen = jnp.where(place_ref[shard_count] == section, line, total_only)
        figures_ref[:, section] = jnp.broadcast_to(
            chosen[None], (figures_ref.shape[0],) + line.shape
        )


def scale_kernel(matrix_count, place_ref, figures_ref, grad_ref, momentum_ref, *refs):
    outputs = refs[:matrix_count]
    clip_ref = refs[matrix_count]
    line = jnp.sum(figures_ref[...], axis=0)
    line_index = lax.broadcasted_iota(jnp.int32, (FIGURES, LANES), 0)
    lane_index = lax.broadcasted_iota(jnp.int32, (FIGURES, LANES), 1)
    sums = jnp.sum(jnp.where(line_index == lane_index, line, 0.0), axis=1, keepdims=True)
    total = sums[3 * matrix_count : 3 * matrix_count + 1]
    clip = jnp.minimum(1.0, max_norm / (jnp.sqrt(total) + 1e-06))
    clip_ref[...] = jnp.broadcast_to(clip, clip_ref.shape)
    grad_scale = (1.0 + mom_beta) * clip
    momentum_scale = mom_beta * mom_beta
    update_norm = (
        grad_scale * grad_scale * sums[:matrix_count]
        + 2.0 * grad_scale * momentum_scale * sums[matrix_count : 2 * matrix_count]
        + momentum_scale * momentum_scale * sums[2 * matrix_count : 3 * matrix_count]
    )
    inverse = 1.0 / (jnp.sqrt(jnp.maximum(update_norm, 0.0)) + 1e-07)
    position = lax.broadcasted_iota(jnp.int32, inverse.shape, 0)
    for place in range(matrix_count):
        matrix = place_ref[place]
        factor = jnp.sum(jnp.where(position == matrix, inverse, 0.0), axis=0, keepdims=True)
        clipped = clip * grad_ref[matrix]
        new_momentum = mom_beta * momentum_ref[matrix] + clipped
        nesterov = clipped + mom_beta * new_momentum
        outputs[place][...] = (nesterov * factor).astype(jnp.bfloat16)


def end_kernel(offsets, place_ref, *refs):
    arrived = refs[: len(offsets)]
    weights_ref = refs[len(offsets)]
    update_ref, new_weights_ref, update_rows, weight_rows, semaphores = refs[-5:]
    step_size = muon_rate * (0.2 * math.sqrt(D))
    copies = []
    for slot, offset in enumerate(offsets):
        matrix = place_ref[offset]
        update = arrived[slot][...]
        update_rows[slot] = update
        weight_rows[slot] = (
            weights_ref[matrix].astype(jnp.float32) * (1.0 - muon_rate * muon_decay)
            - step_size * update.astype(jnp.float32)
        ).astype(jnp.bfloat16)
        for kind, (rows, target) in enumerate(
            ((update_rows, update_ref), (weight_rows, new_weights_ref))
        ):
            copies.append(
                pltpu.make_async_copy(
                    rows.at[slot], target.at[matrix], semaphores.at[2 * slot + kind]
                )
            )
            copies[-1].start()
    for copy in copies:
        copy.wait()


def finished(offsets, place, arrived, weights, partial=()):
    height, width = arrived[0].shape
    anywhere = pl.BlockSpec(memory_space=pltpu.HBM)
    return pl.pallas_call(
        functools.partial(end_kernel, offsets),
        out_shape=[jax.ShapeDtypeStruct(weights.shape, weights.dtype)] * 2,
        in_specs=[pl.BlockSpec(memory_space=pltpu.SMEM)]
        + [pl.BlockSpec(memory_space=pltpu.VMEM)] * (len(arrived) + 1)
        + [anywhere] * len(partial),
        out_specs=[anywhere] * 2,
        scratch_shapes=[
            pltpu.VMEM((len(offsets), height, width), weights.dtype),
            pltpu.VMEM((len(offsets), height, width), weights.dtype),
            pltpu.SemaphoreType.DMA((2 * len(offsets),)),
        ],
        input_output_aliases={len(arrived) + 2 + i: i for i in range(len(partial))},
        compiler_params=pltpu.CompilerParams(vmem_limit_bytes=8 * MIB),
    )(place, *arrived, weights, *partial)


def state_kernel(
    place_ref,
    clip_ref,
    grad_ref,
    momentum_ref,
    sums_ref,
    vectors_ref,
    first_ref,
    second_ref,
    new_momentum_ref,
    direction_ref,
    new_ref,
):
    new_momentum_ref[...] = mom_beta * momentum_ref[...] + clip_ref[0:1, 0:1] * grad_ref[...]
    width = vectors_ref.shape[1]
    count = sums_ref.shape[1] // width
    rows = sums_ref[:, :width]
    for position in range(1, count):
        part = sums_ref[:, position * width : (position + 1) * width]
        rows = jnp.where(place_ref[0] == position, part, rows)
    clipped = clip_ref[0:1, 0:1] * rows
    updated_first = 0.9 * first_ref[...] + 0.1 * clipped
    updated_second = 0.999 * second_ref[...] + 0.001 * clipped * clipped
    direction = updated_first / (jnp.sqrt(updated_second) + 1e-08)
    direction_ref[...] = direction
    new_ref[...] = vectors_ref[...] * (1.0 - adam_rate * adam_decay) - adam_rate * direction


def on_device(kernel, scalars, operands, out_shape):
    return pl.pallas_call(
        kernel,
        out_shape=out_shape,
        in_specs=[pl.BlockSpec(memory_space=pltpu.SMEM)]
        + [pl.BlockSpec(memory_space=pltpu.VMEM)] * len(operands),
        compiler_params=pltpu.CompilerParams(vmem_limit_bytes=16 * MIB),
    )(scalars, *operands)


def swapped(array, axis, offset):
    pairs = [(i, i ^ offset) for i in range(lax.axis_size(axis))]
    return lax.ppermute(array, axis, pairs)


def after(array, earlier):
    return lax.optimization_barrier((array, earlier))[0]


def per_device(grad_parts, vector_grads, momentum, weights, vectors, first_moment, second_moment):
    shard_count = lax.axis_size("shard")
    tensor_count = lax.axis_size("tensor")
    section_count = lax.axis_size("section")
    _, matrix_count, local_height, width = momentum.shape
    if shard_count != matrix_count or shard_count != 4 or tensor_count != 4:
        return general_device(
            grad_parts, vector_grads, momentum, weights, vectors, first_moment, second_moment
        )
    vector_count, vector_width = vectors.shape[1:]
    own_momentum = momentum[0]
    position = jnp.arange(shard_count + 1, dtype=jnp.int32)
    place = jnp.where(
        position == shard_count,
        lax.axis_index("section").astype(jnp.int32),
        lax.axis_index("shard").astype(jnp.int32) ^ position,
    )

    by_rows = grad_parts.reshape(matrix_count, shard_count, local_height, width)
    parts = list(row_slices(place, by_rows))
    for offset in reversed(range(1, shard_count)):
        parts[offset] = swapped(parts[offset], "shard", offset)
    vector_parts = lax.all_to_all(
        jnp.broadcast_to(vector_grads[0], (shard_count, vector_count, vector_width * shard_count)),
        "shard",
        split_axis=0,
        concat_axis=0,
        tiled=True,
    )

    others = shard_count * tensor_count
    grad_rows, vector_whole, figures = on_device(
        functools.partial(sum_kernel, shard_count),
        place,
        parts[::-1] + [vector_parts, own_momentum],
        [
            jax.ShapeDtypeStruct(own_momentum.shape, jnp.float32),
            jax.ShapeDtypeStruct(vector_parts.shape[1:], jnp.float32),
            jax.ShapeDtypeStruct((others, section_count, 1, LANES), jnp.float32),
        ],
    )
    figures = lax.all_to_all(
        figures.reshape(others * section_count, 1, LANES),
        MESH_AXES,
        split_axis=0,
        concat_axis=0,
        tiled=True,
    )
    *scaled, clip_tile = on_device(
        functools.partial(scale_kernel, matrix_count),
        place,
        [figures, grad_rows, own_momentum],
        [jax.ShapeDtypeStruct((local_height, width), jnp.bfloat16)] * matrix_count
        + [jax.ShapeDtypeStruct((8, LANES), jnp.float32)],
    )

    pieces = [scaled[0]] + [None] * 3
    for offset in (2, 3, 1):
        ready = after(scaled[offset], pieces[2]) if offset == 3 else scaled[offset]
        pieces[offset] = swapped(ready, "shard", offset)
    near, side, far = [None] * 4, [None] * 4, [None] * 4
    near[0] = swapped(pieces[0], "tensor", 1)
    side[0] = swapped(pieces[0], "tensor", 2)
    far[0] = swapped(near[0], "tensor", 2)
    near[1] = swapped(pieces[1], "tensor", 1)
    side[1] = swapped(pieces[1], "tensor", 2)
    far[1] = swapped(side[1], "tensor", 1)
    near[2] = swapped(pieces[2], "tensor", 1)
    side[2] = swapped(pieces[2], "tensor", 2)
    far[2] = swapped(near[2], "tensor", 2)
    near[3] = swapped(pieces[3], "tensor", 1)
    side[3] = swapped(pieces[3], "tensor", 2)
    far[3] = swapped(pieces[3], "tensor", 3)
    own_gram = block_gram(pieces[:3] + [after(pieces[3], far[1])])
    results = orthogonalize([pieces, near, side, far], own_gram)

    returned = {
        offset: swapped(results[offset], "shard", offset)
        for offset in reversed(range(1, shard_count))
    }
    early = finished((0,), place, [results[0]], weights[0])
    orthogonal_update, new_weights = finished(
        (3, 2, 1), place, [returned[offset] for offset in (3, 2, 1)], weights[0], early
    )
    new_momentum, adam_direction, new_vectors = on_device(
        state_kernel,
        place,
        [
            after(clip_tile, results[0]),
            grad_rows,
            own_momentum,
            vector_whole,
            vectors[0],
            first_moment[0],
            second_moment[0],
        ],
        [jax.ShapeDtypeStruct(own_momentum.shape, jnp.float32)]
        + [jax.ShapeDtypeStruct(vectors.shape[1:], jnp.float32)] * 2,
    )
    return (
        new_momentum[None],
        orthogonal_update[None],
        new_weights[None],
        adam_direction[None],
        new_vectors[None],
    )


def general_device(grad_parts, vector_grads, momentum, weights, vectors, first_moment, second_moment):
    shard_count = lax.axis_size("shard")
    tensor_count = lax.axis_size("tensor")
    section_count = lax.axis_size("section")
    shard_index = lax.axis_index("shard")
    _, matrix_count, local_height, width = momentum.shape
    vector_width = vectors.shape[2]
    own_momentum = momentum[0]

    rows = matrix_count * local_height
    by_target = (
        grad_parts.reshape(matrix_count, shard_count, local_height, width)
        .transpose(1, 0, 2, 3)
        .reshape(shard_count, rows, width)
    )
    vector_line = jnp.broadcast_to(
        vector_grads.reshape(1, 1, width), (shard_count, VECTOR_ROWS, width)
    )
    payload = jnp.concatenate([by_target, vector_line], axis=1)
    arrived = lax.all_to_all(payload, "shard", split_axis=0, concat_axis=0, tiled=True)
    grad_rows = jnp.sum(arrived[:, :rows].astype(jnp.float32), axis=0).reshape(
        matrix_count, local_height, width
    )
    vector_whole = jnp.sum(arrived[:, rows].astype(jnp.float32), axis=0).reshape(
        vectors.shape[1], vector_width * shard_count
    )
    vector_rows = lax.dynamic_slice_in_dim(
        vector_whole, shard_index * vector_width, vector_width, 1
    )

    grad_squares = jnp.sum(grad_rows * grad_rows, axis=(1, 2))
    cross = jnp.sum(grad_rows * own_momentum, axis=(1, 2))
    momentum_squares = jnp.sum(own_momentum * own_momentum, axis=(1, 2))
    own_total = jnp.sum(grad_squares) + jnp.sum(vector_rows * vector_rows)
    same_section = (
        jnp.arange(section_count) == lax.axis_index("section")
    ).astype(jnp.float32)[:, None]
    matrix_figures = jnp.concatenate([grad_squares, cross, momentum_squares])
    line = jnp.concatenate(
        [
            same_section * matrix_figures[None],
            jnp.broadcast_to(own_total, (section_count, 1)),
            jnp.zeros((section_count, 127 - 3 * matrix_count), jnp.float32),
        ],
        axis=1,
    )
    others = shard_count * tensor_count
    figures = jnp.broadcast_to(line[None, :, None, :], (others, section_count, 8, 128)).reshape(
        others * section_count, 8, 128
    )
    figures = lax.all_to_all(figures, MESH_AXES, split_axis=0, concat_axis=0, tiled=True)
    sums = jnp.sum(figures[:, 0, :], axis=0)
    grand_total = sums[3 * matrix_count]
    clip_factor = jnp.minimum(1.0, max_norm / (jnp.sqrt(grand_total) + 1e-06))
    grad_scale = (1.0 + mom_beta) * clip_factor
    momentum_scale = mom_beta * mom_beta
    update_norm = (
        grad_scale * grad_scale * sums[:matrix_count]
        + 2.0 * grad_scale * momentum_scale * sums[matrix_count : 2 * matrix_count]
        + momentum_scale * momentum_scale * sums[2 * matrix_count : 3 * matrix_count]
    )
    update_norm = jnp.maximum(update_norm, 0.0)[:, None, None]

    new_momentum = mom_beta * own_momentum + clip_factor * grad_rows
    nesterov = clip_factor * grad_rows + mom_beta * new_momentum
    scaled = (nesterov / (jnp.sqrt(update_norm) + 1e-07)).astype(jnp.bfloat16)

    owner_count = shard_count // matrix_count
    if owner_count == 1:
        row_block = lax.all_to_all(scaled, "shard", split_axis=0, concat_axis=0, tiled=True)
        row_block = row_block.reshape(shard_count * local_height, width)
    else:
        everything = lax.all_gather(scaled, "shard", axis=1, tiled=True)
        row_block = lax.dynamic_index_in_dim(
            everything, shard_index // owner_count, 0, keepdims=False
        )

    blocks = [row_block]
    for offset in range(1, tensor_count):
        pairs = [(i, i ^ offset) for i in range(tensor_count)]
        blocks.append(lax.ppermute(row_block, "tensor", pairs))
    (own_result,) = orthogonalize([[block] for block in blocks], block_gram(blocks[:1]))

    if owner_count == 1:
        own_update = lax.all_to_all(
            own_result.reshape(shard_count, local_height, width),
            "shard",
            split_axis=0,
            concat_axis=0,
            tiled=True,
        )
    else:
        piece_length = local_height * width // owner_count
        split_rows = own_result.reshape(shard_count, owner_count, piece_length)
        returning = lax.dynamic_index_in_dim(
            split_rows, shard_index % owner_count, 1, keepdims=False
        )
        received = lax.all_to_all(returning, "shard", split_axis=0, concat_axis=0, tiled=True)
        own_update = received.reshape(matrix_count, local_height, width)
    orthogonal_update = own_update[None]
    muon_scale = 0.2 * math.sqrt(D)
    new_weights = (
        weights.astype(jnp.float32) * (1.0 - muon_rate * muon_decay)
        - muon_rate * muon_scale * orthogonal_update.astype(jnp.float32)
    ).astype(jnp.bfloat16)
    vector_clipped = clip_factor * vector_rows
    updated_first = 0.9 * first_moment + 0.1 * vector_clipped
    updated_second = 0.999 * second_moment + 0.001 * vector_clipped * vector_clipped
    adam_direction = updated_first / (jnp.sqrt(updated_second) + 1e-08)
    new_vectors = vectors * (1.0 - adam_rate * adam_decay) - adam_rate * adam_direction
    return (new_momentum[None], orthogonal_update, new_weights, adam_direction, new_vectors)


def solution(mesh):
    in_specs = (
        P("shard", "section", None, "tensor", None),
        P("shard", "section", None, "tensor"),
        P("section", None, ("tensor", "shard"), None),
        P("section", None, ("tensor", "shard"), None),
        P("section", None, ("tensor", "shard")),
        P("section", None, ("tensor", "shard")),
        P("section", None, ("tensor", "shard")),
    )
    out_specs = (
        P("section", None, ("tensor", "shard"), None),
        P("section", None, ("tensor", "shard"), None),
        P("section", None, ("tensor", "shard"), None),
        P("section", None, ("tensor", "shard")),
        P("section", None, ("tensor", "shard")),
    )
    return jax.shard_map(
        per_device, mesh=mesh, in_specs=in_specs, out_specs=out_specs, check_vma=False
    )
```

```python
import functools
import math

import jax
import jax.numpy as jnp
from jax import lax
from jax.experimental import pallas as pl
from jax.experimental.pallas import tpu as pltpu
from jax.sharding import PartitionSpec as P

D = 1024
NS_STEPS = 2


ns_first = 3.4445
ns_second = -4.775
ns_third = 2.0315
mom_beta = 0.95
max_norm = 1024.0
muon_rate = 0.02
muon_decay = 0.1
adam_rate = 0.001
adam_decay = 0.01

VECTOR_ROWS = 16
FIGURES = 16
MIB = 2**20
LANES = 128
MESH_AXES = ("shard", "tensor", "section")


def gram_of(blocks, gram_ref, ready_ref=None):
    width = blocks[0].shape[1]
    step = 256
    for start in range(0, width, step):
        stop = start + step
        total = None if ready_ref is None else ready_ref[:stop, start:stop].astype(jnp.float32)
        for block in blocks:
            whole = block[...]
            product = lax.dot_general(
                whole[:, :stop],
                whole[:, start:stop],
                (((0,), (0,)), ((), ())),
                preferred_element_type=jnp.float32,
            )
            rounded = product.astype(jnp.bfloat16).astype(jnp.float32)
            total = rounded if total is None else total + rounded
        gram_ref[:stop, start:stop] = total.astype(jnp.bfloat16)
        for above in range(0, start, step):
            tile = gram_ref[above : above + step, start:stop]
            gram_ref[start:stop, above : above + step] = tile.T


def polynomial(block, gram_ref):
    gram = gram_ref[...]
    first = jnp.dot(block, gram, preferred_element_type=jnp.float32).astype(jnp.bfloat16)
    second = jnp.dot(first, gram, preferred_element_type=jnp.float32)
    combined = (
        ns_first * block.astype(jnp.float32)
        + ns_second * first.astype(jnp.float32)
        + ns_third * second
    )
    return combined.astype(jnp.bfloat16)


def block_gram_kernel(*refs):
    pieces, (gram_ref, rows_ref) = refs[:-2], refs[-2:]
    height = pieces[0].shape[0]
    for position, piece_ref in enumerate(pieces):
        rows_ref[position * height : (position + 1) * height, :] = piece_ref[...]
    whole = rows_ref[...]
    step = 256
    for start in range(0, whole.shape[1], step):
        stop = start + step
        gram_ref[:stop, start:stop] = lax.dot_general(
            whole[:, :stop],
            whole[:, start:stop],
            (((0,), (0,)), ((), ())),
            preferred_element_type=jnp.float32,
        ).astype(jnp.bfloat16)


def block_gram(pieces):
    height, width = pieces[0].shape
    return pl.pallas_call(
        block_gram_kernel,
        out_shape=jax.ShapeDtypeStruct((width, width), jnp.bfloat16),
        scratch_shapes=[pltpu.VMEM((len(pieces) * height, width), jnp.bfloat16)],
        compiler_params=pltpu.CompilerParams(vmem_limit_bytes=16 * MIB),
    )(*pieces)


def orthogonalize_kernel(count, pieces, *refs):
    height, width = refs[0].shape
    inputs = refs[: count * pieces]
    ready_ref = refs[count * pieces]
    outputs = refs[count * pieces + 1 : count * pieces + 1 + pieces]
    gram_ref, start_ref, next_ref = refs[count * pieces + 1 + pieces :]
    block = pieces * height
    rows = count * block
    chunk = 2 * block if count % 2 == 0 else block
    for position, piece_ref in enumerate(inputs):
        start_ref[position * height : (position + 1) * height, :] = piece_ref[...]
    current, other = start_ref, next_ref
    for iteration in range(NS_STEPS):
        blocks = [current.at[start : start + block] for start in range(0, rows, block)]
        if iteration == 0:
            gram_of(blocks[1:], gram_ref, ready_ref)
        else:
            gram_of(blocks, gram_ref)
        if iteration + 1 < NS_STEPS:
            for start in range(0, rows, chunk):
                other[start : start + chunk, :] = polynomial(
                    current[start : start + chunk, :], gram_ref
                )
            current, other = other, current
    result = polynomial(current[:block, :], gram_ref)
    for piece in range(pieces):
        outputs[piece][...] = result[piece * height : (piece + 1) * height, :]


def orthogonalize(blocks, own_gram):
    count, pieces = len(blocks), len(blocks[0])
    height, width = blocks[0][0].shape
    return pl.pallas_call(
        functools.partial(orthogonalize_kernel, count, pieces),
        out_shape=[jax.ShapeDtypeStruct((height, width), jnp.bfloat16)] * pieces,
        scratch_shapes=[
            pltpu.VMEM((width, width), jnp.bfloat16),
            pltpu.VMEM((count * pieces * height, width), jnp.bfloat16),
            pltpu.VMEM((count * pieces * height, width), jnp.bfloat16),
        ],
        compiler_params=pltpu.CompilerParams(vmem_limit_bytes=32 * MIB),
    )(*[piece for block in blocks for piece in block], own_gram)


def folded(array):
    line = jnp.sum(array, axis=0, keepdims=True)
    total = line[:, :LANES]
    for start in range(LANES, line.shape[1], LANES):
        total = total + line[:, start : start + LANES]
    return total


def slices_kernel(count, place_ref, grad_ref, *refs):
    outputs, semaphores = refs[:count], refs[count]
    copies = [
        pltpu.make_async_copy(
            grad_ref.at[:, place_ref[offset]], outputs[offset], semaphores.at[offset]
        )
        for offset in range(count)
    ]
    for copy in reversed(copies):
        copy.start()
    for copy in reversed(copies):
        copy.wait()


def row_slices(place, by_rows):
    matrix_count, shard_count, height, width = by_rows.shape
    return pl.pallas_call(
        functools.partial(slices_kernel, shard_count),
        out_shape=[jax.ShapeDtypeStruct((matrix_count, height, width), by_rows.dtype)] * shard_count,
        in_specs=[
            pl.BlockSpec(memory_space=pltpu.SMEM),
            pl.BlockSpec(memory_space=pltpu.HBM),
        ],
        out_specs=[pl.BlockSpec(memory_space=pltpu.VMEM)] * shard_count,
        scratch_shapes=[pltpu.SemaphoreType.DMA((shard_count,))],
        compiler_params=pltpu.CompilerParams(vmem_limit_bytes=4 * MIB),
    )(place, by_rows)


def sum_kernel(shard_count, place_ref, *refs):
    parts = refs[:shard_count]
    vector_parts, momentum_ref, grad_ref, vector_ref, figures_ref = refs[shard_count:]
    vector = jnp.sum(vector_parts[...].astype(jnp.float32), axis=0)
    vector_ref[...] = vector
    total = folded(vector * vector) * (1.0 / shard_count)
    squares, crosses, momentum_squares = [], [], []
    for matrix in range(momentum_ref.shape[0]):
        grad = parts[0][matrix].astype(jnp.float32)
        for part in parts[1:]:
            grad = grad + part[matrix].astype(jnp.float32)
        grad_ref[matrix] = grad
        old = momentum_ref[matrix]
        squares.append(folded(grad * grad))
        crosses.append(folded(grad * old))
        momentum_squares.append(folded(old * old))
        total = total + squares[-1]
    lines = squares + crosses + momentum_squares + [total]
    lines = lines + [jnp.zeros_like(total)] * (FIGURES - len(lines))
    tile = jnp.concatenate(lines, axis=0)
    sums = jnp.sum(tile, axis=1, keepdims=True)
    line_index = lax.broadcasted_iota(jnp.int32, tile.shape, 0)
    lane_index = lax.broadcasted_iota(jnp.int32, tile.shape, 1)
    line = jnp.sum(jnp.where(line_index == lane_index, sums, 0.0), axis=0, keepdims=True)
    total_only = jnp.where(lane_index[:1] == 3 * momentum_ref.shape[0], line, 0.0)
    for section in range(figures_ref.shape[1]):
        chosen = jnp.where(place_ref[shard_count] == section, line, total_only)
        figures_ref[:, section] = jnp.broadcast_to(
            chosen[None], (figures_ref.shape[0],) + line.shape
        )


def scale_kernel(matrix_count, place_ref, figures_ref, grad_ref, momentum_ref, *refs):
    outputs = refs[:matrix_count]
    clip_ref = refs[matrix_count]
    line = jnp.sum(figures_ref[...], axis=0)
    line_index = lax.broadcasted_iota(jnp.int32, (FIGURES, LANES), 0)
    lane_index = lax.broadcasted_iota(jnp.int32, (FIGURES, LANES), 1)
    sums = jnp.sum(jnp.where(line_index == lane_index, line, 0.0), axis=1, keepdims=True)
    total = sums[3 * matrix_count : 3 * matrix_count + 1]
    clip = jnp.minimum(1.0, max_norm / (jnp.sqrt(total) + 1e-06))
    clip_ref[...] = jnp.broadcast_to(clip, clip_ref.shape)
    grad_scale = (1.0 + mom_beta) * clip
    momentum_scale = mom_beta * mom_beta
    update_norm = (
        grad_scale * grad_scale * sums[:matrix_count]
        + 2.0 * grad_scale * momentum_scale * sums[matrix_count : 2 * matrix_count]
        + momentum_scale * momentum_scale * sums[2 * matrix_count : 3 * matrix_count]
    )
    inverse = 1.0 / (jnp.sqrt(jnp.maximum(update_norm, 0.0)) + 1e-07)
    position = lax.broadcasted_iota(jnp.int32, inverse.shape, 0)
    for place in range(matrix_count):
        matrix = place_ref[place]
        factor = jnp.sum(jnp.where(position == matrix, inverse, 0.0), axis=0, keepdims=True)
        clipped = clip * grad_ref[matrix]
        new_momentum = mom_beta * momentum_ref[matrix] + clipped
        nesterov = clipped + mom_beta * new_momentum
        outputs[place][...] = (nesterov * factor).astype(jnp.bfloat16)


def end_kernel(offsets, place_ref, *refs):
    arrived = refs[: len(offsets)]
    weights_ref = refs[len(offsets)]
    update_ref, new_weights_ref, update_rows, weight_rows, semaphores = refs[-5:]
    step_size = muon_rate * (0.2 * math.sqrt(D))
    copies = []
    for slot, offset in enumerate(offsets):
        matrix = place_ref[offset]
        update = arrived[slot][...]
        update_rows[slot] = update
        weight_rows[slot] = (
            weights_ref[matrix].astype(jnp.float32) * (1.0 - muon_rate * muon_decay)
            - step_size * update.astype(jnp.float32)
        ).astype(jnp.bfloat16)
        for kind, (rows, target) in enumerate(
            ((update_rows, update_ref), (weight_rows, new_weights_ref))
        ):
            copies.append(
                pltpu.make_async_copy(
                    rows.at[slot], target.at[matrix], semaphores.at[2 * slot + kind]
                )
            )
            copies[-1].start()
    for copy in copies:
        copy.wait()


def finished(offsets, place, arrived, weights, partial=()):
    height, width = arrived[0].shape
    anywhere = pl.BlockSpec(memory_space=pltpu.HBM)
    return pl.pallas_call(
        functools.partial(end_kernel, offsets),
        out_shape=[jax.ShapeDtypeStruct(weights.shape, weights.dtype)] * 2,
        in_specs=[pl.BlockSpec(memory_space=pltpu.SMEM)]
        + [pl.BlockSpec(memory_space=pltpu.VMEM)] * (len(arrived) + 1)
        + [anywhere] * len(partial),
        out_specs=[anywhere] * 2,
        scratch_shapes=[
            pltpu.VMEM((len(offsets), height, width), weights.dtype),
            pltpu.VMEM((len(offsets), height, width), weights.dtype),
            pltpu.SemaphoreType.DMA((2 * len(offsets),)),
        ],
        input_output_aliases={len(arrived) + 2 + i: i for i in range(len(partial))},
        compiler_params=pltpu.CompilerParams(vmem_limit_bytes=8 * MIB),
    )(place, *arrived, weights, *partial)


def state_kernel(
    place_ref,
    clip_ref,
    grad_ref,
    momentum_ref,
    sums_ref,
    vectors_ref,
    first_ref,
    second_ref,
    new_momentum_ref,
    direction_ref,
    new_ref,
):
    new_momentum_ref[...] = mom_beta * momentum_ref[...] + clip_ref[0:1, 0:1] * grad_ref[...]
    width = vectors_ref.shape[1]
    count = sums_ref.shape[1] // width
    rows = sums_ref[:, :width]
    for position in range(1, count):
        part = sums_ref[:, position * width : (position + 1) * width]
        rows = jnp.where(place_ref[0] == position, part, rows)
    clipped = clip_ref[0:1, 0:1] * rows
    updated_first = 0.9 * first_ref[...] + 0.1 * clipped
    updated_second = 0.999 * second_ref[...] + 0.001 * clipped * clipped
    direction = updated_first / (jnp.sqrt(updated_second) + 1e-08)
    direction_ref[...] = direction
    new_ref[...] = vectors_ref[...] * (1.0 - adam_rate * adam_decay) - adam_rate * direction


def on_device(kernel, scalars, operands, out_shape):
    return pl.pallas_call(
        kernel,
        out_shape=out_shape,
        in_specs=[pl.BlockSpec(memory_space=pltpu.SMEM)]
        + [pl.BlockSpec(memory_space=pltpu.VMEM)] * len(operands),
        compiler_params=pltpu.CompilerParams(vmem_limit_bytes=16 * MIB),
    )(scalars, *operands)


def swapped(array, axis, offset):
    pairs = [(i, i ^ offset) for i in range(lax.axis_size(axis))]
    return lax.ppermute(array, axis, pairs)


def after(array, earlier):
    return lax.optimization_barrier((array, earlier))[0]


def per_device(grad_parts, vector_grads, momentum, weights, vectors, first_moment, second_moment):
    shard_count = lax.axis_size("shard")
    tensor_count = lax.axis_size("tensor")
    section_count = lax.axis_size("section")
    _, matrix_count, local_height, width = momentum.shape
    if shard_count != matrix_count or shard_count != 4 or tensor_count != 4:
        return general_device(
            grad_parts, vector_grads, momentum, weights, vectors, first_moment, second_moment
        )
    vector_count, vector_width = vectors.shape[1:]
    own_momentum = momentum[0]
    position = jnp.arange(shard_count + 1, dtype=jnp.int32)
    place = jnp.where(
        position == shard_count,
        lax.axis_index("section").astype(jnp.int32),
        lax.axis_index("shard").astype(jnp.int32) ^ position,
    )

    by_rows = grad_parts.reshape(matrix_count, shard_count, local_height, width)
    parts = list(row_slices(place, by_rows))
    for offset in reversed(range(1, shard_count)):
        parts[offset] = swapped(parts[offset], "shard", offset)
    vector_parts = lax.all_to_all(
        jnp.broadcast_to(vector_grads[0], (shard_count, vector_count, vector_width * shard_count)),
        "shard",
        split_axis=0,
        concat_axis=0,
        tiled=True,
    )

    others = shard_count * tensor_count
    grad_rows, vector_whole, figures = on_device(
        functools.partial(sum_kernel, shard_count),
        place,
        parts[::-1] + [vector_parts, own_momentum],
        [
            jax.ShapeDtypeStruct(own_momentum.shape, jnp.float32),
            jax.ShapeDtypeStruct(vector_parts.shape[1:], jnp.float32),
            jax.ShapeDtypeStruct((others, section_count, 1, LANES), jnp.float32),
        ],
    )
    figures = lax.all_to_all(
        figures.reshape(others * section_count, 1, LANES),
        MESH_AXES,
        split_axis=0,
        concat_axis=0,
        tiled=True,
    )
    *scaled, clip_tile = on_device(
        functools.partial(scale_kernel, matrix_count),
        place,
        [figures, grad_rows, own_momentum],
        [jax.ShapeDtypeStruct((local_height, width), jnp.bfloat16)] * matrix_count
        + [jax.ShapeDtypeStruct((8, LANES), jnp.float32)],
    )

    pieces = [scaled[0]] + [None] * 3
    for offset in (2, 3, 1):
        pieces[offset] = swapped(scaled[offset], "shard", offset)
    near, side, far = [None] * 4, [None] * 4, [None] * 4
    near[0] = swapped(pieces[0], "tensor", 1)
    side[0] = swapped(pieces[0], "tensor", 2)
    far[0] = swapped(pieces[0], "tensor", 3)
    near[1] = swapped(pieces[1], "tensor", 1)
    side[1] = swapped(after(pieces[1], near[0]), "tensor", 2)
    far[1] = swapped(side[1], "tensor", 1)
    near[2] = swapped(pieces[2], "tensor", 1)
    side[2] = swapped(after(pieces[2], side[0]), "tensor", 2)
    far[2] = swapped(near[2], "tensor", 2)
    near[3] = swapped(after(pieces[3], near[1]), "tensor", 1)
    side[3] = swapped(after(pieces[3], near[1]), "tensor", 2)
    far[3] = swapped(side[3], "tensor", 1)
    own_gram = block_gram(pieces[:3] + [after(pieces[3], far[1])])
    results = orthogonalize([pieces, near, side, far], own_gram)

    returned = {
        offset: swapped(results[offset], "shard", offset)
        for offset in reversed(range(1, shard_count))
    }
    early = finished((0,), place, [results[0]], weights[0])
    orthogonal_update, new_weights = finished(
        (3, 2, 1), place, [returned[offset] for offset in (3, 2, 1)], weights[0], early
    )
    new_momentum, adam_direction, new_vectors = on_device(
        state_kernel,
        place,
        [
            after(clip_tile, results[0]),
            grad_rows,
            own_momentum,
            vector_whole,
            vectors[0],
            first_moment[0],
            second_moment[0],
        ],
        [jax.ShapeDtypeStruct(own_momentum.shape, jnp.float32)]
        + [jax.ShapeDtypeStruct(vectors.shape[1:], jnp.float32)] * 2,
    )
    return (
        new_momentum[None],
        orthogonal_update[None],
        new_weights[None],
        adam_direction[None],
        new_vectors[None],
    )


def general_device(grad_parts, vector_grads, momentum, weights, vectors, first_moment, second_moment):
    shard_count = lax.axis_size("shard")
    tensor_count = lax.axis_size("tensor")
    section_count = lax.axis_size("section")
    shard_index = lax.axis_index("shard")
    _, matrix_count, local_height, width = momentum.shape
    vector_width = vectors.shape[2]
    own_momentum = momentum[0]

    rows = matrix_count * local_height
    by_target = (
        grad_parts.reshape(matrix_count, shard_count, local_height, width)
        .transpose(1, 0, 2, 3)
        .reshape(shard_count, rows, width)
    )
    vector_line = jnp.broadcast_to(
        vector_grads.reshape(1, 1, width), (shard_count, VECTOR_ROWS, width)
    )
    payload = jnp.concatenate([by_target, vector_line], axis=1)
    arrived = lax.all_to_all(payload, "shard", split_axis=0, concat_axis=0, tiled=True)
    grad_rows = jnp.sum(arrived[:, :rows].astype(jnp.float32), axis=0).reshape(
        matrix_count, local_height, width
    )
    vector_whole = jnp.sum(arrived[:, rows].astype(jnp.float32), axis=0).reshape(
        vectors.shape[1], vector_width * shard_count
    )
    vector_rows = lax.dynamic_slice_in_dim(
        vector_whole, shard_index * vector_width, vector_width, 1
    )

    grad_squares = jnp.sum(grad_rows * grad_rows, axis=(1, 2))
    cross = jnp.sum(grad_rows * own_momentum, axis=(1, 2))
    momentum_squares = jnp.sum(own_momentum * own_momentum, axis=(1, 2))
    own_total = jnp.sum(grad_squares) + jnp.sum(vector_rows * vector_rows)
    same_section = (
        jnp.arange(section_count) == lax.axis_index("section")
    ).astype(jnp.float32)[:, None]
    matrix_figures = jnp.concatenate([grad_squares, cross, momentum_squares])
    line = jnp.concatenate(
        [
            same_section * matrix_figures[None],
            jnp.broadcast_to(own_total, (section_count, 1)),
            jnp.zeros((section_count, 127 - 3 * matrix_count), jnp.float32),
        ],
        axis=1,
    )
    others = shard_count * tensor_count
    figures = jnp.broadcast_to(line[None, :, None, :], (others, section_count, 8, 128)).reshape(
        others * section_count, 8, 128
    )
    figures = lax.all_to_all(figures, MESH_AXES, split_axis=0, concat_axis=0, tiled=True)
    sums = jnp.sum(figures[:, 0, :], axis=0)
    grand_total = sums[3 * matrix_count]
    clip_factor = jnp.minimum(1.0, max_norm / (jnp.sqrt(grand_total) + 1e-06))
    grad_scale = (1.0 + mom_beta) * clip_factor
    momentum_scale = mom_beta * mom_beta
    update_norm = (
        grad_scale * grad_scale * sums[:matrix_count]
        + 2.0 * grad_scale * momentum_scale * sums[matrix_count : 2 * matrix_count]
        + momentum_scale * momentum_scale * sums[2 * matrix_count : 3 * matrix_count]
    )
    update_norm = jnp.maximum(update_norm, 0.0)[:, None, None]

    new_momentum = mom_beta * own_momentum + clip_factor * grad_rows
    nesterov = clip_factor * grad_rows + mom_beta * new_momentum
    scaled = (nesterov / (jnp.sqrt(update_norm) + 1e-07)).astype(jnp.bfloat16)

    owner_count = shard_count // matrix_count
    if owner_count == 1:
        row_block = lax.all_to_all(scaled, "shard", split_axis=0, concat_axis=0, tiled=True)
        row_block = row_block.reshape(shard_count * local_height, width)
    else:
        everything = lax.all_gather(scaled, "shard", axis=1, tiled=True)
        row_block = lax.dynamic_index_in_dim(
            everything, shard_index // owner_count, 0, keepdims=False
        )

    blocks = [row_block]
    for offset in range(1, tensor_count):
        pairs = [(i, i ^ offset) for i in range(tensor_count)]
        blocks.append(lax.ppermute(row_block, "tensor", pairs))
    (own_result,) = orthogonalize([[block] for block in blocks], block_gram(blocks[:1]))

    if owner_count == 1:
        own_update = lax.all_to_all(
            own_result.reshape(shard_count, local_height, width),
            "shard",
            split_axis=0,
            concat_axis=0,
            tiled=True,
        )
    else:
        piece_length = local_height * width // owner_count
        split_rows = own_result.reshape(shard_count, owner_count, piece_length)
        returning = lax.dynamic_index_in_dim(
            split_rows, shard_index % owner_count, 1, keepdims=False
        )
        received = lax.all_to_all(returning, "shard", split_axis=0, concat_axis=0, tiled=True)
        own_update = received.reshape(matrix_count, local_height, width)
    orthogonal_update = own_update[None]
    muon_scale = 0.2 * math.sqrt(D)
    new_weights = (
        weights.astype(jnp.float32) * (1.0 - muon_rate * muon_decay)
        - muon_rate * muon_scale * orthogonal_update.astype(jnp.float32)
    ).astype(jnp.bfloat16)
    vector_clipped = clip_factor * vector_rows
    updated_first = 0.9 * first_moment + 0.1 * vector_clipped
    updated_second = 0.999 * second_moment + 0.001 * vector_clipped * vector_clipped
    adam_direction = updated_first / (jnp.sqrt(updated_second) + 1e-08)
    new_vectors = vectors * (1.0 - adam_rate * adam_decay) - adam_rate * adam_direction
    return (new_momentum[None], orthogonal_update, new_weights, adam_direction, new_vectors)


def solution(mesh):
    in_specs = (
        P("shard", "section", None, "tensor", None),
        P("shard", "section", None, "tensor"),
        P("section", None, ("tensor", "shard"), None),
        P("section", None, ("tensor", "shard"), None),
        P("section", None, ("tensor", "shard")),
        P("section", None, ("tensor", "shard")),
        P("section", None, ("tensor", "shard")),
    )
    out_specs = (
        P("section", None, ("tensor", "shard"), None),
        P("section", None, ("tensor", "shard"), None),
        P("section", None, ("tensor", "shard"), None),
        P("section", None, ("tensor", "shard")),
        P("section", None, ("tensor", "shard")),
    )
    return jax.shard_map(
        per_device, mesh=mesh, in_specs=in_specs, out_specs=out_specs, check_vma=False
    )
```
